32 devices in a mesh: dp: 2 (over y), fsdp: 16 (over z, x, core).
Axes of the slice: x: 2, y: 2, z: 4, core: 2. Of those that a mesh axis runs over, the one named last changes fastest.
Arguments:
- images: bfloat16 [32, 64, 64, 256], P(('dp', 'fsdp')), may hold values from -6 to 6
- embedding: bfloat16 [32, 512], P(('dp', 'fsdp')), may hold values from -6 to 6
- conv_first: bfloat16 [589824], P(('dp', 'fsdp')), may hold values from -0.125 to 0.125
- conv_second: bfloat16 [589824], P(('dp', 'fsdp')), may hold values from -0.125 to 0.125
- projection: bfloat16 [131072], P(('dp', 'fsdp')), may hold values from -0.25 to 0.25
- vectors: bfloat16 [1536], P(('dp', 'fsdp')), may hold values from -1 to 1.5, as said below
- cotangent: bfloat16 [32, 64, 64, 256], P(('dp', 'fsdp')), may hold values from -6 to 6
Outputs:
- output: bfloat16 [32, 64, 64, 256], P(('dp', 'fsdp'))
- input_grad: float32 [32, 64, 64, 256], P(('dp', 'fsdp'))
- embedding_grad: float32 [32, 512], P(('dp', 'fsdp'))
- conv_first_grad: float32 [589824], P(('dp', 'fsdp'))
- conv_second_grad: float32 [589824], P(('dp', 'fsdp'))
- projection_grad: float32 [131072], P(('dp', 'fsdp'))
- vectors_grad: float32 [1536], P(('dp', 'fsdp'))
The draws below stay inside these ranges and needn't reach their ends.
Inputs may be any that keep to these rules, and one draw needn't show every extreme that they name: `vectors`: rows 0 and 3 (gains) lie near 1, the other rows near 0.
All inputs are finite; a program needn't handle non-finite values.
Results may differ from the reference program's by a relative error of at most 0.0056.
Values may be sent and summed in bfloat16 or wider, within the bound.
No kernel may reach another device: no remote copies, remote signals or barrier semaphores. Data moves between devices by JAX's collectives and lax.ppermute only.
A program may use at most 128 MiB of HBM per device.

```python
import jax
import jax.numpy as jnp
from jax import lax

C = 256
E = 512
GROUPS = 32
H = 64
W = 64
IMAGES = 32


def draw_vectors(key, part):
    key = jax.random.fold_in(key, 11)
    noise = jnp.clip(jax.random.normal(key, (6, C), jnp.float32), -2.0, 2.0)
    offsets = jnp.array([1.0, 0.0, 0.0, 1.0, 0.0, 0.0], jnp.float32)[:, None]
    scales = jnp.array([0.25, 0.5, 0.5, 0.25, 0.5, 0.5], jnp.float32)[:, None]
    return (offsets + scales * noise).reshape(-1).astype(jnp.bfloat16)


def steps_of(stream_key, extent, split, smallest, high):
    level, own = 1.0, jax.random.fold_in(stream_key, 6)
    for axis_at, shards_of in split:
        draws = jnp.exp(jax.random.uniform(jax.random.fold_in(own, axis_at), (shards_of,), jnp.float32, smallest / len(split), high / len(split)))
        level = level * jnp.repeat(draws, extent[axis_at] // shards_of).reshape([-1 if axis == axis_at else 1 for axis in range(len(extent))])
    return level


def gaussian(stream_key, dims, width, most, pieces=(), kind=jnp.bfloat16):
    factor_of = steps_of(stream_key, dims, pieces, -0.22, 0.18) if pieces else 1.0
    values = jax.random.normal(stream_key, dims, jnp.float32) * width * factor_of
    return jnp.minimum(jnp.maximum(values, -most), most).astype(kind)


def setup_inputs(seed: int = 0) -> dict:
    splits = jax.random.split(jax.random.key(seed), 8)
    images = gaussian(splits[0], (IMAGES, H, W, C), 1.0, 6.0, ((0, 32),))
    embedding = gaussian(splits[1], (IMAGES, E), 1.0, 6.0, ((0, 32),))
    conv_first = gaussian(splits[2], (9 * C * C,), (9 * C) ** -0.5, 0.125, ((0, 32),))
    conv_second = gaussian(splits[3], (9 * C * C,), (9 * C) ** -0.5, 0.125, ((0, 32),))
    projection = gaussian(splits[4], (E * C,), E ** -0.5, 0.25, ((0, 32),))
    vectors = draw_vectors(jax.random.fold_in(splits[7], 71), 0)
    cotangent = gaussian(splits[6], (IMAGES, H, W, C), 1.0, 6.0, ((0, 32),))
    return dict(images=images, embedding=embedding, conv_first=conv_first, conv_second=conv_second, projection=projection, vectors=vectors, cotangent=cotangent)


@jax.custom_vjp
def low(v):
    return lax.optimization_barrier(v.astype(jnp.bfloat16)).astype(jnp.float32)

@jax.custom_vjp
def low_back(v):
    return v

def low_keep(v):
    return (low(v), None)

def low_pass(kept, grad):
    return (grad,)

def back_keep(v):
    return (v, None)

def back_low(kept, grad):
    return (low(grad),)
low.defvjp(low_keep, low_pass)
low_back.defvjp(back_keep, back_low)
EPS = 1e-05

def norm_group(values, gain, shift):
    grouped = values.reshape(H, W, GROUPS, C // GROUPS)
    centre = lax.optimization_barrier(jnp.mean(grouped, axis=(0, 1, 3), keepdims=True))
    centred = grouped - centre
    spread = lax.optimization_barrier(jnp.mean(centred * centred, axis=(0, 1, 3), keepdims=True))
    return (centred * lax.rsqrt(spread + EPS)).reshape(H, W, C) * gain + shift

def convolve(inputs, kernel):
    return lax.conv_general_dilated(inputs[None], kernel, (1, 1), 'SAME', dimension_numbers=('NHWC', 'HWIO', 'NHWC'), precision=lax.Precision.HIGHEST)[0]

def block(image, emb_vec, kernel_one, kernel_two, project, vector):
    act_one = low(jax.nn.silu(norm_group(image, vector[0], vector[1])))
    emb_act = low(jax.nn.silu(emb_vec))
    offset = jnp.dot(emb_act, project, precision=lax.Precision.HIGHEST)
    middle = low_back(convolve(act_one, kernel_one)) + vector[2] + offset
    act_two = low(jax.nn.silu(norm_group(middle, vector[3], vector[4])))
    return image + low_back(convolve(act_two, kernel_two)) + vector[5]

def reference(images, embedding, conv_first, conv_second, projection, vectors, cotangent):
    kernel_one = conv_first.astype(jnp.float32).reshape(3, 3, C, C)
    kernel_two = conv_second.astype(jnp.float32).reshape(3, 3, C, C)
    project = projection.astype(jnp.float32).reshape(E, C)
    vector = vectors.astype(jnp.float32).reshape(6, C)

    def one_image(totals, items):
        image, emb_vec, cot_map = items
        result, pullback = jax.vjp(block, image.astype(jnp.float32), emb_vec.astype(jnp.float32), kernel_one, kernel_two, project, vector)
        grads = pullback(cot_map.astype(jnp.float32))
        totals = jax.tree.map(jnp.add, totals, tuple(grads[2:]))
        return (totals, (result.astype(jnp.bfloat16), grads[0], grads[1]))
    zeros = (jnp.zeros_like(kernel_one), jnp.zeros_like(kernel_two), jnp.zeros_like(project), jnp.zeros_like(vector))
    totals, outputs = lax.scan(one_image, zeros, (images, embedding, cotangent))
    return (outputs[0], outputs[1], outputs[2], totals[0].reshape(-1), totals[1].reshape(-1), totals[2].reshape(-1), totals[3].reshape(-1))
```

```python
import math

import jax
import jax.numpy as jnp
from jax import lax
from jax.sharding import PartitionSpec as P

GROUPS = 32
EPS = 1e-05
AXES = ("dp", "fsdp")


class Wires:
    def __init__(self, n_dp, n_fsdp):
        self.n = n_dp * n_fsdp
        self.bits = int(math.log2(self.n))
        fsdp_bits = int(math.log2(n_fsdp))
        assert 1 << self.bits == self.n and 1 << fsdp_bits == n_fsdp and fsdp_bits >= 2 and n_dp >= 2
        self.cross_a = 1
        self.cross_b = fsdp_bits
        self.far = [b for b in range(self.bits - 1, 0, -1) if b not in (self.cross_a, self.cross_b)]
        self.me = lax.axis_index(AXES)
        self.core = self.me & 1

    def bit(self, b):
        return (self.me >> b) & 1

    def swap(self, value, b):
        return lax.ppermute(value, AXES, [(i, i ^ (1 << b)) for i in range(self.n)])

    def swap_cross(self, value, first):
        even, odd = (self.cross_a, self.cross_b) if first else (self.cross_b, self.cross_a)
        return lax.ppermute(
            value, AXES, [(i, i ^ (1 << (odd if i & 1 else even))) for i in range(self.n)]
        )

    def cross_bit(self, first):
        a, b = self.bit(self.cross_a), self.bit(self.cross_b)
        return jnp.where(self.core == (0 if first else 1), a, b)


def merge(mine, other, axis, bit):
    mine, other = jnp.expand_dims(mine, axis), jnp.expand_dims(other, axis)
    shape = list(mine.shape)
    shape[axis] = 2
    place = lax.broadcasted_iota(jnp.int32, shape, axis)
    return jnp.where(place == bit, mine, other)


def gather(wires, parts):
    bufs = list(parts)
    far = sorted(wires.far, reverse=True)
    for at, b in enumerate(far):
        got = [wires.swap(v, b) for v in bufs]
        bufs = [merge(v, r, at, wires.bit(b)) for v, r in zip(bufs, got)]
    depth = len(far)
    got = [wires.swap_cross(v, True) for v in bufs]
    bufs = [merge(v, r, depth, wires.cross_bit(True)) for v, r in zip(bufs, got)]
    got = [wires.swap_cross(v, False) for v in bufs]
    bufs = [merge(v, r, 0, wires.cross_bit(False)) for v, r in zip(bufs, got)]
    bufs = [jnp.where(wires.core == 0, v, jnp.swapaxes(v, 0, depth + 1)) for v in bufs]
    got = [wires.swap(v, 0) for v in bufs]
    bufs = [merge(v, r, depth + 2, wires.core) for v, r in zip(bufs, got)]
    order = [wires.cross_b, *far, wires.cross_a, 0]
    want = sorted(order, reverse=True)
    out = []
    for v in bufs:
        rest = list(range(len(order), v.ndim))
        v = v.transpose([order.index(b) for b in want] + rest)
        out.append(v.reshape((wires.n,) + v.shape[len(order):]))
    return out


def pick(value, axis, index):
    return lax.dynamic_index_in_dim(value, index, axis, keepdims=False)


def reduce_scatter(wires, value):
    far = sorted(wires.far, reverse=True)
    order = [wires.cross_b, *far, wires.cross_a, 0]
    want = sorted(order, reverse=True)
    v = value.reshape((2,) * len(order) + value.shape[1:])
    rest = list(range(len(order), v.ndim))
    v = v.transpose([want.index(b) for b in order] + rest)
    depth = len(far)

    def step(v, axis, bit, swap):
        sent = pick(v, axis, 1 - bit).astype(jnp.bfloat16)
        return pick(v, axis, bit) + swap(sent).astype(jnp.float32)

    v = step(v, depth + 2, wires.core, lambda s: wires.swap(s, 0))
    v = jnp.where(wires.core == 0, v, jnp.swapaxes(v, 0, depth + 1))
    v = step(v, depth + 1, wires.cross_bit(True), lambda s: wires.swap_cross(s, True))
    v = step(v, 0, wires.cross_bit(False), lambda s: wires.swap_cross(s, False))
    for at in range(len(far) - 1, -1, -1):
        b = far[at]
        v = step(v, at, wires.bit(b), lambda s, b=b: wires.swap(s, b))
    return v


def convolve(inputs, kernel):
    return lax.conv_general_dilated(
        inputs,
        kernel,
        (1, 1),
        "SAME",
        dimension_numbers=("NHWC", "HWIO", "NHWC"),
        preferred_element_type=jnp.float32,
    )


def convolve_back(grads, kernel):
    return convolve(grads, jnp.flip(kernel, (0, 1)).transpose(0, 1, 3, 2))


def kernel_grad(inputs, grads):
    height = inputs.shape[1]
    width = inputs.shape[2]
    padded = jnp.pad(inputs, ((0, 0), (1, 1), (1, 1), (0, 0)))
    taps = []
    for shift_row in range(3):
        for shift_col in range(3):
            window = padded[:, shift_row : shift_row + height, shift_col : shift_col + width, :]
            taps.append(
                lax.dot_general(
                    window,
                    grads,
                    (((0, 1, 2), (0, 1, 2)), ((), ())),
                    preferred_element_type=jnp.float32,
                )
            )
    return jnp.stack(taps).reshape(-1)


def group_spread(totals, count):
    grouped = totals.reshape(totals.shape[0], GROUPS, -1)
    return jnp.repeat(grouped.sum(-1) / count, grouped.shape[-1], axis=-1)


def normalize(values):
    count = values.shape[1] * values.shape[2] * (values.shape[3] // GROUPS)
    centre = group_spread(jnp.sum(values, (1, 2)), count)
    centred = values - centre[:, None, None, :]
    spread = group_spread(jnp.sum(centred * centred, (1, 2)), count)
    scale_inv = lax.rsqrt(spread + EPS)
    return (centred * scale_inv[:, None, None, :], scale_inv)


def norm_back(grad_out, normed, scale_inv, gain):
    count = normed.shape[1] * normed.shape[2] * (normed.shape[3] // GROUPS)
    scaled = grad_out * gain
    first = group_spread(jnp.sum(scaled, (1, 2)), count)
    second = group_spread(jnp.sum(scaled * normed, (1, 2)), count)
    grad_in = scale_inv[:, None, None, :] * (
        scaled - first[:, None, None, :] - normed * second[:, None, None, :]
    )
    return (grad_in, jnp.sum(grad_out * normed, (0, 1, 2)), jnp.sum(grad_out, (0, 1, 2)))


def swish_slope(values):
    sigma = jax.nn.sigmoid(values)
    return sigma * (1.0 + values * (1.0 - sigma))


def local(sizes, images, embedding, conv_first, conv_second, projection, vectors, cotangent):
    channels = images.shape[-1]
    emb_width = embedding.shape[-1]
    wires = Wires(*sizes)
    n = wires.n
    n_vec = vectors.shape[0]
    rows_conv = conv_first.shape[0] // channels
    rows_proj = projection.shape[0] // channels
    rows_vec = -(-n_vec // channels)

    def vec_rows(v):
        return jnp.pad(v, ((0, 0), (0, rows_vec * channels - n_vec))).reshape(-1, rows_vec, channels)

    small = jnp.concatenate([projection.reshape(rows_proj, channels), vec_rows(vectors[None])[0]])
    one, small = gather(wires, [conv_first.reshape(rows_conv, channels), small])
    two, = gather(wires, [conv_second.reshape(rows_conv, channels)])
    kernel_one = one.reshape(3, 3, channels, channels)
    kernel_two = two.reshape(3, 3, channels, channels)
    project = small[:, :rows_proj].reshape(emb_width, channels)
    vector = small[:, rows_proj:].reshape(n, -1)[:, :n_vec].reshape(6, channels).astype(jnp.float32)

    inputs = images.astype(jnp.float32)
    normed_one, inv_one = normalize(inputs)
    pre_one = normed_one * vector[0] + vector[1]
    act_one = jax.nn.silu(pre_one).astype(jnp.bfloat16)
    emb_float = embedding.astype(jnp.float32)
    emb_act = jax.nn.silu(emb_float).astype(jnp.bfloat16)
    offset = jnp.dot(emb_act, project, preferred_element_type=jnp.float32)
    middle = convolve(act_one, kernel_one) + vector[2] + offset[:, None, None, :]
    normed_two, inv_two = normalize(middle)
    pre_two = normed_two * vector[3] + vector[4]
    act_two = jax.nn.silu(pre_two).astype(jnp.bfloat16)
    output = (inputs + convolve(act_two, kernel_two) + vector[5]).astype(jnp.bfloat16)
    grad_top = cotangent.astype(jnp.float32)
    bias_two_grad = jnp.sum(grad_top, (0, 1, 2))
    kernel_two_grad = kernel_grad(act_two, cotangent)
    second_sum = reduce_scatter(wires, kernel_two_grad.reshape(n, rows_conv, channels))
    grad_act_two = convolve_back(cotangent, kernel_two)
    grad_pre_two = grad_act_two * swish_slope(pre_two)
    grad_middle, gain_two_grad, shift_two_grad = norm_back(
        grad_pre_two, normed_two, inv_two, vector[3]
    )
    bias_one_grad = jnp.sum(grad_middle, (0, 1, 2))
    grad_offset = jnp.sum(grad_middle, (1, 2))
    project_grad = jnp.dot(
        emb_act.astype(jnp.float32).T, grad_offset, precision=lax.Precision.HIGHEST
    )
    grad_emb_act = jnp.dot(
        grad_offset, project.astype(jnp.float32).T, precision=lax.Precision.HIGHEST
    )
    embedding_grad = grad_emb_act * swish_slope(emb_float)
    middle_low = grad_middle.astype(jnp.bfloat16)
    kernel_one_grad = kernel_grad(act_one, middle_low)
    first_sum = reduce_scatter(wires, kernel_one_grad.reshape(n, rows_conv, channels))
    grad_act_one = convolve_back(middle_low, kernel_one)
    grad_pre_one = grad_act_one * swish_slope(pre_one)
    grad_normed, gain_one_grad, shift_one_grad = norm_back(
        grad_pre_one, normed_one, inv_one, vector[0]
    )
    input_grad = grad_top + grad_normed
    vector_grad = jnp.concatenate(
        [gain_one_grad, shift_one_grad, bias_one_grad, gain_two_grad, shift_two_grad, bias_two_grad]
    )
    small_grad = jnp.concatenate(
        [project_grad.reshape(n, rows_proj, channels), vec_rows(vector_grad.reshape(n, n_vec))], axis=1
    )
    small_sum = reduce_scatter(wires, small_grad)
    return (
        output,
        input_grad,
        embedding_grad,
        first_sum.reshape(-1),
        second_sum.reshape(-1),
        small_sum[:rows_proj].reshape(-1),
        small_sum[rows_proj:].reshape(-1)[:n_vec],
    )


def solution(mesh):
    sizes = (mesh.shape["dp"], mesh.shape["fsdp"])
    split = P(AXES)
    maps = P(AXES, None, None, None)
    in_specs = (maps, P(AXES, None), split, split, split, split, maps)
    out_specs = (maps, maps, P(AXES, None), split, split, split, split)

    def body(*args):
        return local(sizes, *args)

    return jax.shard_map(body, mesh=mesh, in_specs=in_specs, out_specs=out_specs, check_vma=False)
```

```python
import functools
import math

import jax
import jax.numpy as jnp
from jax import lax
from jax.experimental import pallas as pl
from jax.experimental.pallas import tpu as pltpu
from jax.sharding import PartitionSpec as P

GROUPS = 32
EPS = 1e-05
AXES = ("dp", "fsdp")


class Wires:
    def __init__(self, n_dp, n_fsdp):
        self.n = n_dp * n_fsdp
        self.bits = int(math.log2(self.n))
        fsdp_bits = int(math.log2(n_fsdp))
        assert 1 << self.bits == self.n and 1 << fsdp_bits == n_fsdp and fsdp_bits >= 2 and n_dp >= 2
        self.cross_a = 1
        self.cross_b = fsdp_bits
        self.far = [b for b in range(self.bits - 1, 0, -1) if b not in (self.cross_a, self.cross_b)]
        self.me = lax.axis_index(AXES)
        self.core = self.me & 1

    def bit(self, b):
        return (self.me >> b) & 1

    def swap(self, value, b):
        return lax.ppermute(value, AXES, [(i, i ^ (1 << b)) for i in range(self.n)])

    def swap_cross(self, value, first):
        even, odd = (self.cross_a, self.cross_b) if first else (self.cross_b, self.cross_a)
        return lax.ppermute(
            value, AXES, [(i, i ^ (1 << (odd if i & 1 else even))) for i in range(self.n)]
        )

    def cross_bit(self, first):
        a, b = self.bit(self.cross_a), self.bit(self.cross_b)
        return jnp.where(self.core == (0 if first else 1), a, b)


def merge(mine, other, axis, bit):
    mine, other = jnp.expand_dims(mine, axis), jnp.expand_dims(other, axis)
    shape = list(mine.shape)
    shape[axis] = 2
    place = lax.broadcasted_iota(jnp.int32, shape, axis)
    return jnp.where(place == bit, mine, other)


def gather(wires, parts):
    bufs = list(parts)
    far = sorted(wires.far, reverse=True)
    for at, b in enumerate(far):
        got = [wires.swap(v, b) for v in bufs]
        bufs = [merge(v, r, at, wires.bit(b)) for v, r in zip(bufs, got)]
    depth = len(far)
    got = [wires.swap_cross(v, True) for v in bufs]
    bufs = [merge(v, r, depth, wires.cross_bit(True)) for v, r in zip(bufs, got)]
    got = [wires.swap_cross(v, False) for v in bufs]
    bufs = [merge(v, r, 0, wires.cross_bit(False)) for v, r in zip(bufs, got)]
    bufs = [jnp.where(wires.core == 0, v, jnp.swapaxes(v, 0, depth + 1)) for v in bufs]
    got = [wires.swap(v, 0) for v in bufs]
    bufs = [merge(v, r, depth + 2, wires.core) for v, r in zip(bufs, got)]
    order = [wires.cross_b, *far, wires.cross_a, 0]
    want = sorted(order, reverse=True)
    out = []
    for v in bufs:
        rest = list(range(len(order), v.ndim))
        v = v.transpose([order.index(b) for b in want] + rest)
        out.append(v.reshape((wires.n,) + v.shape[len(order):]))
    return out


def pick(value, axis, index):
    return lax.dynamic_index_in_dim(value, index, axis, keepdims=False)


def reduce_scatter(wires, value):
    far = sorted(wires.far, reverse=True)
    order = [wires.cross_b, *far, wires.cross_a, 0]
    want = sorted(order, reverse=True)
    v = value.reshape((2,) * len(order) + value.shape[1:])
    rest = list(range(len(order), v.ndim))
    v = v.transpose([want.index(b) for b in order] + rest)
    depth = len(far)

    def step(v, axis, bit, swap):
        sent = pick(v, axis, 1 - bit).astype(jnp.bfloat16)
        return pick(v, axis, bit) + swap(sent).astype(jnp.float32)

    v = step(v, depth + 2, wires.core, lambda s: wires.swap(s, 0))
    v = jnp.where(wires.core == 0, v, jnp.swapaxes(v, 0, depth + 1))
    v = step(v, depth + 1, wires.cross_bit(True), lambda s: wires.swap_cross(s, True))
    v = step(v, 0, wires.cross_bit(False), lambda s: wires.swap_cross(s, False))
    for at in range(len(far) - 1, -1, -1):
        b = far[at]
        v = step(v, at, wires.bit(b), lambda s, b=b: wires.swap(s, b))
    return v


ROWS = 16
F32 = jnp.float32
BF16 = jnp.bfloat16
VMEM_BYTES = 44 * 1024 * 1024


def group_sum(totals):
    channels = totals.shape[1]
    lane = lax.broadcasted_iota(jnp.int32, totals.shape, 1)
    span = 1
    while span < channels // GROUPS:
        up = pltpu.roll(totals, channels - span, 1)
        down = pltpu.roll(totals, span, 1)
        totals = totals + jnp.where((lane & span) == 0, up, down)
        span *= 2
    return totals


def fold(values):
    channels = values.shape[-1]
    return jnp.sum(values.reshape(-1, 8, channels), 0)


def total(partial):
    return jnp.sum(partial, 0, keepdims=True)


def sigmoid(v):
    return 0.5 * jnp.tanh(0.5 * v) + 0.5


def clear_edges(three):
    height = three.shape[1] - 2
    zero = jnp.zeros((3, 1) + three.shape[2:], three.dtype)
    three[:, 0:1] = zero
    three[:, height + 1 : height + 2] = zero


def store_three(three, row, value):
    width = value.shape[0]
    column = lax.broadcasted_iota(jnp.int32, value.shape, 0)
    left = jnp.where(column == 0, 0.0, pltpu.roll(value, 1, 0))
    right = jnp.where(column == width - 1, 0.0, pltpu.roll(value, width - 1, 0))
    three[0, row + 1] = left.astype(three.dtype)
    three[1, row + 1] = value.astype(three.dtype)
    three[2, row + 1] = right.astype(three.dtype)


def conv_rows(three, kernel, start, back):
    width, channels = three.shape[2:]
    acc = None
    for tap in range(9):
        lhs = three[tap % 3, pl.ds(start + tap // 3, ROWS)].reshape(ROWS * width, channels)
        at = (8 - tap if back else tap) * channels
        rhs = kernel[at : at + channels, :]
        part = lax.dot_general(
            lhs, rhs, (((1,), (1 if back else 0,)), ((), ())), preferred_element_type=F32
        )
        acc = part if acc is None else acc + part
    return acc


def kernel_grad(acts, three, out):
    height, width, channels = acts.shape

    def step(tap, _):
        row = tap // 3
        col = tap - 3 * row
        lhs = acts[...].reshape(height * width, channels)
        rhs = three[2 - col, pl.ds(2 - row, height)].reshape(height * width, channels)
        out[pl.ds(pl.multiple_of(tap * channels, channels), channels), :] = lax.dot_general(
            lhs, rhs, (((0,), (0,)), ((), ())), preferred_element_type=F32
        )
        return 0

    lax.fori_loop(0, 9, step, 0)


def prepare_kernel(x, g, stats, three, g_sum):
    height, width, channels = x.shape
    count = height * width * (channels // GROUPS)
    zero = jnp.zeros((8, channels), F32)
    clear_edges(three)

    def first(i, carry):
        s, gs = carry
        row = i * 4
        s = s + fold(x[pl.ds(row, 4)].astype(F32))
        rows = g[pl.ds(row, 4)].astype(F32)
        for j in range(4):
            store_three(three, row + j, rows[j])
        return s, gs + fold(rows)

    s, gs = lax.fori_loop(0, height // 4, first, (zero, zero))
    g_sum[...] = total(gs)
    mean = group_sum(total(s)) / count

    def second(i, v):
        d = x[pl.ds(i * 4, 4)].astype(F32) - mean
        return v + fold(d * d)

    v = lax.fori_loop(0, height // 4, second, zero)
    inv = lax.rsqrt(group_sum(total(v)) / count + EPS)
    stats[0:1, :] = mean
    stats[1:2, :] = inv


def first_kernel(x, stats, vec, time, kernel, act, centred, stats_out, three):
    height, width, channels = x.shape
    count = height * width * (channels // GROUPS)
    mean, scale, shift = stats[0:1, :], stats[1:2, :] * vec[0:1, :], vec[1:2, :]
    offset = vec[2:3, :] + time[...]
    zero = jnp.zeros((8, channels), F32)
    clear_edges(three)

    def activate(i, _):
        row = i * 4
        h = (x[pl.ds(row, 4)].astype(F32) - mean) * scale + shift
        a = h * sigmoid(h)
        act[pl.ds(row, 4)] = a.astype(BF16)
        for j in range(4):
            store_three(three, row + j, a[j])
        return 0

    lax.fori_loop(0, height // 4, activate, 0)

    def conv(i, s):
        row = pl.multiple_of(i * ROWS, ROWS)
        acc = conv_rows(three, kernel, row, False)
        centred[pl.ds(row * width, ROWS * width), :] = acc
        return s + fold(acc)

    s = lax.fori_loop(0, height // ROWS, conv, zero)
    mean_two = group_sum(total(s) / (height * width) + offset) / (channels // GROUPS)
    move = offset - mean_two

    def centre(i, v):
        at = pl.ds(i * 256, 256)
        d = centred[at, :] + move
        centred[at, :] = d
        return v + fold(d * d)

    v = lax.fori_loop(0, height * width // 256, centre, zero)
    stats_out[...] = lax.rsqrt(group_sum(total(v)) / count + EPS)


def second_kernel(three, centred, inv, vec, kernel, dh, act, sums, grad):
    height, width, channels = act.shape
    scale, shift = inv[...] * vec[3:4, :], vec[4:5, :]
    zero = jnp.zeros((8, channels), F32)

    def conv(i, carry):
        s, sc = carry
        row = pl.multiple_of(i * ROWS, ROWS)
        at = pl.ds(row * width, ROWS * width)
        acc = conv_rows(three, kernel, row, True)
        c = centred[at, :]
        h = c * scale + shift
        sig = sigmoid(h)
        a = h * sig
        act[pl.ds(row, ROWS)] = a.astype(BF16).reshape(ROWS, width, channels)
        d = acc * (sig + a * (1.0 - sig))
        dh[at, :] = d
        return s + fold(d), sc + fold(d * c)

    s, sc = lax.fori_loop(0, height // ROWS, conv, (zero, zero))
    sums[0:1, :] = total(sc) * inv[...]
    sums[1:2, :] = total(s)
    kernel_grad(act, three, grad)


def third_kernel(dh, centred, inv, sums, vec, act, three, dc_sum, grad):
    height, width, channels = act.shape
    count = height * width * (channels // GROUPS)
    gain = vec[3:4, :]
    mean_u = group_sum(sums[1:2, :] * gain) / count
    mean_un = group_sum(sums[0:1, :] * gain) / count
    scale = inv[...] * gain
    base = inv[...] * mean_u
    slope = inv[...] * inv[...] * mean_un
    clear_edges(three)

    def back(i, s):
        row = i * 4
        at = pl.ds(row * width, 4 * width)
        d = dh[at, :] * scale - base - centred[at, :] * slope
        rows = d.reshape(4, width, channels)
        for j in range(4):
            store_three(three, row + j, rows[j])
        return s + fold(d)

    dc_sum[...] = total(lax.fori_loop(0, height // 4, back, jnp.zeros((8, channels), F32)))
    kernel_grad(act, three, grad)


def fourth_kernel(three, x, g, stats, vec, kernel, result, sums, dh):
    height, width, channels = x.shape
    count = height * width * (channels // GROUPS)
    mean, inv, gain, shift = stats[0:1, :], stats[1:2, :], vec[0:1, :], vec[1:2, :]
    scale = inv * gain
    zero = jnp.zeros((8, channels), F32)

    def conv(i, carry):
        s, sn = carry
        row = pl.multiple_of(i * ROWS, ROWS)
        acc = conv_rows(three, kernel, row, True)
        c = x[pl.ds(row, ROWS)].astype(F32).reshape(ROWS * width, channels) - mean
        h = c * scale + shift
        sig = sigmoid(h)
        d = acc * (sig + h * sig * (1.0 - sig))
        dh[pl.ds(row * width, ROWS * width), :] = d
        return s + fold(d), sn + fold(d * c)

    s, sn = lax.fori_loop(0, height // ROWS, conv, (zero, zero))
    s, sn = total(s), total(sn) * inv
    sums[0:1, :] = sn
    sums[1:2, :] = s
    base = inv * (group_sum(s * gain) / count)
    slope = inv * inv * (group_sum(sn * gain) / count)

    def back(i, _):
        row = i * 4
        d = dh[pl.ds(row * width, 4 * width), :].reshape(4, width, channels)
        c = x[pl.ds(row, 4)].astype(F32) - mean
        result[pl.ds(row, 4)] = g[pl.ds(row, 4)].astype(F32) + (d * scale - base - c * slope)
        return 0

    lax.fori_loop(0, height // 4, back, 0)


def last_kernel(act, x, vec, kernel, result, three):
    height, width, channels = x.shape
    bias = vec[5:6, :]
    clear_edges(three)

    def spread(i, _):
        rows = act[pl.ds(i * 4, 4)].astype(F32)
        for j in range(4):
            store_three(three, i * 4 + j, rows[j])
        return 0

    lax.fori_loop(0, height // 4, spread, 0)

    def conv(i, _):
        row = pl.multiple_of(i * ROWS, ROWS)
        acc = conv_rows(three, kernel, row, False).reshape(ROWS, width, channels)
        result[pl.ds(row, ROWS)] = (x[pl.ds(row, ROWS)].astype(F32) + acc + bias).astype(BF16)
        return 0

    lax.fori_loop(0, height // ROWS, conv, 0)


def call(body, outs, *args, scratch=(), flops=0):
    return pl.pallas_call(
        body,
        out_shape=[jax.ShapeDtypeStruct(shape, dtype) for shape, dtype in outs],
        scratch_shapes=[pltpu.VMEM(shape, dtype) for shape, dtype in scratch],
        compiler_params=pltpu.CompilerParams(vmem_limit_bytes=VMEM_BYTES),
        cost_estimate=pl.CostEstimate(flops=flops, bytes_accessed=4 << 20, transcendentals=0),
    )(*args)


def swish_slope(values):
    sigma = jax.nn.sigmoid(values)
    return sigma * (1.0 + values * (1.0 - sigma))


def local(sizes, images, embedding, conv_first, conv_second, projection, vectors, cotangent):
    count, height, width, channels = images.shape
    assert count == 1
    emb_width = embedding.shape[-1]
    wires = Wires(*sizes)
    n = wires.n
    n_vec = vectors.shape[0]
    rows_conv = conv_first.shape[0] // channels
    rows_proj = projection.shape[0] // channels
    rows_vec = -(-n_vec // channels)
    pixels = height * width
    three = ((3, height + 2, width, channels), BF16)
    maps = ((height, width, channels), BF16)
    flat = ((pixels, channels), F32)
    line = ((1, channels), F32)
    pair = ((2, channels), F32)
    taps = ((9 * channels, channels), F32)
    conv_flops = 2 * 9 * pixels * channels * channels

    def vec_rows(v):
        return jnp.pad(v, ((0, 0), (0, rows_vec * channels - n_vec))).reshape(-1, rows_vec, channels)

    x, g = images[0], cotangent[0]
    stats_one, g_three, g_sum = call(prepare_kernel, [pair, three, line], x, g)

    small = jnp.concatenate([projection.reshape(rows_proj, channels), vec_rows(vectors[None])[0]])
    one, small = gather(wires, [conv_first.reshape(rows_conv, channels), small])
    two, = gather(wires, [conv_second.reshape(rows_conv, channels)])
    kernel_one = one.reshape(9 * channels, channels)
    kernel_two = two.reshape(9 * channels, channels)
    project = small[:, :rows_proj].reshape(emb_width, channels)
    vector = small[:, rows_proj:].reshape(n, -1)[:, :n_vec].reshape(6, channels).astype(F32)

    emb_float = embedding.astype(F32)
    emb_act = jax.nn.silu(emb_float).astype(BF16)
    time = jnp.dot(emb_act, project, preferred_element_type=F32)
    act_one, centred, inv_two = call(
        first_kernel, [maps, flat, line], x, stats_one, vector, time, kernel_one, scratch=[three], flops=conv_flops
    )
    dh, act_two, sums_two, grad_two = call(
        second_kernel,
        [flat, maps, pair, taps],
        g_three,
        centred,
        inv_two,
        vector,
        kernel_two,
        flops=2 * conv_flops,
    )
    second_sum = reduce_scatter(wires, grad_two.reshape(n, rows_conv, channels))
    e_three, dc_sum, grad_one = call(
        third_kernel, [three, line, taps], dh, centred, inv_two, sums_two, vector, act_one, flops=conv_flops
    )
    first_sum = reduce_scatter(wires, grad_one.reshape(n, rows_conv, channels))
    project_grad = emb_act.astype(F32).reshape(emb_width, 1) * dc_sum
    grad_emb_act = jnp.dot(dc_sum, project.astype(F32).T, precision=lax.Precision.HIGHEST)
    embedding_grad = grad_emb_act * swish_slope(emb_float)
    input_grad, sums_one = call(
        fourth_kernel, [(maps[0], F32), pair], e_three, x, g, stats_one, vector, kernel_one, scratch=[flat], flops=conv_flops
    )
    vector_grad = jnp.concatenate([sums_one, dc_sum, sums_two, g_sum]).reshape(-1)
    small_grad = jnp.concatenate(
        [project_grad.reshape(n, rows_proj, channels), vec_rows(vector_grad.reshape(n, n_vec))], axis=1
    )
    small_sum = reduce_scatter(wires, small_grad)
    output, = call(last_kernel, [maps], act_two, x, vector, kernel_two, scratch=[three], flops=conv_flops)
    return (
        output[None],
        input_grad[None],
        embedding_grad,
        first_sum.reshape(-1),
        second_sum.reshape(-1),
        small_sum[:rows_proj].reshape(-1),
        small_sum[rows_proj:].reshape(-1)[:n_vec],
    )


def solution(mesh):
    sizes = (mesh.shape["dp"], mesh.shape["fsdp"])
    split = P(AXES)
    maps = P(AXES, None, None, None)
    in_specs = (maps, P(AXES, None), split, split, split, split, maps)
    out_specs = (maps, maps, P(AXES, None), split, split, split, split)

    def body(*args):
        return local(sizes, *args)

    return jax.shard_map(body, mesh=mesh, in_specs=in_specs, out_specs=out_specs, check_vma=False)
```

```python
import functools
import math

import jax
import jax.numpy as jnp
from jax import lax
from jax.experimental import pallas as pl
from jax.experimental.pallas import tpu as pltpu
from jax.sharding import PartitionSpec as P

GROUPS = 32
EPS = 1e-05
AXES = ("dp", "fsdp")
LANES = 128
VEC_ROWS = 16


class Wires:
    def __init__(self, n_dp, n_fsdp):
        self.n_fsdp = n_fsdp
        self.n = n_dp * n_fsdp
        self.bits = int(math.log2(self.n))
        fsdp_bits = int(math.log2(n_fsdp))
        assert 1 << self.bits == self.n and 1 << fsdp_bits == n_fsdp and fsdp_bits >= 2 and n_dp >= 2
        a, b = 1, fsdp_bits
        far = [bit for bit in range(self.bits - 1, 0, -1) if bit not in (a, b)]
        self.order = {0: [*far, a, b], 1: [*far, b, a]}
        self.stages = self.bits - 1
        self.slots = 1 << self.stages

    def swap(self, value, stage):
        bit = (lambda i: 0) if stage == self.stages else (lambda i: self.order[i & 1][stage])
        return lax.ppermute(value, AXES, [(i, i ^ (1 << bit(i))) for i in range(self.n)])

    def mask(self, slot, core):
        return sum(1 << self.order[core][i] for i in range(self.stages) if slot >> i & 1)

    def me(self):
        return lax.axis_index("dp") * self.n_fsdp + lax.axis_index("fsdp")

    def owner(self, slot, other, me):
        core = me & 1
        if other:
            me, core = me ^ 1, 1 - core
        return me ^ jnp.where(core == 0, self.mask(slot, 0), self.mask(slot, 1))


ROWS = 16
F32 = jnp.float32
BF16 = jnp.bfloat16
VMEM_BYTES = 14 * 1024 * 1024


def group_sum(totals):
    channels = totals.shape[1]
    lane = lax.broadcasted_iota(jnp.int32, totals.shape, 1)
    span = 1
    while span < channels // GROUPS:
        up = pltpu.roll(totals, channels - span, 1)
        down = pltpu.roll(totals, span, 1)
        totals = totals + jnp.where((lane & span) == 0, up, down)
        span *= 2
    return totals


def fold(values):
    channels = values.shape[-1]
    return jnp.sum(values.reshape(-1, 8, channels), 0)


def total(partial):
    return jnp.sum(partial, 0, keepdims=True)


def sigmoid(v):
    return 0.5 * jnp.tanh(0.5 * v) + 0.5


def clear_edges(three):
    height = three.shape[1] - 2
    zero = jnp.zeros((3, 1) + three.shape[2:], three.dtype)
    three[:, 0:1] = zero
    three[:, height + 1 : height + 2] = zero


def store_three(three, row, value):
    width = value.shape[0]
    column = lax.broadcasted_iota(jnp.int32, value.shape, 0)
    left = jnp.where(column == 0, 0.0, pltpu.roll(value, 1, 0))
    right = jnp.where(column == width - 1, 0.0, pltpu.roll(value, width - 1, 0))
    three[0, row + 1] = left.astype(three.dtype)
    three[1, row + 1] = value.astype(three.dtype)
    three[2, row + 1] = right.astype(three.dtype)


def conv_rows(three, kernel, start, back):
    width, channels = three.shape[2:]
    acc = None
    for tap in range(9):
        lhs = three[tap % 3, pl.ds(start + tap // 3, ROWS)].reshape(ROWS * width, channels)
        at = (8 - tap if back else tap) * channels
        rhs = kernel[at : at + channels, :]
        part = lax.dot_general(
            lhs, rhs, (((1,), (1 if back else 0,)), ((), ())), preferred_element_type=F32
        )
        acc = part if acc is None else acc + part
    return acc


def store_flat(flat, start, value):
    rows = value.shape[0]
    flat[pl.ds(start, rows, stride=2), :] = value[:, :LANES]
    flat[pl.ds(start + 1, rows, stride=2), :] = value[:, LANES:]


def load_flat(flat, start, rows):
    left = flat[pl.ds(start, rows, stride=2), :]
    right = flat[pl.ds(start + 1, rows, stride=2), :]
    return jnp.concatenate([left, right], axis=1)


def kernel_grad(acts, three, flat):
    height, width, channels = acts.shape

    def step(tap, _):
        row = tap // 3
        col = tap - 3 * row
        lhs = acts[...].reshape(height * width, channels)
        rhs = three[2 - col, pl.ds(2 - row, height)].reshape(height * width, channels)
        out = lax.dot_general(lhs, rhs, (((0,), (0,)), ((), ())), preferred_element_type=F32)
        store_flat(flat, pl.multiple_of(tap * 2 * channels, 2 * channels), out)
        return 0

    lax.fori_loop(0, 9, step, 0)


def prepare_kernel(x, g, stats, three, g_sum):
    height, width, channels = x.shape
    count = height * width * (channels // GROUPS)
    zero = jnp.zeros((8, channels), F32)
    clear_edges(three)

    def first(i, carry):
        s, gs = carry
        row = i * 4
        s = s + fold(x[pl.ds(row, 4)].astype(F32))
        rows = g[pl.ds(row, 4)].astype(F32)
        for j in range(4):
            store_three(three, row + j, rows[j])
        return s, gs + fold(rows)

    s, gs = lax.fori_loop(0, height // 4, first, (zero, zero))
    g_sum[...] = total(gs)
    mean = group_sum(total(s)) / count

    def second(i, v):
        d = x[pl.ds(i * 4, 4)].astype(F32) - mean
        return v + fold(d * d)

    v = lax.fori_loop(0, height // 4, second, zero)
    inv = lax.rsqrt(group_sum(total(v)) / count + EPS)
    stats[0:1, :] = mean
    stats[1:2, :] = inv


def first_kernel(x, stats, vec, q, kernel, act, centred, stats_out, three):
    height, width, channels = x.shape
    count = height * width * (channels // GROUPS)
    mean, scale, shift = stats[0:1, :], stats[1:2, :] * vec[0:1, :], vec[1:2, :]
    time = jnp.dot(q[...], kernel[9 * channels :, :], preferred_element_type=F32)
    offset = vec[2:3, :] + time
    zero = jnp.zeros((8, channels), F32)
    clear_edges(three)

    def activate(i, _):
        row = i * 4
        h = (x[pl.ds(row, 4)].astype(F32) - mean) * scale + shift
        a = h * sigmoid(h)
        act[pl.ds(row, 4)] = a.astype(BF16)
        for j in range(4):
            store_three(three, row + j, a[j])
        return 0

    lax.fori_loop(0, height // 4, activate, 0)

    def conv(i, s):
        row = pl.multiple_of(i * ROWS, ROWS)
        acc = conv_rows(three, kernel, row, False)
        centred[pl.ds(row * width, ROWS * width), :] = acc
        return s + fold(acc)

    s = lax.fori_loop(0, height // ROWS, conv, zero)
    mean_two = group_sum(total(s) / (height * width) + offset) / (channels // GROUPS)
    move = offset - mean_two

    def centre(i, v):
        at = pl.ds(i * 256, 256)
        d = centred[at, :] + move
        centred[at, :] = d
        return v + fold(d * d)

    v = lax.fori_loop(0, height * width // 256, centre, zero)
    stats_out[...] = lax.rsqrt(group_sum(total(v)) / count + EPS)


def second_kernel(three, centred, inv, vec, kernel, dh, act, sums, grad):
    height, width, channels = act.shape
    scale, shift = inv[...] * vec[3:4, :], vec[4:5, :]
    zero = jnp.zeros((8, channels), F32)

    def conv(i, carry):
        s, sc = carry
        row = pl.multiple_of(i * ROWS, ROWS)
        at = pl.ds(row * width, ROWS * width)
        acc = conv_rows(three, kernel, row, True)
        c = centred[at, :]
        h = c * scale + shift
        sig = sigmoid(h)
        a = h * sig
        act[pl.ds(row, ROWS)] = a.astype(BF16).reshape(ROWS, width, channels)
        d = acc * (sig + a * (1.0 - sig))
        dh[at, :] = d
        return s + fold(d), sc + fold(d * c)

    s, sc = lax.fori_loop(0, height // ROWS, conv, (zero, zero))
    sums[0:1, :] = total(sc) * inv[...]
    sums[1:2, :] = total(s)
    kernel_grad(act, three, grad)


def middle_kernel(dh_two, centred, inv_two, sums_two, x, stats, vec, kernel, three, dc_sum, dq, dh, sums):
    height, width, channels = x.shape
    count = height * width * (channels // GROUPS)
    gain = vec[3:4, :]
    inv = inv_two[...]
    scale = inv * gain
    base = inv * (group_sum(sums_two[1:2, :] * gain) / count)
    slope = inv * inv * (group_sum(sums_two[0:1, :] * gain) / count)
    zero = jnp.zeros((8, channels), F32)
    clear_edges(three)

    def back(i, s):
        row = i * 4
        at = pl.ds(row * width, 4 * width)
        d = dh_two[at, :] * scale - base - centred[at, :] * slope
        rows = d.reshape(4, width, channels)
        for j in range(4):
            store_three(three, row + j, rows[j])
        return s + fold(d)

    dc = total(lax.fori_loop(0, height // 4, back, zero))
    dc_sum[...] = dc
    dq[...] = lax.dot_general(
        dc,
        kernel[9 * channels :, :].astype(F32),
        (((1,), (1,)), ((), ())),
        precision=lax.Precision.HIGHEST,
        preferred_element_type=F32,
    )
    mean, scale, shift = stats[0:1, :], stats[1:2, :] * vec[0:1, :], vec[1:2, :]

    def conv(i, carry):
        s, sn = carry
        row = pl.multiple_of(i * ROWS, ROWS)
        acc = conv_rows(three, kernel, row, True)
        c = x[pl.ds(row, ROWS)].astype(F32).reshape(ROWS * width, channels) - mean
        h = c * scale + shift
        sig = sigmoid(h)
        d = acc * (sig + h * sig * (1.0 - sig))
        dh[pl.ds(row * width, ROWS * width), :] = d
        return s + fold(d), sn + fold(d * c)

    s, sn = lax.fori_loop(0, height // ROWS, conv, (zero, zero))
    sums[0:1, :] = total(sn) * stats[1:2, :]
    sums[1:2, :] = total(s)


def input_kernel(dh, x, g, stats, sums, vec, result, done):
    height, width, channels = x.shape
    count = height * width * (channels // GROUPS)
    mean, inv, gain = stats[0:1, :], stats[1:2, :], vec[0:1, :]
    scale = inv * gain
    base = inv * (group_sum(sums[1:2, :] * gain) / count)
    slope = inv * inv * (group_sum(sums[0:1, :] * gain) / count)

    def back(i, _):
        row = i * 4
        d = dh[pl.ds(row * width, 4 * width), :].reshape(4, width, channels)
        c = x[pl.ds(row, 4)].astype(F32) - mean
        result[pl.ds(row, 4)] = g[pl.ds(row, 4)].astype(F32) + (d * scale - base - c * slope)
        return 0

    lax.fori_loop(0, height // 4, back, 0)
    done[...] = base


def last_kernel(act, x, vec, kernel, result, done, three):
    height, width, channels = x.shape
    bias = vec[5:6, :]
    clear_edges(three)

    def spread(i, _):
        rows = act[pl.ds(i * 4, 4)].astype(F32)
        for j in range(4):
            store_three(three, i * 4 + j, rows[j])
        return 0

    lax.fori_loop(0, height // 4, spread, 0)

    def conv(i, _):
        row = pl.multiple_of(i * ROWS, ROWS)
        acc = conv_rows(three, kernel, row, False).reshape(ROWS, width, channels)
        result[pl.ds(row, ROWS)] = (x[pl.ds(row, ROWS)].astype(F32) + acc + bias).astype(BF16)
        return 0

    lax.fori_loop(0, height // ROWS, conv, 0)
    done[...] = bias


def join_kernel(mine, got, out):
    rows = mine.shape[0] - VEC_ROWS
    out[0:rows, :] = mine[0:rows, :]
    out[rows : 2 * rows, :] = got[0:rows, :]
    out[2 * rows : 2 * rows + VEC_ROWS, :] = mine[rows : rows + VEC_ROWS, :] + got[rows : rows + VEC_ROWS, :]


def halve_kernel(keep, got, send_next, keep_next):
    rows = (keep.shape[0] - VEC_ROWS) // 2
    keep_next[0:rows, :] = keep[0:rows, :] + got[0:rows, :].astype(F32)
    send_next[0:rows, :] = (keep[rows : 2 * rows, :] + got[rows : 2 * rows, :].astype(F32)).astype(BF16)
    vec = keep[2 * rows : 2 * rows + VEC_ROWS, :] + got[2 * rows : 2 * rows + VEC_ROWS, :].astype(F32)
    keep_next[rows : rows + VEC_ROWS, :] = vec
    send_next[rows : rows + VEC_ROWS, :] = vec.astype(BF16)


def arrange_kernel(wires, cuts, mine, got, first, kernel_two, vec, flat_one, flat_two, flat_project, flat_vec):
    me = wires.me()
    block = sum(cuts)
    flats = (flat_one, flat_two, flat_project)
    for slot in range(wires.slots):
        for other, source in ((False, mine), (True, got)):
            owner = wires.owner(slot, other, me)
            values = source[slot * block : (slot + 1) * block, :].astype(F32)
            at = 0
            for flat, rows in zip(flats, cuts):
                flat[pl.ds(pl.multiple_of(owner * rows, rows), rows), :] = values[at : at + rows]
                at += rows
    rows_one = flat_one.shape[0] // 2
    for flat, out, base in ((flat_one, first, 0), (flat_two, kernel_two, 0), (flat_project, first, rows_one)):
        for start in range(0, flat.shape[0] // 2, 256):
            out[base + start : base + start + 256, :] = load_flat(flat, 2 * start, 256).astype(BF16)
    at = wires.slots * block
    flat_vec[...] = mine[at : at + VEC_ROWS, :].astype(F32) + got[at : at + VEC_ROWS, :].astype(F32)
    vec[...] = load_flat(flat_vec, 0, VEC_ROWS // 2)


def pack_kernel(wires, cuts, act, three, flat_two, q, dc_sum, sums_one, sums_two, g_sum, send, keep, flat_one, flat_project):
    me = wires.me()
    block = sum(cuts)
    kernel_grad(act, three, flat_one)
    for start in range(0, q.shape[0], 256):
        store_flat(flat_project, 2 * start, q[start : start + 256, :] * dc_sum[...])
    for slot in range(wires.slots):
        for other in (True, False):
            owner = wires.owner(slot, other, me)
            at = slot * block
            for flat, rows in zip((flat_one, flat_two, flat_project), cuts):
                values = flat[pl.ds(pl.multiple_of(owner * rows, rows), rows), :]
                if other:
                    send[at : at + rows, :] = values.astype(BF16)
                else:
                    keep[at : at + rows, :] = values
                at += rows
    at = wires.slots * block
    vectors = [sums_one[0:1, :], sums_one[1:2, :], dc_sum[...], sums_two[0:1, :], sums_two[1:2, :], g_sum[...]]
    halves = [row[:, i * LANES : (i + 1) * LANES] for row in vectors for i in range(2)]
    values = jnp.concatenate(halves + [jnp.zeros((VEC_ROWS - len(halves), LANES), F32)], axis=0)
    keep[at : at + VEC_ROWS, :] = values
    send[at : at + VEC_ROWS, :] = values.astype(BF16)


def finish_kernel(wires, cuts, n_vec, keep, got, one, two, project, vec):
    at = 0
    for out, rows in zip((one, two, project), cuts):
        out[...] = keep[at : at + rows, :] + got[at : at + rows, :].astype(F32)
        at += rows
    vectors = keep[at : at + VEC_ROWS, :] + got[at : at + VEC_ROWS, :].astype(F32)
    start = wires.me() * n_vec
    row, lane = start // LANES, start % LANES
    place = lax.broadcasted_iota(jnp.int32, vectors.shape, 0)
    own = jnp.sum(jnp.where(place == row, vectors, 0.0), 0, keepdims=True)
    following = jnp.sum(jnp.where(place == row + 1, vectors, 0.0), 0, keepdims=True)
    column = lax.broadcasted_iota(jnp.int32, own.shape, 1)
    shifted = pltpu.roll(jnp.where(column >= lane, own, following), (LANES - lane) % LANES, 1)
    vec[...] = shifted[:, :n_vec]


def call(body, outs, *args, scratch=(), flops=0, size=4 << 20, after=()):
    held, n_in = len(after), len(args)

    def run(*refs):
        body(*refs[:n_in], *refs[n_in + held :])

    return pl.pallas_call(
        run,
        out_shape=[jax.ShapeDtypeStruct(shape, dtype) for shape, dtype in outs],
        in_specs=[pl.BlockSpec(memory_space=pltpu.VMEM)] * n_in + [pl.BlockSpec(memory_space=pl.ANY)] * held,
        scratch_shapes=[pltpu.VMEM(shape, dtype) for shape, dtype in scratch],
        compiler_params=pltpu.CompilerParams(vmem_limit_bytes=VMEM_BYTES),
        cost_estimate=pl.CostEstimate(flops=flops, bytes_accessed=size, transcendentals=0),
    )(*args, *after)


def gather(wires, cuts, parts, vectors, beside):
    block = sum(cuts)
    n_vec = vectors.shape[0]
    me = wires.me()
    wide = VEC_ROWS * LANES
    placed = lax.dynamic_slice(jnp.pad(vectors, (wide, wide - n_vec)), (wide - me * n_vec,), (wide,))
    held = jnp.concatenate([v.reshape(-1, LANES) for v in (*parts, placed)], axis=0)
    for stage in range(wires.stages):
        got = wires.swap(held, stage)
        shape = (2 * (held.shape[0] - VEC_ROWS) + VEC_ROWS, LANES)
        after = beside.get(stage, ())
        held, = call(join_kernel, [(shape, BF16)], held, got, size=4 * LANES * shape[0], after=after)
    got = wires.swap(held, wires.stages)
    channels = 2 * LANES
    totals = [wires.n * rows for rows in cuts]
    outs = [((rows // 2, channels), BF16) for rows in (totals[0] + totals[2], totals[1])]
    if all(rows % 8 == 0 for rows in cuts):
        return call(
            functools.partial(arrange_kernel, wires, cuts),
            [*outs, ((VEC_ROWS // 2, channels), F32)],
            held,
            got,
            scratch=[((rows, LANES), F32) for rows in (*totals, VEC_ROWS)],
        )
    rows = wires.slots * block
    both = jnp.concatenate([held[:rows], got[:rows]]).reshape(wires.n, block, LANES)
    owners = jnp.stack([wires.owner(j, other, me) for other in (False, True) for j in range(wires.slots)])
    both = jnp.zeros_like(both).at[owners].set(both)
    at, whole = 0, []
    for cut in cuts:
        whole.append(both[:, at : at + cut].reshape(-1, channels))
        at += cut
    vec = (held[rows:].astype(F32) + got[rows:].astype(F32)).reshape(VEC_ROWS // 2, channels)
    return jnp.concatenate([whole[0], whole[2]]), whole[1], vec


def pack(wires, cuts, act, three, flat_two, q, dc_sum, sums_one, sums_two, g_sum):
    block = sum(cuts)
    shape = (wires.slots * block + VEC_ROWS, LANES)
    totals = [wires.n * rows for rows in cuts]
    if all(rows % 8 == 0 for rows in cuts):
        return call(
            functools.partial(pack_kernel, wires, cuts),
            [(shape, BF16), (shape, F32)],
            act,
            three,
            flat_two,
            q,
            dc_sum,
            sums_one,
            sums_two,
            g_sum,
            scratch=[((totals[0], LANES), F32), ((totals[2], LANES), F32)],
            flops=2 * 9 * act.size * act.shape[-1],
        )
    flat_one, = call(kernel_grad, [((totals[0], LANES), F32)], act, three, flops=2 * 9 * act.size * act.shape[-1])
    flats = (flat_one, flat_two, (q * dc_sum).reshape(-1, LANES))
    blocks = jnp.concatenate([f.reshape(wires.n, rows, LANES) for f, rows in zip(flats, cuts)], axis=1)
    me = wires.me()
    vec = jnp.concatenate([sums_one, dc_sum, sums_two, g_sum]).reshape(-1, LANES)
    vec = jnp.pad(vec, ((0, VEC_ROWS - vec.shape[0]), (0, 0)))
    halves = []
    for other in (True, False):
        owners = jnp.stack([wires.owner(j, other, me) for j in range(wires.slots)])
        halves.append(jnp.concatenate([blocks[owners].reshape(-1, LANES), vec]))
    return halves[0].astype(BF16), halves[1]


def reduce_scatter(wires, cuts, n_vec, send, keep, beside):
    for stage in range(wires.stages, 0, -1):
        got = wires.swap(send, stage)
        shape = ((keep.shape[0] - VEC_ROWS) // 2 + VEC_ROWS, LANES)
        send, keep = call(halve_kernel, [(shape, BF16), (shape, F32)], keep, got, size=12 * LANES * shape[0], after=beside.get(stage, ()))
    got = wires.swap(send, 0)
    return call(
        functools.partial(finish_kernel, wires, cuts, n_vec),
        [*[((rows, LANES), F32) for rows in cuts], ((1, n_vec), F32)],
        keep,
        got,
        size=12 * LANES * keep.shape[0],
    )


def swish_slope(values):
    sigma = jax.nn.sigmoid(values)
    return sigma * (1.0 + values * (1.0 - sigma))


def local(sizes, images, embedding, conv_first, conv_second, projection, vectors, cotangent):
    count, height, width, channels = images.shape
    emb_width = embedding.shape[-1]
    wires = Wires(*sizes)
    n_vec = vectors.shape[0]
    assert count == 1 and channels == 2 * LANES and n_vec <= LANES
    cuts = [v.shape[0] // LANES for v in (conv_first, conv_second, projection)]
    pixels = height * width
    three = ((3, height + 2, width, channels), BF16)
    maps = ((height, width, channels), BF16)
    flat = ((pixels, channels), F32)
    line = ((1, channels), F32)
    pair = ((2, channels), F32)
    taps = ((18 * channels, LANES), F32)
    conv_flops = 2 * 9 * pixels * channels * channels

    x, g = images[0], cotangent[0]
    stats, g_three, g_sum = call(prepare_kernel, [pair, three, line], x, g)
    first, kernel_two, vec = gather(
        wires, cuts, (conv_first, conv_second, projection), vectors, {wires.stages - 1: (g_sum,)}
    )

    emb_float = embedding.astype(F32)
    emb_act = jax.nn.silu(emb_float).astype(BF16)
    q = emb_act.astype(F32).reshape(emb_width, 1)
    act_one, centred, inv_two = call(
        first_kernel, [maps, flat, line], x, stats, vec, emb_act, first, scratch=[three], flops=conv_flops
    )
    dh_two, act_two, sums_two, grad_two = call(
        second_kernel,
        [flat, maps, pair, taps],
        g_three,
        centred,
        inv_two,
        vec,
        kernel_two,
        flops=2 * conv_flops,
    )
    e_three, dc_sum, dq, dh_one, sums_one = call(
        middle_kernel,
        [three, line, ((1, emb_width), F32), flat, pair],
        dh_two,
        centred,
        inv_two,
        sums_two,
        x,
        stats,
        vec,
        first,
        flops=conv_flops,
    )
    send, keep = pack(wires, cuts, act_one, e_three, grad_two, q, dc_sum, sums_one, sums_two, g_sum)
    input_grad, input_done = call(input_kernel, [(maps[0], F32), line], dh_one, x, g, stats, sums_one, vec)
    output, output_done = call(last_kernel, [maps, line], act_two, x, vec, kernel_two, scratch=[three], flops=conv_flops)
    beside = {wires.stages - 1: (output_done,), wires.stages - 2: (input_done,)}
    summed = reduce_scatter(wires, cuts, n_vec, send, keep, beside)
    embedding_grad = dq * swish_slope(emb_float)
    return (output[None], input_grad[None], embedding_grad, *[v.reshape(-1) for v in summed])


def solution(mesh):
    sizes = (mesh.shape["dp"], mesh.shape["fsdp"])
    split = P(AXES)
    maps = P(AXES, None, None, None)
    in_specs = (maps, P(AXES, None), split, split, split, split, maps)
    out_specs = (maps, maps, P(AXES, None), split, split, split, split)

    def body(*args):
        return local(sizes, *args)

    return jax.shard_map(body, mesh=mesh, in_specs=in_specs, out_specs=out_specs, check_vma=False)
```

```python
import functools
import math

import jax
import jax.numpy as jnp
from jax import lax
from jax.experimental import pallas as pl
from jax.experimental.pallas import tpu as pltpu
from jax.sharding import PartitionSpec as P

GROUPS = 32
EPS = 1e-05
AXES = ("dp", "fsdp")
LANES = 128
VEC_ROWS = 16


class Wires:
    def __init__(self, n_dp, n_fsdp):
        self.n_fsdp = n_fsdp
        self.n = n_dp * n_fsdp
        self.bits = int(math.log2(self.n))
        fsdp_bits = int(math.log2(n_fsdp))
        assert 1 << self.bits == self.n and 1 << fsdp_bits == n_fsdp and fsdp_bits >= 2 and n_dp >= 2
        a, b = 1, fsdp_bits
        far = [bit for bit in range(self.bits - 1, 0, -1) if bit not in (a, b)]
        self.order = {0: [*far, a, b], 1: [*far, b, a]}
        self.stages = self.bits - 1
        self.slots = 1 << self.stages

    def swap(self, value, stage):
        bit = (lambda i: 0) if stage == self.stages else (lambda i: self.order[i & 1][stage])
        return lax.ppermute(value, AXES, [(i, i ^ (1 << bit(i))) for i in range(self.n)])

    def mask(self, slot, core):
        return sum(1 << self.order[core][i] for i in range(self.stages) if slot >> i & 1)

    def me(self):
        return lax.axis_index("dp") * self.n_fsdp + lax.axis_index("fsdp")

    def owner(self, slot, other, me):
        core = me & 1
        if other:
            me, core = me ^ 1, 1 - core
        return me ^ jnp.where(core == 0, self.mask(slot, 0), self.mask(slot, 1))


ROWS = 4
UNITS = 2
PIECE = 64
F32 = jnp.float32
BF16 = jnp.bfloat16
VMEM_BYTES = 14 * 1024 * 1024


def group_sum(totals):
    channels = totals.shape[1]
    lane = lax.broadcasted_iota(jnp.int32, totals.shape, 1)
    span = 1
    while span < channels // GROUPS:
        up = pltpu.roll(totals, channels - span, 1)
        down = pltpu.roll(totals, span, 1)
        totals = totals + jnp.where((lane & span) == 0, up, down)
        span *= 2
    return totals


def fold(values):
    channels = values.shape[-1]
    return jnp.sum(values.reshape(-1, 8, channels), 0)


def total(partial):
    return jnp.sum(partial, 0, keepdims=True)


def sigmoid(v):
    return 0.5 * jnp.tanh(0.5 * v) + 0.5


def clear_edges(three):
    height = three.shape[1] - 2
    zero = jnp.zeros((3, 1) + three.shape[2:], three.dtype)
    three[:, 0:1] = zero
    three[:, height + 1 : height + 2] = zero


def store_three(three, row, value):
    width = value.shape[0]
    column = lax.broadcasted_iota(jnp.int32, value.shape, 0)
    left = jnp.where(column == 0, 0.0, pltpu.roll(value, 1, 0))
    right = jnp.where(column == width - 1, 0.0, pltpu.roll(value, width - 1, 0))
    three[0, row + 1] = left.astype(three.dtype)
    three[1, row + 1] = value.astype(three.dtype)
    three[2, row + 1] = right.astype(three.dtype)


def accumulators(body, *refs):
    groups = 4

    def run(*accs):
        accs = iter(accs)
        body(*refs, [[[next(accs) for _ in range(ROWS)] for _ in range(groups)] for _ in range(UNITS)])

    pl.run_scoped(run, *[pltpu.ACC(unit)((PIECE, 2 * LANES), F32) for unit in range(UNITS) for _ in range(groups * ROWS)])


def interleave(pieces, slots):
    return [pieces * (i + 1) // slots - pieces * i // slots for i in range(slots)]


def times(value, size):
    return value * size if isinstance(value, int) else pl.multiple_of(value * size, size)


def conv_step(accs, three, kernel, step, parity, back, others=()):
    others = list(others)
    for tap, share in enumerate(interleave(len(others), 9)):
        at = (8 - tap if back else tap) * three.shape[3]
        stage = (parity + tap) % 2
        for unit in range(UNITS):
            pltpu.matmul_push_rhs(kernel[at : at + three.shape[3], :], stage, unit, transpose=back)
        for piece in range(ROWS):
            for unit in range(UNITS):
                row = (UNITS * step + unit) * ROWS + piece + tap // 3
                pltpu.matmul_acc_lhs(
                    accs[unit][parity][piece], three[tap % 3, row], load_staged_rhs=stage if piece == 0 else None
                )
        for _ in range(share):
            others.pop(0)()


def conv_rows(accs, step, parity, use):
    def one(unit, piece):
        use((UNITS * step + unit) * ROWS + piece, pltpu.matmul_pop(accs[unit][parity][piece]))

    return [functools.partial(one, unit, piece) for unit in range(UNITS) for piece in range(ROWS)]


def conv_all(accs, three, kernel, back, use):
    steps = (three.shape[1] - 2) // (UNITS * ROWS)
    for step in range(steps):
        others = conv_rows(accs, step - 1, (step - 1) % 2, use) if step else ()
        conv_step(accs, three, kernel, step, step % 2, back, others)
    for other in conv_rows(accs, steps - 1, (steps - 1) % 2, use):
        other()


class Sums:
    def __init__(self, channels, count):
        self.values = [jnp.zeros((8, channels), F32)] * count

    def add(self, *values):
        self.values = [s + fold(v) for s, v in zip(self.values, values)]

    def totals(self):
        return [total(s) for s in self.values]


def store_turned(turned, padded, row):
    width, channels = padded.shape[1:]
    size = ROWS * width
    lanes = pl.ds(times(row // ROWS, size), size)
    turned[0, :, lanes] = padded[pl.ds(row + 1, ROWS)].reshape(size, channels).T
    turned[1, :, lanes] = padded[pl.ds(row, ROWS)].reshape(size, channels).T


def turn_end(turned, padded):
    height = padded.shape[0] - 2
    width, channels = padded.shape[1:]
    at = height * width
    turned[1, :, at : at + 2 * width] = padded[height : height + 2].reshape(2 * width, channels).T


def grad_step(accs, turned, three, work, stage, others=()):
    others = list(others)
    width, channels = three.shape[2:]
    size = ROWS * width
    for unit, column, chunk, _ in work:
        rhs = three[column, pl.ds(1 + times(chunk, ROWS), ROWS)].reshape(size, channels)
        pltpu.matmul_push_rhs(rhs, stage, unit)
    shares = iter(interleave(len(others), 3 * ROWS))
    for row in range(3):
        for piece in range(ROWS):
            for unit, _, chunk, groups in work:
                source, at = (0, times(chunk, size)) if row == 1 else (1, times(chunk, size) + row * width)
                lhs = turned[source, piece * PIECE : (piece + 1) * PIECE, pl.ds(at, size)]
                first = row == 0 and piece == 0
                pltpu.matmul_acc_lhs(accs[unit][groups[row]][piece], lhs, load_staged_rhs=stage if first else None)
            for _ in range(next(shares)):
                others.pop(0)()


def kernel_grad(accs, turned, three, flat, beside, carry):
    height, channels = three.shape[1] - 2, three.shape[3]
    chunks = height // ROWS

    def outer(i, carry):
        kept = [carry]

        def other(row):
            kept[0] = beside(row, kept[0])

        for k in range(4):
            chunk = 4 * i + k
            work = [(0, 0, chunk, (0, 1, 2)), (1, 2, chunk, (0, 1, 2))]
            others = [functools.partial(other, ROWS * chunk + j) for j in range(ROWS)] if beside else ()
            grad_step(accs, turned, three, work, k % 2, others)
        return kept[0]

    if beside:
        carry = lax.fori_loop(0, chunks // 4, outer, carry)
    else:
        for i in range(chunks // 4):
            outer(i, carry)

    def store(tap, piece, value):
        store_flat(flat, (tap * channels + piece * PIECE) * 2, value)

    def side(unit, column, row, piece):
        store(3 * row + 2 - column, piece, pltpu.matmul_pop(accs[unit][row][piece]))

    for row in range(2):
        for unit, column in ((0, 0), (1, 2)):
            for piece in range(ROWS):
                side(unit, column, row, piece)
    half = chunks // UNITS
    for chunk in range(half):
        work = [(unit, 1, unit * half + chunk, (3, 0, 1)) for unit in range(UNITS)]
        others = [functools.partial(side, unit, 2 * unit, 2, piece) for unit in range(UNITS) for piece in range(ROWS)]
        grad_step(accs, turned, three, work, chunk % 2, others if chunk == 0 else ())
    for row, group in enumerate((3, 0, 1)):
        for piece in range(ROWS):
            store(3 * row + 1, piece, pltpu.matmul_pop(accs[0][group][piece]) + pltpu.matmul_pop(accs[1][group][piece]))
    return carry


def store_flat(flat, start, value):
    rows = value.shape[0]
    flat[pl.ds(start, rows, stride=2), :] = value[:, :LANES]
    flat[pl.ds(start + 1, rows, stride=2), :] = value[:, LANES:]


def load_flat(flat, start, rows):
    left = flat[pl.ds(start, rows, stride=2), :]
    right = flat[pl.ds(start + 1, rows, stride=2), :]
    return jnp.concatenate([left, right], axis=1)


def prepare_kernel(x, g, stats, three, g_sum):
    height, width, channels = x.shape
    count = height * width * (channels // GROUPS)
    zero = jnp.zeros((8, channels), F32)
    clear_edges(three)

    def first(i, carry):
        s, gs = carry
        row = i * 4
        s = s + fold(x[pl.ds(row, 4)].astype(F32))
        rows = g[pl.ds(row, 4)].astype(F32)
        for j in range(4):
            store_three(three, row + j, rows[j])
        return s, gs + fold(rows)

    s, gs = lax.fori_loop(0, height // 4, first, (zero, zero))
    g_sum[...] = total(gs)
    mean = group_sum(total(s)) / count

    def second(i, v):
        d = x[pl.ds(i * 4, 4)].astype(F32) - mean
        return v + fold(d * d)

    v = lax.fori_loop(0, height // 4, second, zero)
    inv = lax.rsqrt(group_sum(total(v)) / count + EPS)
    stats[0:1, :] = mean
    stats[1:2, :] = inv


def first_kernel(x, stats, vec, time, kernel, turned, raw, stats_out, three):
    accumulators(first_body, x, stats, vec, time, kernel, turned, raw, stats_out, three)


def first_body(x, stats, vec, time, kernel, turned, raw, stats_out, three, accs):
    height, width, channels = x.shape
    pixels = height * width
    per_group = channels // GROUPS
    mean, scale, shift = stats[0:1, :], stats[1:2, :] * vec[0:1, :], vec[1:2, :]
    offset = vec[2:3, :] + time[...]
    sums = Sums(channels, 2)
    pivot = []
    clear_edges(three)

    def activate(row):
        h = (x[row].astype(F32) - mean) * scale + shift
        store_three(three, row, h * sigmoid(h))
        if row % ROWS == ROWS - 1:
            store_turned(turned, three.at[1], row + 1 - ROWS)

    def use(row, v):
        if row == 0:
            pivot.append(total(fold(v)) / width)
        raw[row * width : (row + 1) * width, :] = v
        d = v - pivot[0]
        sums.add(d, d * d)

    per_step = UNITS * ROWS
    steps = height // per_step
    for row in range(per_step + 1):
        activate(row)
    for step in range(steps):
        ahead = range((step + 1) * per_step + 1, min((step + 2) * per_step + 1, height))
        others = [functools.partial(activate, row) for row in ahead]
        done = conv_rows(accs, step - 1, (step - 1) % 2, use) if step else []
        mixed = [f for i in range(per_step) for f in (*others[i : i + 1], *done[i : i + 1])]
        conv_step(accs, three, kernel, step, step % 2, False, mixed)
    turn_end(turned, three.at[1])
    for other in conv_rows(accs, steps - 1, (steps - 1) % 2, use):
        other()
    part, square = [v / pixels for v in sums.totals()]
    spread = square - part * part
    middle = pivot[0] + part + offset
    mean_two = group_sum(middle) / per_group
    away = middle - mean_two
    stats_out[0:1, :] = offset - mean_two
    stats_out[1:2, :] = lax.rsqrt(group_sum(spread + away * away) / per_group + EPS)


def second_kernel(g_three, raw, stats, vec, kernel, act, sums, flat, three, dc_sum, dh, turned):
    accumulators(second_body, g_three, raw, stats, vec, kernel, act, sums, flat, three, dc_sum, dh, turned)


def second_body(g_three, raw, stats, vec, kernel, act, sums, flat, three, dc_sum, dh, turned, accs):
    height, width, channels = act.shape[0] - 2, act.shape[1], act.shape[2]
    count = height * width * (channels // GROUPS)
    move, inv, gain, shift = stats[0:1, :], stats[1:2, :], vec[3:4, :], vec[4:5, :]
    scale = inv * gain
    both = Sums(channels, 2)
    act[0:1] = jnp.zeros((1, width, channels), BF16)
    act[height + 1 : height + 2] = jnp.zeros((1, width, channels), BF16)
    clear_edges(three)

    def use(row, v):
        at = slice(row * width, (row + 1) * width)
        c = raw[at, :] + move
        h = c * scale + shift
        sig = sigmoid(h)
        a = h * sig
        act[row + 1] = a.astype(BF16)
        d = v * (sig + a * (1.0 - sig))
        dh[at, :] = d
        both.add(d, d * c)
        if row % ROWS == ROWS - 1:
            store_turned(turned, act, row + 1 - ROWS)

    conv_all(accs, g_three, kernel, True, use)
    turn_end(turned, act)
    s, sc = both.totals()
    sn = sc * inv
    sums[0:1, :] = sn
    sums[1:2, :] = s
    base = inv * (group_sum(s * gain) / count)
    slope = inv * inv * (group_sum(sn * gain) / count)

    def back(row, dc):
        at = pl.ds(times(row, width), width)
        d = dh[at, :] * scale - base - (raw[at, :] + move) * slope
        store_three(three, row, d)
        return dc + fold(d)

    dc_sum[...] = total(kernel_grad(accs, turned, g_three, flat, back, jnp.zeros((8, channels), F32)))


def third_kernel(three, x, stats, vec, kernel, dh, sums):
    accumulators(third_body, three, x, stats, vec, kernel, dh, sums)


def third_body(three, x, stats, vec, kernel, dh, sums, accs):
    height, width, channels = x.shape
    mean, scale, shift = stats[0:1, :], stats[1:2, :] * vec[0:1, :], vec[1:2, :]
    both = Sums(channels, 2)

    def use(row, v):
        c = x[row].astype(F32) - mean
        h = c * scale + shift
        sig = sigmoid(h)
        d = v * (sig + h * sig * (1.0 - sig))
        dh[row * width : (row + 1) * width, :] = d
        both.add(d, d * c)

    conv_all(accs, three, kernel, True, use)
    s, sn = both.totals()
    sums[0:1, :] = sn * stats[1:2, :]
    sums[1:2, :] = s


def input_kernel(dh, x, g, stats, sums, vec, dc_sum, kernel, result, dq, done):
    height, width, channels = x.shape
    count = height * width * (channels // GROUPS)
    mean, inv, gain = stats[0:1, :], stats[1:2, :], vec[0:1, :]
    scale = inv * gain
    base = inv * (group_sum(sums[1:2, :] * gain) / count)
    slope = inv * inv * (group_sum(sums[0:1, :] * gain) / count)

    def back(i, _):
        row = i * 4
        d = dh[pl.ds(row * width, 4 * width), :].reshape(4, width, channels)
        c = x[pl.ds(row, 4)].astype(F32) - mean
        result[pl.ds(row, 4)] = g[pl.ds(row, 4)].astype(F32) + (d * scale - base - c * slope)
        return 0

    lax.fori_loop(0, height // 4, back, 0)
    dq[...] = lax.dot_general(
        dc_sum[...],
        kernel[9 * channels :, :].astype(F32),
        (((1,), (1,)), ((), ())),
        precision=lax.Precision.HIGHEST,
        preferred_element_type=F32,
    )
    done[...] = base


def last_kernel(act, x, vec, kernel, result, done, three):
    accumulators(last_body, act, x, vec, kernel, result, done, three)


def last_body(act, x, vec, kernel, result, done, three, accs):
    height = x.shape[0]
    bias = vec[5:6, :]
    clear_edges(three)

    def spread(row):
        store_three(three, row, act[row + 1].astype(F32))

    def use(row, v):
        result[row] = (x[row].astype(F32) + v + bias).astype(BF16)

    per_step = UNITS * ROWS
    steps = height // per_step
    for row in range(per_step + 1):
        spread(row)
    for step in range(steps):
        ahead = range((step + 1) * per_step + 1, min((step + 2) * per_step + 1, height))
        others = [functools.partial(spread, row) for row in ahead]
        done_rows = conv_rows(accs, step - 1, (step - 1) % 2, use) if step else []
        mixed = [f for i in range(per_step) for f in (*others[i : i + 1], *done_rows[i : i + 1])]
        conv_step(accs, three, kernel, step, step % 2, False, mixed)
    for other in conv_rows(accs, steps - 1, (steps - 1) % 2, use):
        other()
    done[...] = bias


def join_kernel(mine, got, out):
    rows = mine.shape[0] - VEC_ROWS
    out[0:rows, :] = mine[0:rows, :]
    out[rows : 2 * rows, :] = got[0:rows, :]
    out[2 * rows : 2 * rows + VEC_ROWS, :] = mine[rows : rows + VEC_ROWS, :] + got[rows : rows + VEC_ROWS, :]


def halve_kernel(keep, got, send_next, keep_next):
    rows = (keep.shape[0] - VEC_ROWS) // 2
    keep_next[0:rows, :] = keep[0:rows, :] + got[0:rows, :].astype(F32)
    send_next[0:rows, :] = (keep[rows : 2 * rows, :] + got[rows : 2 * rows, :].astype(F32)).astype(BF16)
    vec = keep[2 * rows : 2 * rows + VEC_ROWS, :] + got[2 * rows : 2 * rows + VEC_ROWS, :].astype(F32)
    keep_next[rows : rows + VEC_ROWS, :] = vec
    send_next[rows : rows + VEC_ROWS, :] = vec.astype(BF16)


def arrange_kernel(wires, cuts, mine, got, q, first, kernel_two, vec, time, flat_one, flat_two, flat_project, flat_vec):
    me = wires.me()
    block = sum(cuts)
    flats = (flat_one, flat_two, flat_project)
    for slot in range(wires.slots):
        for other, source in ((False, mine), (True, got)):
            owner = wires.owner(slot, other, me)
            values = source[slot * block : (slot + 1) * block, :].astype(F32)
            at = 0
            for flat, rows in zip(flats, cuts):
                flat[pl.ds(pl.multiple_of(owner * rows, rows), rows), :] = values[at : at + rows]
                at += rows
    rows_one = flat_one.shape[0] // 2
    for flat, out, base in ((flat_one, first, 0), (flat_two, kernel_two, 0), (flat_project, first, rows_one)):
        for start in range(0, flat.shape[0] // 2, 256):
            out[base + start : base + start + 256, :] = load_flat(flat, 2 * start, 256).astype(BF16)
    at = wires.slots * block
    flat_vec[...] = mine[at : at + VEC_ROWS, :].astype(F32) + got[at : at + VEC_ROWS, :].astype(F32)
    vec[...] = load_flat(flat_vec, 0, VEC_ROWS // 2)
    time[...] = jnp.dot(q[...], first[rows_one:, :], preferred_element_type=F32)


def grad_kernel(turned, three, flat):
    accumulators(lambda *refs: kernel_grad(refs[-1], *refs[:-1], None, 0), turned, three, flat)


def pack_kernel(wires, cuts, turned, three, flat_two, q, dc_sum, sums_one, sums_two, g_sum, send, keep, flat_one, flat_project):
    me = wires.me()
    block = sum(cuts)
    grad_kernel(turned, three, flat_one)
    for start in range(0, q.shape[0], 256):
        store_flat(flat_project, 2 * start, q[start : start + 256, :] * dc_sum[...])
    for slot in range(wires.slots):
        for other in (True, False):
            owner = wires.owner(slot, other, me)
            at = slot * block
            for flat, rows in zip((flat_one, flat_two, flat_project), cuts):
                values = flat[pl.ds(pl.multiple_of(owner * rows, rows), rows), :]
                if other:
                    send[at : at + rows, :] = values.astype(BF16)
                else:
                    keep[at : at + rows, :] = values
                at += rows
    at = wires.slots * block
    vectors = [sums_one[0:1, :], sums_one[1:2, :], dc_sum[...], sums_two[0:1, :], sums_two[1:2, :], g_sum[...]]
    halves = [row[:, i * LANES : (i + 1) * LANES] for row in vectors for i in range(2)]
    values = jnp.concatenate(halves + [jnp.zeros((VEC_ROWS - len(halves), LANES), F32)], axis=0)
    keep[at : at + VEC_ROWS, :] = values
    send[at : at + VEC_ROWS, :] = values.astype(BF16)


def finish_kernel(wires, cuts, n_vec, keep, got, one, two, project, vec):
    at = 0
    for out, rows in zip((one, two, project), cuts):
        out[...] = keep[at : at + rows, :] + got[at : at + rows, :].astype(F32)
        at += rows
    vectors = keep[at : at + VEC_ROWS, :] + got[at : at + VEC_ROWS, :].astype(F32)
    start = wires.me() * n_vec
    row, lane = start // LANES, start % LANES
    place = lax.broadcasted_iota(jnp.int32, vectors.shape, 0)
    own = jnp.sum(jnp.where(place == row, vectors, 0.0), 0, keepdims=True)
    following = jnp.sum(jnp.where(place == row + 1, vectors, 0.0), 0, keepdims=True)
    column = lax.broadcasted_iota(jnp.int32, own.shape, 1)
    shifted = pltpu.roll(jnp.where(column >= lane, own, following), (LANES - lane) % LANES, 1)
    vec[...] = shifted[:, :n_vec]


def call(body, outs, *args, scratch=(), flops=0, size=4 << 20, after=()):
    held, n_in = len(after), len(args)

    def run(*refs):
        body(*refs[:n_in], *refs[n_in + held :])

    return pl.pallas_call(
        run,
        out_shape=[jax.ShapeDtypeStruct(shape, dtype) for shape, dtype in outs],
        in_specs=[pl.BlockSpec(memory_space=pltpu.VMEM)] * n_in + [pl.BlockSpec(memory_space=pl.ANY)] * held,
        out_specs=[pl.BlockSpec(memory_space=pltpu.VMEM)] * len(outs),
        scratch_shapes=[pltpu.VMEM(shape, dtype) for shape, dtype in scratch],
        compiler_params=pltpu.CompilerParams(vmem_limit_bytes=VMEM_BYTES),
        cost_estimate=pl.CostEstimate(flops=flops, bytes_accessed=size, transcendentals=0),
    )(*args, *after)


def gather(wires, cuts, parts, vectors, q, beside):
    block = sum(cuts)
    n_vec = vectors.shape[0]
    me = wires.me()
    wide = VEC_ROWS * LANES
    placed = lax.dynamic_slice(jnp.pad(vectors, (wide, wide - n_vec)), (wide - me * n_vec,), (wide,))
    held = jnp.concatenate([v.reshape(-1, LANES) for v in (*parts, placed)], axis=0)
    for stage in range(wires.stages):
        got = wires.swap(held, stage)
        shape = (2 * (held.shape[0] - VEC_ROWS) + VEC_ROWS, LANES)
        after = beside.get(stage, ())
        held, = call(join_kernel, [(shape, BF16)], held, got, size=4 * LANES * shape[0], after=after)
    got = wires.swap(held, wires.stages)
    channels = 2 * LANES
    totals = [wires.n * rows for rows in cuts]
    outs = [((rows // 2, channels), BF16) for rows in (totals[0] + totals[2], totals[1])]
    if all(rows % 8 == 0 for rows in cuts):
        return call(
            functools.partial(arrange_kernel, wires, cuts),
            [*outs, ((VEC_ROWS // 2, channels), F32), ((1, channels), F32)],
            held,
            got,
            q,
            scratch=[((rows, LANES), F32) for rows in (*totals, VEC_ROWS)],
        )
    rows = wires.slots * block
    both = jnp.concatenate([held[:rows], got[:rows]]).reshape(wires.n, block, LANES)
    owners = jnp.stack([wires.owner(j, other, me) for other in (False, True) for j in range(wires.slots)])
    both = jnp.zeros_like(both).at[owners].set(both)
    at, whole = 0, []
    for cut in cuts:
        whole.append(both[:, at : at + cut].reshape(-1, channels))
        at += cut
    vec = (held[rows:].astype(F32) + got[rows:].astype(F32)).reshape(VEC_ROWS // 2, channels)
    time = jnp.dot(q, whole[2], preferred_element_type=F32)
    return jnp.concatenate([whole[0], whole[2]]), whole[1], vec, time


def pack(wires, cuts, turned, three, flat_two, q, dc_sum, sums_one, sums_two, g_sum):
    block = sum(cuts)
    shape = (wires.slots * block + VEC_ROWS, LANES)
    totals = [wires.n * rows for rows in cuts]
    if all(rows % 8 == 0 for rows in cuts):
        return call(
            functools.partial(pack_kernel, wires, cuts),
            [(shape, BF16), (shape, F32)],
            turned,
            three,
            flat_two,
            q,
            dc_sum,
            sums_one,
            sums_two,
            g_sum,
            scratch=[((totals[0], LANES), F32), ((totals[2], LANES), F32)],
            flops=9 * three.size * three.shape[-1] // 2,
        )
    flat_one, = call(grad_kernel, [((totals[0], LANES), F32)], turned, three)
    flats = (flat_one, flat_two, (q * dc_sum).reshape(-1, LANES))
    blocks = jnp.concatenate([f.reshape(wires.n, rows, LANES) for f, rows in zip(flats, cuts)], axis=1)
    me = wires.me()
    vec = jnp.concatenate([sums_one, dc_sum, sums_two, g_sum]).reshape(-1, LANES)
    vec = jnp.pad(vec, ((0, VEC_ROWS - vec.shape[0]), (0, 0)))
    halves = []
    for other in (True, False):
        owners = jnp.stack([wires.owner(j, other, me) for j in range(wires.slots)])
        halves.append(jnp.concatenate([blocks[owners].reshape(-1, LANES), vec]))
    return halves[0].astype(BF16), halves[1]


def reduce_scatter(wires, cuts, n_vec, send, keep, beside):
    for stage in range(wires.stages, 0, -1):
        got = wires.swap(send, stage)
        shape = ((keep.shape[0] - VEC_ROWS) // 2 + VEC_ROWS, LANES)
        send, keep = call(halve_kernel, [(shape, BF16), (shape, F32)], keep, got, size=12 * LANES * shape[0], after=beside.get(stage, ()))
    got = wires.swap(send, 0)
    return call(
        functools.partial(finish_kernel, wires, cuts, n_vec),
        [*[((rows, LANES), F32) for rows in cuts], ((1, n_vec), F32)],
        keep,
        got,
        size=12 * LANES * keep.shape[0],
    )


def swish_slope(values):
    sigma = jax.nn.sigmoid(values)
    return sigma * (1.0 + values * (1.0 - sigma))


def local(sizes, images, embedding, conv_first, conv_second, projection, vectors, cotangent):
    count, height, width, channels = images.shape
    emb_width = embedding.shape[-1]
    wires = Wires(*sizes)
    n_vec = vectors.shape[0]
    assert count == 1 and channels == 2 * LANES and n_vec <= LANES
    cuts = [v.shape[0] // LANES for v in (conv_first, conv_second, projection)]
    pixels = height * width
    three = ((3, height + 2, width, channels), BF16)
    maps = ((height, width, channels), BF16)
    flat = ((pixels, channels), F32)
    line = ((1, channels), F32)
    pair = ((2, channels), F32)
    taps = ((18 * channels, LANES), F32)
    padded = ((height + 2, width, channels), BF16)
    turned = ((2, channels, pixels + 2 * width), BF16)
    conv_flops = 2 * 9 * pixels * channels * channels

    x, g = images[0], cotangent[0]
    stats, g_three, g_sum = call(prepare_kernel, [pair, three, line], x, g)
    emb_float = embedding.astype(F32)
    emb_act = jax.nn.silu(emb_float).astype(BF16)
    q = emb_act.astype(F32).reshape(emb_width, 1)
    parts = (conv_first, conv_second, projection)
    first, kernel_two, vec, time = gather(wires, cuts, parts, vectors, emb_act, {wires.stages - 1: (g_sum,)})

    turned_one, raw, stats_two = call(
        first_kernel, [turned, flat, pair], x, stats, vec, time, first, scratch=[three], flops=conv_flops
    )
    act_two, sums_two, grad_two, e_three, dc_sum = call(
        second_kernel,
        [padded, pair, taps, three, line],
        g_three,
        raw,
        stats_two,
        vec,
        kernel_two,
        scratch=[flat, turned],
        flops=2 * conv_flops,
    )
    dh_one, sums_one = call(third_kernel, [flat, pair], e_three, x, stats, vec, first, flops=conv_flops)
    send, keep = pack(wires, cuts, turned_one, e_three, grad_two, q, dc_sum, sums_one, sums_two, g_sum)
    input_grad, dq, input_done = call(
        input_kernel, [(maps[0], F32), ((1, emb_width), F32), line], dh_one, x, g, stats, sums_one, vec, dc_sum, first
    )
    output, output_done = call(
        last_kernel, [maps, line], act_two, x, vec, kernel_two, scratch=[three], flops=conv_flops
    )
    beside = {wires.stages - 1: (output_done,), wires.stages - 2: (input_done,)}
    summed = reduce_scatter(wires, cuts, n_vec, send, keep, beside)
    embedding_grad = dq * swish_slope(emb_float)
    return (output[None], input_grad[None], embedding_grad, *[v.reshape(-1) for v in summed])


def solution(mesh):
    sizes = (mesh.shape["dp"], mesh.shape["fsdp"])
    split = P(AXES)
    maps = P(AXES, None, None, None)
    in_specs = (maps, P(AXES, None), split, split, split, split, maps)
    out_specs = (maps, maps, P(AXES, None), split, split, split, split)

    def body(*args):
        return local(sizes, *args)

    return jax.shard_map(body, mesh=mesh, in_specs=in_specs, out_specs=out_specs, check_vma=False)
```

```python
import functools
import math

import jax
import jax.numpy as jnp
from jax import lax
from jax.experimental import pallas as pl
from jax.experimental.pallas import tpu as pltpu
from jax.sharding import PartitionSpec as P

GROUPS = 32
EPS = 1e-05
AXES = ("dp", "fsdp")
LANES = 128
VEC_ROWS = 16


class Wires:
    def __init__(self, n_dp, n_fsdp):
        self.n_fsdp = n_fsdp
        self.n = n_dp * n_fsdp
        self.bits = int(math.log2(self.n))
        fsdp_bits = int(math.log2(n_fsdp))
        assert 1 << self.bits == self.n and 1 << fsdp_bits == n_fsdp and fsdp_bits >= 3 and n_dp >= 2
        a, b = 1, fsdp_bits
        far = [bit for bit in range(self.bits - 1, 0, -1) if bit not in (a, b)]
        self.far = len(far)
        self.order = {0: [*far, a, b], 1: [*far[::-1], b, a]}
        self.stages = self.bits - 1
        self.slots = 1 << self.stages

    def swap(self, value, stage, turned=0):
        def bit(core):
            return 0 if stage == self.stages else self.bit_of(stage, core, turned)

        return lax.ppermute(value, AXES, [(i, i ^ (1 << bit(i & 1))) for i in range(self.n)])

    def bit_of(self, stage, core, turned):
        return self.order[core ^ turned if stage >= self.far else core][stage]

    def mask(self, slot, core, turned):
        return sum(1 << self.bit_of(i, core, turned) for i in range(self.stages) if slot >> i & 1)

    def me(self):
        return lax.axis_index("dp") * self.n_fsdp + lax.axis_index("fsdp")

    def owner(self, slot, other, me, turned=0):
        core = me & 1
        if other:
            me, core = me ^ 1, 1 - core
        return me ^ jnp.where(core == 0, self.mask(slot, 0, turned), self.mask(slot, 1, turned))


def owner(self, slot, other, me):
        core = me & 1
        if other:
            me, core = me ^ 1, 1 - core
        return me ^ jnp.where(core == 0, self.mask(slot, 0), self.mask(slot, 1))


ROWS = 4
UNITS = 2
PIECE = 64
F32 = jnp.float32
BF16 = jnp.bfloat16
VMEM_BYTES = 14 * 1024 * 1024


def group_sum(totals):
    channels = totals.shape[1]
    lane = lax.broadcasted_iota(jnp.int32, totals.shape, 1)
    span = 1
    while span < channels // GROUPS:
        up = pltpu.roll(totals, channels - span, 1)
        down = pltpu.roll(totals, span, 1)
        totals = totals + jnp.where((lane & span) == 0, up, down)
        span *= 2
    return totals


def fold(values):
    channels = values.shape[-1]
    return jnp.sum(values.reshape(-1, 8, channels), 0)


def total(partial):
    return jnp.sum(partial, 0, keepdims=True)


def sigmoid(v):
    return 0.5 * jnp.tanh(0.5 * v) + 0.5


def clear_edges(three):
    height = three.shape[1] - 2
    zero = jnp.zeros((3, 1) + three.shape[2:], three.dtype)
    three[:, 0:1] = zero
    three[:, height + 1 : height + 2] = zero


def store_three(three, row, value):
    width = value.shape[0]
    column = lax.broadcasted_iota(jnp.int32, value.shape, 0)
    left = jnp.where(column == 0, 0.0, pltpu.roll(value, 1, 0))
    right = jnp.where(column == width - 1, 0.0, pltpu.roll(value, width - 1, 0))
    three[0, row + 1] = left.astype(three.dtype)
    three[1, row + 1] = value.astype(three.dtype)
    three[2, row + 1] = right.astype(three.dtype)


def accumulators(body, *refs):
    groups = 4

    def run(*accs):
        accs = iter(accs)
        body(*refs, [[[next(accs) for _ in range(ROWS)] for _ in range(groups)] for _ in range(UNITS)])

    pl.run_scoped(run, *[pltpu.ACC(unit)((PIECE, 2 * LANES), F32) for unit in range(UNITS) for _ in range(groups * ROWS)])


def interleave(pieces, slots):
    return [pieces * (i + 1) // slots - pieces * i // slots for i in range(slots)]


def times(value, size):
    return value * size if isinstance(value, int) else pl.multiple_of(value * size, size)


def conv_step(accs, three, kernel, step, parity, back, others=()):
    others = list(others)
    for tap, share in enumerate(interleave(len(others), 9)):
        at = (8 - tap if back else tap) * three.shape[3]
        stage = (parity + tap) % 2
        for unit in range(UNITS):
            pltpu.matmul_push_rhs(kernel[at : at + three.shape[3], :], stage, unit, transpose=back)
        for piece in range(ROWS):
            for unit in range(UNITS):
                row = (UNITS * step + unit) * ROWS + piece + tap // 3
                pltpu.matmul_acc_lhs(
                    accs[unit][parity][piece], three[tap % 3, row], load_staged_rhs=stage if piece == 0 else None
                )
        for _ in range(share):
            others.pop(0)()


def conv_rows(accs, step, parity, use):
    def one(unit, piece):
        use((UNITS * step + unit) * ROWS + piece, pltpu.matmul_pop(accs[unit][parity][piece]))

    return [functools.partial(one, unit, piece) for unit in range(UNITS) for piece in range(ROWS)]


def conv_all(accs, three, kernel, back, use):
    steps = (three.shape[1] - 2) // (UNITS * ROWS)
    for step in range(steps):
        others = conv_rows(accs, step - 1, (step - 1) % 2, use) if step else ()
        conv_step(accs, three, kernel, step, step % 2, back, others)
    for other in conv_rows(accs, steps - 1, (steps - 1) % 2, use):
        other()


class Sums:
    def __init__(self, channels, count):
        self.values = [jnp.zeros((8, channels), F32)] * count

    def add(self, *values):
        self.values = [s + fold(v) for s, v in zip(self.values, values)]

    def totals(self):
        return [total(s) for s in self.values]


def store_turned(turned, padded, row):
    width, channels = padded.shape[1:]
    size = ROWS * width
    lanes = pl.ds(times(row // ROWS, size), size)
    turned[0, :, lanes] = padded[pl.ds(row + 1, ROWS)].reshape(size, channels).T
    turned[1, :, lanes] = padded[pl.ds(row, ROWS)].reshape(size, channels).T


def turn_end(turned, padded):
    height = padded.shape[0] - 2
    width, channels = padded.shape[1:]
    at = height * width
    turned[1, :, at : at + 2 * width] = padded[height : height + 2].reshape(2 * width, channels).T


def grad_step(accs, turned, three, work, stage, others=()):
    others = list(others)
    width, channels = three.shape[2:]
    size = ROWS * width
    for unit, column, chunk, _ in work:
        rhs = three[column, pl.ds(1 + times(chunk, ROWS), ROWS)].reshape(size, channels)
        pltpu.matmul_push_rhs(rhs, stage, unit)
    shares = iter(interleave(len(others), 3 * ROWS))
    for row in range(3):
        for piece in range(ROWS):
            for unit, _, chunk, groups in work:
                source, at = (0, times(chunk, size)) if row == 1 else (1, times(chunk, size) + row * width)
                lhs = turned[source, piece * PIECE : (piece + 1) * PIECE, pl.ds(at, size)]
                first = row == 0 and piece == 0
                pltpu.matmul_acc_lhs(accs[unit][groups[row]][piece], lhs, load_staged_rhs=stage if first else None)
            for _ in range(next(shares)):
                others.pop(0)()


def kernel_grad(accs, turned, three, flat, beside, carry):
    height, channels = three.shape[1] - 2, three.shape[3]
    chunks = height // ROWS

    def outer(i, carry):
        kept = [carry]

        def other(row):
            kept[0] = beside(row, kept[0])

        for k in range(4):
            chunk = 4 * i + k
            work = [(0, 0, chunk, (0, 1, 2)), (1, 2, chunk, (0, 1, 2))]
            others = [functools.partial(other, ROWS * chunk + j) for j in range(ROWS)] if beside else ()
            grad_step(accs, turned, three, work, k % 2, others)
        return kept[0]

    if beside:
        carry = lax.fori_loop(0, chunks // 4, outer, carry)
    else:
        for i in range(chunks // 4):
            outer(i, carry)

    def store(tap, piece, value):
        store_flat(flat, (tap * channels + piece * PIECE) * 2, value)

    def side(unit, column, row, piece):
        store(3 * row + 2 - column, piece, pltpu.matmul_pop(accs[unit][row][piece]))

    for row in range(2):
        for unit, column in ((0, 0), (1, 2)):
            for piece in range(ROWS):
                side(unit, column, row, piece)
    half = chunks // UNITS
    for chunk in range(half):
        work = [(unit, 1, unit * half + chunk, (3, 0, 1)) for unit in range(UNITS)]
        others = [functools.partial(side, unit, 2 * unit, 2, piece) for unit in range(UNITS) for piece in range(ROWS)]
        grad_step(accs, turned, three, work, chunk % 2, others if chunk == 0 else ())
    for row, group in enumerate((3, 0, 1)):
        for piece in range(ROWS):
            store(3 * row + 1, piece, pltpu.matmul_pop(accs[0][group][piece]) + pltpu.matmul_pop(accs[1][group][piece]))
    return carry


def store_flat(flat, start, value):
    rows = value.shape[0]
    flat[pl.ds(start, rows, stride=2), :] = value[:, :LANES]
    flat[pl.ds(start + 1, rows, stride=2), :] = value[:, LANES:]


def load_flat(flat, start, rows):
    left = flat[pl.ds(start, rows, stride=2), :]
    right = flat[pl.ds(start + 1, rows, stride=2), :]
    return jnp.concatenate([left, right], axis=1)


def stats_kernel(x_hbm, stats, x, arrived):
    height, width, channels = x.shape
    count = height * width * (channels // GROUPS)
    zero = jnp.zeros((8, channels), F32)
    parts = arrived.shape[0]
    rows = height // parts
    copies = [
        pltpu.make_async_copy(x_hbm.at[pl.ds(k * rows, rows)], x.at[pl.ds(k * rows, rows)], arrived.at[k])
        for k in range(parts)
    ]
    for copy in copies:
        copy.start()
    s = zero
    for k, copy in enumerate(copies):
        copy.wait()
        s = lax.fori_loop(0, rows // 4, lambda i, s, k=k: s + fold(x[pl.ds(k * rows + i * 4, 4)].astype(F32)), s)
    mean = group_sum(total(s)) / count

    def second(i, v):
        d = x[pl.ds(i * 4, 4)].astype(F32) - mean
        return v + fold(d * d)

    v = lax.fori_loop(0, height // 4, second, zero)
    inv = lax.rsqrt(group_sum(total(v)) / count + EPS)
    stats[0:1, :] = mean
    stats[1:2, :] = inv


def spread_kernel(g_hbm, three_hbm, g_sum, g, three, arrived, left):
    height, width, channels = g.shape
    parts = arrived.shape[0]
    rows = height // parts
    copies = [
        pltpu.make_async_copy(g_hbm.at[pl.ds(k * rows, rows)], g.at[pl.ds(k * rows, rows)], arrived.at[k])
        for k in range(parts)
    ]
    for copy in copies:
        copy.start()
    clear_edges(three)
    s = jnp.zeros((8, channels), F32)
    out = []
    for k, copy in enumerate(copies):
        copy.wait()

        def step(i, s, k=k):
            row = k * rows + i * 4
            values = g[pl.ds(row, 4)].astype(F32)
            for j in range(4):
                store_three(three, row + j, values[j])
            return s + fold(values)

        s = lax.fori_loop(0, rows // 4, step, s)
        start = k * rows + (1 if k else 0)
        size = rows + (1 if k == 0 else 0) + (1 if k == parts - 1 else 0)
        away = pltpu.make_async_copy(three.at[:, pl.ds(start, size)], three_hbm.at[:, pl.ds(start, size)], left.at[k])
        away.start()
        out.append(away)
    g_sum[...] = total(s)
    for away in out:
        away.wait()


def first_kernel(x, stats, vec, time, kernel, turned, raw, stats_out, three):
    accumulators(first_body, x, stats, vec, time, kernel, turned, raw, stats_out, three)


def first_body(x, stats, vec, time, kernel, turned, raw, stats_out, three, accs):
    height, width, channels = x.shape
    pixels = height * width
    per_group = channels // GROUPS
    mean, scale, shift = stats[0:1, :], stats[1:2, :] * vec[0:1, :], vec[1:2, :]
    offset = vec[2:3, :] + time[...]
    sums = Sums(channels, 2)
    pivot = []
    clear_edges(three)

    def activate(row):
        h = (x[row].astype(F32) - mean) * scale + shift
        store_three(three, row, h * sigmoid(h))
        if row % ROWS == ROWS - 1:
            store_turned(turned, three.at[1], row + 1 - ROWS)

    def use(row, v):
        if row == 0:
            pivot.append(total(fold(v)) / width)
        raw[row * width : (row + 1) * width, :] = v
        d = v - pivot[0]
        sums.add(d, d * d)

    per_step = UNITS * ROWS
    steps = height // per_step
    for row in range(per_step + 1):
        activate(row)
    for step in range(steps):
        ahead = range((step + 1) * per_step + 1, min((step + 2) * per_step + 1, height))
        others = [functools.partial(activate, row) for row in ahead]
        done = conv_rows(accs, step - 1, (step - 1) % 2, use) if step else []
        mixed = [f for i in range(per_step) for f in (*others[i : i + 1], *done[i : i + 1])]
        conv_step(accs, three, kernel, step, step % 2, False, mixed)
    turn_end(turned, three.at[1])
    for other in conv_rows(accs, steps - 1, (steps - 1) % 2, use):
        other()
    part, square = [v / pixels for v in sums.totals()]
    spread = square - part * part
    middle = pivot[0] + part + offset
    mean_two = group_sum(middle) / per_group
    away = middle - mean_two
    stats_out[0:1, :] = offset - mean_two
    stats_out[1:2, :] = lax.rsqrt(group_sum(spread + away * away) / per_group + EPS)


def second_kernel(g_three, raw, stats, vec, kernel, act, sums, flat, three, dc_sum, dh, turned):
    accumulators(second_body, g_three, raw, stats, vec, kernel, act, sums, flat, three, dc_sum, dh, turned)


def second_body(g_three, raw, stats, vec, kernel, act, sums, flat, three, dc_sum, dh, turned, accs):
    height, width, channels = act.shape[0] - 2, act.shape[1], act.shape[2]
    count = height * width * (channels // GROUPS)
    move, inv, gain, shift = stats[0:1, :], stats[1:2, :], vec[3:4, :], vec[4:5, :]
    scale = inv * gain
    both = Sums(channels, 2)
    act[0:1] = jnp.zeros((1, width, channels), BF16)
    act[height + 1 : height + 2] = jnp.zeros((1, width, channels), BF16)
    clear_edges(three)

    def use(row, v):
        at = slice(row * width, (row + 1) * width)
        c = raw[at, :] + move
        h = c * scale + shift
        sig = sigmoid(h)
        a = h * sig
        act[row + 1] = a.astype(BF16)
        d = v * (sig + a * (1.0 - sig))
        dh[at, :] = d
        both.add(d, d * c)
        if row % ROWS == ROWS - 1:
            store_turned(turned, act, row + 1 - ROWS)

    conv_all(accs, g_three, kernel, True, use)
    turn_end(turned, act)
    s, sc = both.totals()
    sn = sc * inv
    sums[0:1, :] = sn
    sums[1:2, :] = s
    base = inv * (group_sum(s * gain) / count)
    slope = inv * inv * (group_sum(sn * gain) / count)

    def back(row, dc):
        at = pl.ds(times(row, width), width)
        d = dh[at, :] * scale - base - (raw[at, :] + move) * slope
        store_three(three, row, d)
        return dc + fold(d)

    dc_sum[...] = total(kernel_grad(accs, turned, g_three, flat, back, jnp.zeros((8, channels), F32)))


def third_kernel(three, x, stats, vec, kernel, dh, sums):
    accumulators(third_body, three, x, stats, vec, kernel, dh, sums)


def third_body(three, x, stats, vec, kernel, dh, sums, accs):
    height, width, channels = x.shape
    mean, scale, shift = stats[0:1, :], stats[1:2, :] * vec[0:1, :], vec[1:2, :]
    both = Sums(channels, 2)

    def use(row, v):
        c = x[row].astype(F32) - mean
        h = c * scale + shift
        sig = sigmoid(h)
        d = v * (sig + h * sig * (1.0 - sig))
        dh[row * width : (row + 1) * width, :] = d
        both.add(d, d * c)

    conv_all(accs, three, kernel, True, use)
    s, sn = both.totals()
    sums[0:1, :] = sn * stats[1:2, :]
    sums[1:2, :] = s


def input_kernel(dh, x, g, stats, sums, vec, dc_sum, kernel, embedding, result, emb_grad, done):
    height, width, channels = x.shape
    count = height * width * (channels // GROUPS)
    mean, inv, gain = stats[0:1, :], stats[1:2, :], vec[0:1, :]
    scale = inv * gain
    base = inv * (group_sum(sums[1:2, :] * gain) / count)
    slope = inv * inv * (group_sum(sums[0:1, :] * gain) / count)

    def back(i, _):
        row = i * 4
        d = dh[pl.ds(row * width, 4 * width), :].reshape(4, width, channels)
        c = x[pl.ds(row, 4)].astype(F32) - mean
        result[pl.ds(row, 4)] = g[pl.ds(row, 4)].astype(F32) + (d * scale - base - c * slope)
        return 0

    lax.fori_loop(0, height // 4, back, 0)
    dq = lax.dot_general(
        dc_sum[...],
        kernel[9 * channels :, :].astype(F32),
        (((1,), (1,)), ((), ())),
        precision=lax.Precision.HIGHEST,
        preferred_element_type=F32,
    )
    emb = embedding[...].astype(F32)
    sig = sigmoid(emb)
    emb_grad[...] = dq * (sig * (1.0 + emb * (1.0 - sig)))
    done[...] = base


def last_kernel(part, parts, *refs):
    accumulators(functools.partial(last_body, part, parts), *refs)


def last_body(part, parts, act, x, vec, kernel, *refs):
    out, done, three, result, left, accs = refs[-6:]
    height = x.shape[0]
    rows = height // parts
    base = part * rows
    bias = vec[5:6, :]

    def spread(row):
        if 0 <= base + row < height:
            store_three(three, row, act[base + row + 1].astype(F32))
        else:
            three[:, row + 1 : row + 2] = jnp.zeros((3, 1) + three.shape[2:], BF16)

    def use(row, v):
        result[row] = (x[base + row].astype(F32) + v + bias).astype(BF16)

    per_step = UNITS * ROWS
    steps = rows // per_step
    copies = []

    def send(step):
        here = pl.ds(step * per_step, per_step)
        copies.append(pltpu.make_async_copy(result.at[here], out.at[pl.ds(base + step * per_step, per_step)], left.at[step]))
        copies[-1].start()

    for row in range(-1, per_step + 1):
        spread(row)
    for step in range(steps):
        ahead = range((step + 1) * per_step + 1, min((step + 2) * per_step, rows) + 1)
        others = [functools.partial(spread, row) for row in ahead]
        done_rows = conv_rows(accs, step - 1, (step - 1) % 2, use) if step else []
        mixed = [f for i in range(per_step) for f in (*others[i : i + 1], *done_rows[i : i + 1])]
        conv_step(accs, three, kernel, step, step % 2, False, mixed)
        if step:
            send(step - 1)
    for other in conv_rows(accs, steps - 1, (steps - 1) % 2, use):
        other()
    send(steps - 1)
    done[...] = bias
    for copy in copies:
        copy.wait()


def join_kernel(mine, got, out, tail=VEC_ROWS):
    rows = mine.shape[0] - tail
    out[0:rows, :] = mine[0:rows, :]
    out[rows : 2 * rows, :] = got[0:rows, :]
    if tail:
        out[2 * rows :, :] = mine[rows:, :] + got[rows:, :]


def join_both_kernel(first, first_got, second, second_got, first_out, second_out):
    join_kernel(first, first_got, first_out)
    join_kernel(second, second_got, second_out, 0)


def part_kernel(cuts, mine, got, first, second):
    block, cut = sum(cuts), sum(cuts[:-1])
    slots = (mine.shape[0] - VEC_ROWS) // block
    for half, source in enumerate((mine, got)):
        for slot in range(slots):
            at, to = slot * block, half * slots + slot
            first[to * cut : (to + 1) * cut, :] = source[at : at + cut, :]
            second[to * cuts[-1] : (to + 1) * cuts[-1], :] = source[at + cut : at + block, :]
    first[2 * slots * cut :, :] = mine[slots * block :, :] + got[slots * block :, :]


def halve_kernel(keep, got, send_next, keep_next, tail=VEC_ROWS):
    rows = (keep.shape[0] - tail) // 2
    keep_next[0:rows, :] = keep[0:rows, :] + got[0:rows, :].astype(F32)
    send_next[0:rows, :] = (keep[rows : 2 * rows, :] + got[rows : 2 * rows, :].astype(F32)).astype(BF16)
    if tail:
        vec = keep[2 * rows :, :] + got[2 * rows :, :].astype(F32)
        keep_next[rows:, :] = vec
        send_next[rows:, :] = vec.astype(BF16)


def halve_second_kernel(keep, got, send_next, keep_next):
    halve_kernel(keep, got, send_next, keep_next, 0)


def merge_kernel(wide, narrow, one, one_got, two_send, two, send, keep):
    slots = two.shape[0] // narrow
    for slot in range(slots):
        to = slot * (wide + narrow)
        at, up = slot * wide, (slots + slot) * wide
        keep[to : to + wide, :] = one[at : at + wide, :] + one_got[at : at + wide, :].astype(F32)
        send[to : to + wide, :] = (one[up : up + wide, :] + one_got[up : up + wide, :].astype(F32)).astype(BF16)
        at, to, up = slot * narrow, to + wide, to + wide + narrow
        keep[to:up, :] = two[at : at + narrow, :]
        send[to:up, :] = two_send[at : at + narrow, :]
    at, to = 2 * slots * wide, slots * (wide + narrow)
    values = one[at:, :] + one_got[at:, :].astype(F32)
    keep[to:, :] = values
    send[to:, :] = values.astype(BF16)


def place_blocks(wires, cuts, mine, got, flats, turned=0):
    me = wires.me()
    block = sum(cuts)
    for slot in range(wires.slots):
        for other, source in ((False, mine), (True, got)):
            owner = wires.owner(slot, other, me, turned)
            values = source[slot * block : (slot + 1) * block, :].astype(F32)
            at = 0
            for flat, rows in zip(flats, cuts):
                flat[pl.ds(pl.multiple_of(owner * rows, rows), rows), :] = values[at : at + rows]
                at += rows


def unflatten(flat, out, base):
    for start in range(0, flat.shape[0] // 2, 256):
        out[base + start : base + start + 256, :] = load_flat(flat, 2 * start, 256).astype(BF16)


def arrange_first_kernel(wires, cuts, mine, got, embedding, first, vec, time, flat_one, flat_project, flat_vec):
    place_blocks(wires, cuts, mine, got, (flat_one, flat_project))
    rows_one = flat_one.shape[0] // 2
    unflatten(flat_project, first, rows_one)
    emb = embedding[...].astype(F32)
    act = (emb * sigmoid(emb)).astype(BF16)
    time[...] = jnp.dot(act, first[rows_one:, :], preferred_element_type=F32)
    unflatten(flat_one, first, 0)
    at = wires.slots * sum(cuts)
    flat_vec[...] = mine[at : at + VEC_ROWS, :].astype(F32) + got[at : at + VEC_ROWS, :].astype(F32)
    vec[...] = load_flat(flat_vec, 0, VEC_ROWS // 2)


def arrange_second_kernel(wires, cuts, mine, got, second, flat_two):
    place_blocks(wires, cuts, mine, got, (flat_two,), 1)
    unflatten(flat_two, second, 0)


def grad_kernel(turned, three, flat):
    accumulators(lambda *refs: kernel_grad(refs[-1], *refs[:-1], None, 0), turned, three, flat)


def take_blocks(wires, cuts, flats, send, keep):
    me = wires.me()
    block = sum(cuts)
    for slot in range(wires.slots):
        for other in (True, False):
            owner = wires.owner(slot, other, me)
            at = slot * block
            for flat, rows in zip(flats, cuts):
                values = flat[pl.ds(pl.multiple_of(owner * rows, rows), rows), :]
                if other:
                    send[at : at + rows, :] = values.astype(BF16)
                else:
                    keep[at : at + rows, :] = values
                at += rows


def pack_first_kernel(
    wires, cuts, flat_one, embedding, dc_sum, sums_one, sums_two, g_sum, two, two_got,
    send, keep, two_send, two_keep, flat_project,
):
    halve_kernel(two, two_got, two_send, two_keep, 0)
    emb = embedding[...].astype(F32)
    q = (emb * sigmoid(emb)).astype(BF16).astype(F32)
    q = jnp.broadcast_to(q, (LANES, q.shape[1])).T
    dc = dc_sum[...]
    store_flat(flat_project, 0, jnp.concatenate([q * dc[:, :LANES], q * dc[:, LANES:]], axis=1))
    take_blocks(wires, cuts, (flat_one, flat_project), send, keep)
    at = wires.slots * sum(cuts)
    vectors = [sums_one[0:1, :], sums_one[1:2, :], dc, sums_two[0:1, :], sums_two[1:2, :], g_sum[...]]
    halves = [row[:, i * LANES : (i + 1) * LANES] for row in vectors for i in range(2)]
    values = jnp.concatenate(halves + [jnp.zeros((VEC_ROWS - len(halves), LANES), F32)], axis=0)
    keep[at : at + VEC_ROWS, :] = values
    send[at : at + VEC_ROWS, :] = values.astype(BF16)


def pack_second_kernel(wires, cuts, flat, send, keep):
    take_blocks(wires, cuts, (flat,), send, keep)


def finish_kernel(wires, cuts, n_vec, keep, got, one, project, two, vec):
    at = 0
    for out, rows in zip((one, project, two), cuts):
        out[...] = keep[at : at + rows, :] + got[at : at + rows, :].astype(F32)
        at += rows
    vectors = keep[at : at + VEC_ROWS, :] + got[at : at + VEC_ROWS, :].astype(F32)
    start = wires.me() * n_vec
    row, lane = start // LANES, start % LANES
    place = lax.broadcasted_iota(jnp.int32, vectors.shape, 0)
    own = jnp.sum(jnp.where(place == row, vectors, 0.0), 0, keepdims=True)
    following = jnp.sum(jnp.where(place == row + 1, vectors, 0.0), 0, keepdims=True)
    column = lax.broadcasted_iota(jnp.int32, own.shape, 1)
    shifted = pltpu.roll(jnp.where(column >= lane, own, following), (LANES - lane) % LANES, 1)
    vec[...] = shifted[:, :n_vec]


def call(body, outs, *args, scratch=(), flops=0, size=4 << 20, after=(), far=(), far_outs=(), semaphores=(), same=None):
    held, n_in = len(after), len(args)

    def run(*refs):
        body(*refs[:n_in], *refs[n_in + held :])

    args = [pltpu.with_memory_space_constraint(v, pltpu.HBM) if i in far else v for i, v in enumerate(args)]

    def spec(is_far):
        return pl.BlockSpec(memory_space=pltpu.HBM if is_far else pltpu.VMEM)

    return pl.pallas_call(
        run,
        out_shape=[
            pltpu.HBM(shape, dtype) if i in far_outs else jax.ShapeDtypeStruct(shape, dtype)
            for i, (shape, dtype) in enumerate(outs)
        ],
        in_specs=[spec(i in far) for i in range(n_in)] + [pl.BlockSpec(memory_space=pl.ANY)] * held,
        out_specs=[spec(i in far_outs) for i in range(len(outs))],
        scratch_shapes=[pltpu.VMEM(shape, dtype) for shape, dtype in scratch]
        + [pltpu.SemaphoreType.DMA((n,)) for n in semaphores],
        input_output_aliases=same or {},
        compiler_params=pltpu.CompilerParams(vmem_limit_bytes=VMEM_BYTES),
        cost_estimate=pl.CostEstimate(flops=flops, bytes_accessed=size, transcendentals=0),
    )(*args, *after)


def joined(held, tail=VEC_ROWS):
    return ((2 * (held.shape[0] - tail) + tail, LANES), BF16)


def gather_start(wires, cuts, held, beside):
    part = wires.far - 1
    for stage in range(part):
        after = beside.get(stage, ())
        held, = call(join_kernel, [joined(held)], held, wires.swap(held, stage), after=after)
    got = wires.swap(held, part)
    slots = 2 << part
    shapes = [(slots * sum(cuts[:-1]) + VEC_ROWS, LANES), (slots * cuts[-1], LANES)]
    outs = [(shape, BF16) for shape in shapes]
    first, second = call(functools.partial(part_kernel, cuts), outs, held, got, after=beside.get(part, ()))
    for stage in range(wires.far, wires.stages):
        first_got, second_got = wires.swap(first, stage), wires.swap(second, stage, 1)
        outs = [joined(first), joined(second, 0)]
        after = beside.get(stage, ())
        first, second = call(join_both_kernel, outs, first, first_got, second, second_got, after=after)
    return first, wires.swap(first, wires.stages), second, wires.swap(second, wires.stages)


def in_order(wires, cuts, mine, got, turned=0):
    block = sum(cuts)
    rows = wires.slots * block
    both = jnp.concatenate([mine[:rows], got[:rows]]).reshape(wires.n, block, LANES)
    me = wires.me()
    owners = jnp.stack([wires.owner(j, other, me, turned) for other in (False, True) for j in range(wires.slots)])
    both = jnp.zeros_like(both).at[owners].set(both)
    ends = [sum(cuts[:i]) for i in range(len(cuts) + 1)]
    return [both[:, a:b].reshape(-1, 2 * LANES) for a, b in zip(ends, ends[1:])]


def arrange_first(wires, cuts, mine, got, embedding):
    channels = 2 * LANES
    totals = [wires.n * rows for rows in cuts]
    if all(rows % 8 == 0 for rows in cuts):
        return call(
            functools.partial(arrange_first_kernel, wires, cuts),
            [((sum(totals) // 2, channels), BF16), ((VEC_ROWS // 2, channels), F32), ((1, channels), F32)],
            mine,
            got,
            embedding,
            scratch=[((rows, LANES), F32) for rows in (*totals, VEC_ROWS)],
        )
    one, project = in_order(wires, cuts, mine, got)
    vec = (mine[-VEC_ROWS:].astype(F32) + got[-VEC_ROWS:].astype(F32)).reshape(VEC_ROWS // 2, channels)
    act = jax.nn.silu(embedding.astype(F32)).astype(BF16)
    return jnp.concatenate([one, project]), vec, jnp.dot(act, project, preferred_element_type=F32)


def arrange_second(wires, cuts, mine, got, after):
    rows = wires.n * cuts[0]
    if cuts[0] % 8 == 0:
        body = functools.partial(arrange_second_kernel, wires, cuts)
        return call(body, [((rows // 2, 2 * LANES), BF16)], mine, got, scratch=[((rows, LANES), F32)], after=after)[0]
    return in_order(wires, cuts, mine, got, 1)[0]


def out_of_order(wires, cuts, parts, tail):
    me = wires.me()
    blocks = jnp.concatenate([v.reshape(wires.n, rows, LANES) for v, rows in zip(parts, cuts)], axis=1)
    halves = []
    for other in (True, False):
        owners = jnp.stack([wires.owner(j, other, me) for j in range(wires.slots)])
        halves.append(jnp.concatenate([blocks[owners].reshape(-1, LANES), tail]))
    return halves[0].astype(BF16), halves[1]


def pack_first(wires, cuts, flat_one, embedding, dc_sum, sums_one, sums_two, g_sum, two, two_got):
    shape = (wires.slots * sum(cuts) + VEC_ROWS, LANES)
    if all(rows % 8 == 0 for rows in cuts):
        return call(
            functools.partial(pack_first_kernel, wires, cuts),
            [(shape, BF16), (shape, F32), *halved(two, 0)],
            flat_one,
            embedding,
            dc_sum,
            sums_one,
            sums_two,
            g_sum,
            two,
            two_got,
            scratch=[((wires.n * cuts[1], LANES), F32)],
        )
    q = jax.nn.silu(embedding.astype(F32)).astype(BF16).astype(F32).reshape(-1, 1)
    vec = jnp.concatenate([sums_one, dc_sum, sums_two, g_sum]).reshape(-1, LANES)
    vec = jnp.pad(vec, ((0, VEC_ROWS - vec.shape[0]), (0, 0)))
    send, keep = out_of_order(wires, cuts, (flat_one, (q * dc_sum).reshape(-1, LANES)), vec)
    return send, keep, *call(halve_second_kernel, halved(two, 0), two, two_got)


def pack_second(wires, cuts, flat):
    if cuts[0] % 8 == 0:
        shape = (wires.slots * cuts[0], LANES)
        return call(functools.partial(pack_second_kernel, wires, cuts), [(shape, BF16), (shape, F32)], flat)
    return out_of_order(wires, cuts, (flat,), jnp.zeros((0, LANES), F32))


def halved(keep, tail=VEC_ROWS):
    shape = ((keep.shape[0] - tail) // 2 + tail, LANES)
    return [(shape, BF16), (shape, F32)]


def local(sizes, images, embedding, conv_first, conv_second, projection, vectors, cotangent):
    count, height, width, channels = images.shape
    emb_width = embedding.shape[-1]
    wires = Wires(*sizes)
    n_vec = vectors.shape[0]
    assert count == 1 and channels == 2 * LANES and n_vec <= LANES
    cuts = [v.shape[0] // LANES for v in (conv_first, conv_second, projection)]
    pixels = height * width
    three = ((3, height + 2, width, channels), BF16)
    maps = ((height, width, channels), BF16)
    flat = ((pixels, channels), F32)
    line = ((1, channels), F32)
    pair = ((2, channels), F32)
    taps = ((18 * channels, LANES), F32)
    padded = ((height + 2, width, channels), BF16)
    turned = ((2, channels, pixels + 2 * width), BF16)
    conv_flops = 2 * 9 * pixels * channels * channels

    x, g = images[0], cotangent[0]
    stats, x_near = call(stats_kernel, [pair, maps], x, far=(0,), semaphores=(4,))
    g_three, g_sum = call(
        spread_kernel, [three, line], g, scratch=[maps, three], far=(0,), far_outs=(0,), semaphores=(4, 4)
    )
    wide = VEC_ROWS * LANES
    placed = lax.dynamic_slice(jnp.pad(vectors, (wide, wide - n_vec)), (wide - wires.me() * n_vec,), (wide,))
    start = jnp.concatenate([v.reshape(-1, LANES) for v in (conv_first, projection, conv_second, placed)])
    beside = {wires.stages - 2: (g_sum,), wires.stages - 1: (stats,)}
    one, one_got, two, two_got = gather_start(wires, (cuts[0], cuts[2], cuts[1]), start, beside)
    first, vec, time = arrange_first(wires, (cuts[0], cuts[2]), one, one_got, embedding)

    turned_one, raw, stats_two = call(
        first_kernel, [turned, flat, pair], x_near, stats, vec, time, first, scratch=[three], flops=conv_flops
    )
    kernel_two = arrange_second(wires, cuts[1:2], two, two_got, (stats_two,))
    act_two, sums_two, grad_two, e_three, dc_sum = call(
        second_kernel,
        [padded, pair, taps, three, line],
        g_three,
        raw,
        stats_two,
        vec,
        kernel_two,
        scratch=[flat, turned],
        flops=2 * conv_flops,
    )
    last = wires.stages
    two_send, two = pack_second(wires, cuts[1:2], grad_two)
    two_got = wires.swap(two_send, last)
    dh_one, sums_one = call(third_kernel, [flat, pair], e_three, x_near, stats, vec, first, flops=conv_flops)
    two_send, two = call(halve_second_kernel, halved(two, 0), two, two_got, after=(sums_one,))
    two_got = wires.swap(two_send, last - 1)
    grad_one, = call(grad_kernel, [taps], turned_one, e_three, flops=conv_flops)
    one_cuts = (cuts[0], cuts[2])
    one_send, one, two_send, two = pack_first(
        wires, one_cuts, grad_one, embedding, dc_sum, sums_one, sums_two, g_sum, two, two_got
    )
    input_grad, embedding_grad, input_done = call(
        input_kernel,
        [(maps[0], F32), ((1, emb_width), F32), line],
        dh_one,
        x,
        g,
        stats,
        sums_one,
        vec,
        dc_sum,
        first,
        embedding,
    )
    parts = 2
    rows = height // parts
    output, output_done = (), []
    for part in range(parts):
        *output, done = call(
            functools.partial(last_kernel, part, parts),
            [maps, line],
            act_two,
            x_near,
            vec,
            kernel_two,
            *output,
            scratch=[((3, rows + 2, width, channels), BF16), ((rows, width, channels), BF16)],
            far=(4,),
            far_outs=(0,),
            semaphores=(rows // (UNITS * ROWS),),
            same={4: 0} if output else None,
            flops=conv_flops // parts,
        )
        output_done.append(done)
    one_got = wires.swap(one_send, last)
    one_send, one = call(halve_kernel, halved(one), one, one_got, after=(input_done,))
    one_got = wires.swap(one_send, last - 1)
    wide, narrow = sum(one_cuts), cuts[1]
    shape = (wires.slots // 4 * (wide + narrow) + VEC_ROWS, LANES)
    send, keep = call(
        functools.partial(merge_kernel, wide, narrow),
        [(shape, BF16), (shape, F32)],
        one,
        one_got,
        two_send,
        two,
        after=(output_done[0],),
    )
    for stage in range(last - 2, 0, -1):
        after = (output_done[1],) if stage == last - 2 else ()
        send, keep = call(halve_kernel, halved(keep), keep, wires.swap(send, stage), after=after)
    all_cuts = (*one_cuts, cuts[1])
    first_sum, project_sum, second_sum, vec_sum = call(
        functools.partial(finish_kernel, wires, all_cuts, n_vec),
        [*[((rows, LANES), F32) for rows in all_cuts], ((1, n_vec), F32)],
        keep,
        wires.swap(send, 0),
    )
    summed = (first_sum, second_sum, project_sum, vec_sum)
    return (output[0][None], input_grad[None], embedding_grad, *[v.reshape(-1) for v in summed])


def solution(mesh):
    sizes = (mesh.shape["dp"], mesh.shape["fsdp"])
    split = P(AXES)
    maps = P(AXES, None, None, None)
    in_specs = (maps, P(AXES, None), split, split, split, split, maps)
    out_specs = (maps, maps, P(AXES, None), split, split, split, split)

    def body(*args):
        return local(sizes, *args)

    return jax.shard_map(body, mesh=mesh, in_specs=in_specs, out_specs=out_specs, check_vma=False)
```

```python
import functools
import math

import jax
import jax.numpy as jnp
from jax import lax
from jax.experimental import pallas as pl
from jax.experimental.pallas import tpu as pltpu
from jax.sharding import PartitionSpec as P

GROUPS = 32
EPS = 1e-05
AXES = ("dp", "fsdp")
LANES = 128
VEC_ROWS = 16


class Wires:
    def __init__(self, n_dp, n_fsdp):
        self.n_fsdp = n_fsdp
        self.n = n_dp * n_fsdp
        self.bits = int(math.log2(self.n))
        fsdp_bits = int(math.log2(n_fsdp))
        assert 1 << self.bits == self.n and 1 << fsdp_bits == n_fsdp and fsdp_bits >= 3 and n_dp >= 2
        a, b = 1, fsdp_bits
        far = [bit for bit in range(self.bits - 1, 0, -1) if bit not in (a, b)]
        self.order = {0: [*far, a, b], 1: [*far[::-1], b, a]}
        self.stages = self.bits - 1
        self.slots = 1 << self.stages

    def swap(self, value, stage):
        def bit(core):
            return 0 if stage == self.stages else self.order[core][stage]

        return lax.ppermute(value, AXES, [(i, i ^ (1 << bit(i & 1))) for i in range(self.n)])

    def mask(self, slot, core):
        return sum(1 << self.order[core][i] for i in range(self.stages) if slot >> i & 1)

    def me(self):
        return lax.axis_index("dp") * self.n_fsdp + lax.axis_index("fsdp")

    def owner(self, slot, other, me):
        core = me & 1
        if other:
            me, core = me ^ 1, 1 - core
        return me ^ jnp.where(core == 0, self.mask(slot, 0), self.mask(slot, 1))


def owner(self, slot, other, me):
        core = me & 1
        if other:
            me, core = me ^ 1, 1 - core
        return me ^ jnp.where(core == 0, self.mask(slot, 0), self.mask(slot, 1))


ROWS = 4
UNITS = 2
PIECE = 64
F32 = jnp.float32
BF16 = jnp.bfloat16
VMEM_BYTES = 14 * 1024 * 1024


def group_sum(totals):
    channels = totals.shape[1]
    lane = lax.broadcasted_iota(jnp.int32, totals.shape, 1)
    span = 1
    while span < channels // GROUPS:
        up = pltpu.roll(totals, channels - span, 1)
        down = pltpu.roll(totals, span, 1)
        totals = totals + jnp.where((lane & span) == 0, up, down)
        span *= 2
    return totals


def fold(values):
    channels = values.shape[-1]
    return jnp.sum(values.reshape(-1, 8, channels), 0)


def total(partial):
    return jnp.sum(partial, 0, keepdims=True)


def sigmoid(v):
    return 0.5 * jnp.tanh(0.5 * v) + 0.5


def clear_edges(three):
    height = three.shape[1] - 2
    zero = jnp.zeros((3, 1) + three.shape[2:], three.dtype)
    three[:, 0:1] = zero
    three[:, height + 1 : height + 2] = zero


def store_three(three, row, value):
    width = value.shape[0]
    column = lax.broadcasted_iota(jnp.int32, value.shape, 0)
    left = jnp.where(column == 0, 0.0, pltpu.roll(value, 1, 0))
    right = jnp.where(column == width - 1, 0.0, pltpu.roll(value, width - 1, 0))
    three[0, row + 1] = left.astype(three.dtype)
    three[1, row + 1] = value.astype(three.dtype)
    three[2, row + 1] = right.astype(three.dtype)


def accumulators(body, *refs):
    groups = 4

    def run(*accs):
        accs = iter(accs)
        body(*refs, [[[next(accs) for _ in range(ROWS)] for _ in range(groups)] for _ in range(UNITS)])

    pl.run_scoped(run, *[pltpu.ACC(unit)((PIECE, 2 * LANES), F32) for unit in range(UNITS) for _ in range(groups * ROWS)])


def interleave(pieces, slots):
    return [pieces * (i + 1) // slots - pieces * i // slots for i in range(slots)]


def times(value, size):
    return value * size if isinstance(value, int) else pl.multiple_of(value * size, size)


def conv_step(accs, three, kernel, step, parity, back, others=()):
    others = list(others)
    for tap, share in enumerate(interleave(len(others), 9)):
        at = (8 - tap if back else tap) * three.shape[3]
        stage = (parity + tap) % 2
        for unit in range(UNITS):
            pltpu.matmul_push_rhs(kernel[at : at + three.shape[3], :], stage, unit, transpose=back)
        for piece in range(ROWS):
            for unit in range(UNITS):
                row = (UNITS * step + unit) * ROWS + piece + tap // 3
                pltpu.matmul_acc_lhs(
                    accs[unit][parity][piece], three[tap % 3, row], load_staged_rhs=stage if piece == 0 else None
                )
        for _ in range(share):
            others.pop(0)()


def conv_rows(accs, step, parity, use):
    def one(unit, piece):
        use((UNITS * step + unit) * ROWS + piece, pltpu.matmul_pop(accs[unit][parity][piece]))

    return [functools.partial(one, unit, piece) for unit in range(UNITS) for piece in range(ROWS)]


def conv_all(accs, three, kernel, back, use):
    steps = (three.shape[1] - 2) // (UNITS * ROWS)
    for step in range(steps):
        others = conv_rows(accs, step - 1, (step - 1) % 2, use) if step else ()
        conv_step(accs, three, kernel, step, step % 2, back, others)
    for other in conv_rows(accs, steps - 1, (steps - 1) % 2, use):
        other()


class Sums:
    def __init__(self, channels, count):
        self.values = [jnp.zeros((8, channels), F32)] * count

    def add(self, *values):
        self.values = [s + fold(v) for s, v in zip(self.values, values)]

    def totals(self):
        return [total(s) for s in self.values]


def store_turned(turned, padded, row):
    width, channels = padded.shape[1:]
    size = ROWS * width
    lanes = pl.ds(times(row // ROWS, size), size)
    turned[0, :, lanes] = padded[pl.ds(row + 1, ROWS)].reshape(size, channels).T
    turned[1, :, lanes] = padded[pl.ds(row, ROWS)].reshape(size, channels).T


def turn_end(turned, padded):
    height = padded.shape[0] - 2
    width, channels = padded.shape[1:]
    at = height * width
    turned[1, :, at : at + 2 * width] = padded[height : height + 2].reshape(2 * width, channels).T


def grad_step(accs, turned, three, work, stage, others=()):
    others = list(others)
    width, channels = three.shape[2:]
    size = ROWS * width
    for unit, column, chunk, _ in work:
        rhs = three[column, pl.ds(1 + times(chunk, ROWS), ROWS)].reshape(size, channels)
        pltpu.matmul_push_rhs(rhs, stage, unit)
    shares = iter(interleave(len(others), 3 * ROWS))
    for row in range(3):
        for piece in range(ROWS):
            for unit, _, chunk, groups in work:
                source, at = (0, times(chunk, size)) if row == 1 else (1, times(chunk, size) + row * width)
                lhs = turned[source, piece * PIECE : (piece + 1) * PIECE, pl.ds(at, size)]
                first = row == 0 and piece == 0
                pltpu.matmul_acc_lhs(accs[unit][groups[row]][piece], lhs, load_staged_rhs=stage if first else None)
            for _ in range(next(shares)):
                others.pop(0)()


def kernel_grad(accs, turned, three, flat, beside, carry):
    height, channels = three.shape[1] - 2, three.shape[3]
    chunks = height // ROWS

    def outer(i, carry):
        kept = [carry]

        def other(row):
            kept[0] = beside(row, kept[0])

        for k in range(4):
            chunk = 4 * i + k
            work = [(0, 0, chunk, (0, 1, 2)), (1, 2, chunk, (0, 1, 2))]
            others = [functools.partial(other, ROWS * chunk + j) for j in range(ROWS)] if beside else ()
            grad_step(accs, turned, three, work, k % 2, others)
        return kept[0]

    if beside:
        carry = lax.fori_loop(0, chunks // 4, outer, carry)
    else:
        for i in range(chunks // 4):
            outer(i, carry)

    def store(tap, piece, value):
        store_flat(flat, (tap * channels + piece * PIECE) * 2, value)

    def side(unit, column, row, piece):
        store(3 * row + 2 - column, piece, pltpu.matmul_pop(accs[unit][row][piece]))

    for row in range(2):
        for unit, column in ((0, 0), (1, 2)):
            for piece in range(ROWS):
                side(unit, column, row, piece)
    half = chunks // UNITS
    for chunk in range(half):
        work = [(unit, 1, unit * half + chunk, (3, 0, 1)) for unit in range(UNITS)]
        others = [functools.partial(side, unit, 2 * unit, 2, piece) for unit in range(UNITS) for piece in range(ROWS)]
        grad_step(accs, turned, three, work, chunk % 2, others if chunk == 0 else ())
    for row, group in enumerate((3, 0, 1)):
        for piece in range(ROWS):
            store(3 * row + 1, piece, pltpu.matmul_pop(accs[0][group][piece]) + pltpu.matmul_pop(accs[1][group][piece]))
    return carry


def store_flat(flat, start, value):
    rows = value.shape[0]
    flat[pl.ds(start, rows, stride=2), :] = value[:, :LANES]
    flat[pl.ds(start + 1, rows, stride=2), :] = value[:, LANES:]


def load_flat(flat, start, rows):
    left = flat[pl.ds(start, rows, stride=2), :]
    right = flat[pl.ds(start + 1, rows, stride=2), :]
    return jnp.concatenate([left, right], axis=1)


def stats_kernel(x_hbm, stats, x, arrived):
    height, width, channels = x.shape
    count = height * width * (channels // GROUPS)
    zero = jnp.zeros((8, channels), F32)
    parts = arrived.shape[0]
    rows = height // parts
    copies = [
        pltpu.make_async_copy(x_hbm.at[pl.ds(k * rows, rows)], x.at[pl.ds(k * rows, rows)], arrived.at[k])
        for k in range(parts)
    ]
    for copy in copies:
        copy.start()
    s = zero
    for k, copy in enumerate(copies):
        copy.wait()
        s = lax.fori_loop(0, rows // 4, lambda i, s, k=k: s + fold(x[pl.ds(k * rows + i * 4, 4)].astype(F32)), s)
    mean = group_sum(total(s)) / count

    def second(i, v):
        d = x[pl.ds(i * 4, 4)].astype(F32) - mean
        return v + fold(d * d)

    v = lax.fori_loop(0, height // 4, second, zero)
    inv = lax.rsqrt(group_sum(total(v)) / count + EPS)
    stats[0:1, :] = mean
    stats[1:2, :] = inv


def spread_kernel(g_hbm, three_hbm, g_sum, g, three, arrived, left):
    height, width, channels = g.shape
    parts = arrived.shape[0]
    rows = height // parts
    copies = [
        pltpu.make_async_copy(g_hbm.at[pl.ds(k * rows, rows)], g.at[pl.ds(k * rows, rows)], arrived.at[k])
        for k in range(parts)
    ]
    for copy in copies:
        copy.start()
    clear_edges(three)
    s = jnp.zeros((8, channels), F32)
    out = []
    for k, copy in enumerate(copies):
        copy.wait()

        def step(i, s, k=k):
            row = k * rows + i * 4
            values = g[pl.ds(row, 4)].astype(F32)
            for j in range(4):
                store_three(three, row + j, values[j])
            return s + fold(values)

        s = lax.fori_loop(0, rows // 4, step, s)
        start = k * rows + (1 if k else 0)
        size = rows + (1 if k == 0 else 0) + (1 if k == parts - 1 else 0)
        away = pltpu.make_async_copy(three.at[:, pl.ds(start, size)], three_hbm.at[:, pl.ds(start, size)], left.at[k])
        away.start()
        out.append(away)
    g_sum[...] = total(s)
    for away in out:
        away.wait()


def first_kernel(x, stats, vec, time, kernel, turned, raw, stats_out, three):
    accumulators(first_body, x, stats, vec, time, kernel, turned, raw, stats_out, three)


def first_body(x, stats, vec, time, kernel, turned, raw, stats_out, three, accs):
    height, width, channels = x.shape
    pixels = height * width
    per_group = channels // GROUPS
    mean, scale, shift = stats[0:1, :], stats[1:2, :] * vec[0:1, :], vec[1:2, :]
    offset = vec[2:3, :] + time[...]
    sums = Sums(channels, 2)
    pivot = []
    clear_edges(three)

    def activate(row):
        h = (x[row].astype(F32) - mean) * scale + shift
        store_three(three, row, h * sigmoid(h))
        if row % ROWS == ROWS - 1:
            store_turned(turned, three.at[1], row + 1 - ROWS)

    def use(row, v):
        if row == 0:
            pivot.append(total(fold(v)) / width)
        raw[row * width : (row + 1) * width, :] = v
        d = v - pivot[0]
        sums.add(d, d * d)

    per_step = UNITS * ROWS
    steps = height // per_step
    for row in range(per_step + 1):
        activate(row)
    for step in range(steps):
        ahead = range((step + 1) * per_step + 1, min((step + 2) * per_step + 1, height))
        others = [functools.partial(activate, row) for row in ahead]
        done = conv_rows(accs, step - 1, (step - 1) % 2, use) if step else []
        mixed = [f for i in range(per_step) for f in (*others[i : i + 1], *done[i : i + 1])]
        conv_step(accs, three, kernel, step, step % 2, False, mixed)
    turn_end(turned, three.at[1])
    for other in conv_rows(accs, steps - 1, (steps - 1) % 2, use):
        other()
    part, square = [v / pixels for v in sums.totals()]
    spread = square - part * part
    middle = pivot[0] + part + offset
    mean_two = group_sum(middle) / per_group
    away = middle - mean_two
    stats_out[0:1, :] = offset - mean_two
    stats_out[1:2, :] = lax.rsqrt(group_sum(spread + away * away) / per_group + EPS)


def second_kernel(g_three, raw, stats, vec, kernel, act, sums, flat, three, dc_sum, dh, turned):
    accumulators(second_body, g_three, raw, stats, vec, kernel, act, sums, flat, three, dc_sum, dh, turned)


def second_body(g_three, raw, stats, vec, kernel, act, sums, flat, three, dc_sum, dh, turned, accs):
    height, width, channels = act.shape[0] - 2, act.shape[1], act.shape[2]
    count = height * width * (channels // GROUPS)
    move, inv, gain, shift = stats[0:1, :], stats[1:2, :], vec[3:4, :], vec[4:5, :]
    scale = inv * gain
    both = Sums(channels, 2)
    act[0:1] = jnp.zeros((1, width, channels), BF16)
    act[height + 1 : height + 2] = jnp.zeros((1, width, channels), BF16)
    clear_edges(three)

    def use(row, v):
        at = slice(row * width, (row + 1) * width)
        c = raw[at, :] + move
        h = c * scale + shift
        sig = sigmoid(h)
        a = h * sig
        act[row + 1] = a.astype(BF16)
        d = v * (sig + a * (1.0 - sig))
        dh[at, :] = d
        both.add(d, d * c)
        if row % ROWS == ROWS - 1:
            store_turned(turned, act, row + 1 - ROWS)

    conv_all(accs, g_three, kernel, True, use)
    turn_end(turned, act)
    s, sc = both.totals()
    sn = sc * inv
    sums[0:1, :] = sn
    sums[1:2, :] = s
    base = inv * (group_sum(s * gain) / count)
    slope = inv * inv * (group_sum(sn * gain) / count)

    def back(row, dc):
        at = pl.ds(times(row, width), width)
        d = dh[at, :] * scale - base - (raw[at, :] + move) * slope
        store_three(three, row, d)
        return dc + fold(d)

    dc_sum[...] = total(kernel_grad(accs, turned, g_three, flat, back, jnp.zeros((8, channels), F32)))


def third_kernel(three, x, stats, vec, kernel, dh, sums):
    accumulators(third_body, three, x, stats, vec, kernel, dh, sums)


def third_body(three, x, stats, vec, kernel, dh, sums, accs):
    height, width, channels = x.shape
    mean, scale, shift = stats[0:1, :], stats[1:2, :] * vec[0:1, :], vec[1:2, :]
    both = Sums(channels, 2)

    def use(row, v):
        c = x[row].astype(F32) - mean
        h = c * scale + shift
        sig = sigmoid(h)
        d = v * (sig + h * sig * (1.0 - sig))
        dh[row * width : (row + 1) * width, :] = d
        both.add(d, d * c)

    conv_all(accs, three, kernel, True, use)
    s, sn = both.totals()
    sums[0:1, :] = sn * stats[1:2, :]
    sums[1:2, :] = s


def input_kernel(dh, x, g, stats, sums, vec, dc_sum, kernel, embedding, result, emb_grad, done):
    height, width, channels = x.shape
    count = height * width * (channels // GROUPS)
    mean, inv, gain = stats[0:1, :], stats[1:2, :], vec[0:1, :]
    scale = inv * gain
    base = inv * (group_sum(sums[1:2, :] * gain) / count)
    slope = inv * inv * (group_sum(sums[0:1, :] * gain) / count)

    def back(i, _):
        row = i * 4
        d = dh[pl.ds(row * width, 4 * width), :].reshape(4, width, channels)
        c = x[pl.ds(row, 4)].astype(F32) - mean
        result[pl.ds(row, 4)] = g[pl.ds(row, 4)].astype(F32) + (d * scale - base - c * slope)
        return 0

    lax.fori_loop(0, height // 4, back, 0)
    dq = lax.dot_general(
        dc_sum[...],
        kernel[9 * channels :, :].astype(F32),
        (((1,), (1,)), ((), ())),
        precision=lax.Precision.HIGHEST,
        preferred_element_type=F32,
    )
    emb = embedding[...].astype(F32)
    sig = sigmoid(emb)
    emb_grad[...] = dq * (sig * (1.0 + emb * (1.0 - sig)))
    done[...] = base


def last_kernel(part, parts, *refs):
    accumulators(functools.partial(last_body, part, parts), *refs)


def last_body(part, parts, act, x, vec, kernel, *refs):
    out, done, three, result, left, accs = refs[-6:]
    height = x.shape[0]
    rows = height // parts
    base = part * rows
    bias = vec[5:6, :]

    def spread(row):
        if 0 <= base + row < height:
            store_three(three, row, act[base + row + 1].astype(F32))
        else:
            three[:, row + 1 : row + 2] = jnp.zeros((3, 1) + three.shape[2:], BF16)

    def use(row, v):
        result[row] = (x[base + row].astype(F32) + v + bias).astype(BF16)

    per_step = UNITS * ROWS
    steps = rows // per_step
    copies = []

    def send(step):
        here = pl.ds(step * per_step, per_step)
        copies.append(pltpu.make_async_copy(result.at[here], out.at[pl.ds(base + step * per_step, per_step)], left.at[step]))
        copies[-1].start()

    for row in range(-1, per_step + 1):
        spread(row)
    for step in range(steps):
        ahead = range((step + 1) * per_step + 1, min((step + 2) * per_step, rows) + 1)
        others = [functools.partial(spread, row) for row in ahead]
        done_rows = conv_rows(accs, step - 1, (step - 1) % 2, use) if step else []
        mixed = [f for i in range(per_step) for f in (*others[i : i + 1], *done_rows[i : i + 1])]
        conv_step(accs, three, kernel, step, step % 2, False, mixed)
        if step:
            send(step - 1)
    for other in conv_rows(accs, steps - 1, (steps - 1) % 2, use):
        other()
    send(steps - 1)
    done[...] = bias
    for copy in copies:
        copy.wait()


def join_kernel(mine, got, out, tail=VEC_ROWS):
    rows = mine.shape[0] - tail
    out[0:rows, :] = mine[0:rows, :]
    out[rows : 2 * rows, :] = got[0:rows, :]
    if tail:
        out[2 * rows :, :] = mine[rows:, :] + got[rows:, :]


def join_second_kernel(mine, got, out, mark):
    join_kernel(mine, got, out, 0)
    mark[...] = jnp.zeros_like(mark)


def part_kernel(cuts, mine, got, first, second):
    block, cut = sum(cuts), sum(cuts[:-1])
    slots = (mine.shape[0] - VEC_ROWS) // block
    for half, source in enumerate((mine, got)):
        for slot in range(slots):
            at, to = slot * block, half * slots + slot
            first[to * cut : (to + 1) * cut, :] = source[at : at + cut, :]
            second[to * cuts[-1] : (to + 1) * cuts[-1], :] = source[at + cut : at + block, :]
    first[2 * slots * cut :, :] = mine[slots * block :, :] + got[slots * block :, :]


def halve_kernel(keep, got, send_next, keep_next, tail=VEC_ROWS):
    rows = (keep.shape[0] - tail) // 2
    keep_next[0:rows, :] = keep[0:rows, :] + got[0:rows, :].astype(F32)
    send_next[0:rows, :] = (keep[rows : 2 * rows, :] + got[rows : 2 * rows, :].astype(F32)).astype(BF16)
    if tail:
        vec = keep[2 * rows :, :] + got[2 * rows :, :].astype(F32)
        keep_next[rows:, :] = vec
        send_next[rows:, :] = vec.astype(BF16)


def halve_second_kernel(keep, got, send_next, keep_next):
    halve_kernel(keep, got, send_next, keep_next, 0)


def merge_kernel(wide, narrow, one, one_got, two_send, two, send, keep):
    slots = two.shape[0] // narrow
    for slot in range(slots):
        to = slot * (wide + narrow)
        at, up = slot * wide, (slots + slot) * wide
        keep[to : to + wide, :] = one[at : at + wide, :] + one_got[at : at + wide, :].astype(F32)
        send[to : to + wide, :] = (one[up : up + wide, :] + one_got[up : up + wide, :].astype(F32)).astype(BF16)
        at, to, up = slot * narrow, to + wide, to + wide + narrow
        keep[to:up, :] = two[at : at + narrow, :]
        send[to:up, :] = two_send[at : at + narrow, :]
    at, to = 2 * slots * wide, slots * (wide + narrow)
    values = one[at:, :] + one_got[at:, :].astype(F32)
    keep[to:, :] = values
    send[to:, :] = values.astype(BF16)


def place_blocks(wires, cuts, mine, got, flats):
    me = wires.me()
    block = sum(cuts)
    for slot in range(wires.slots):
        for other, source in ((False, mine), (True, got)):
            owner = wires.owner(slot, other, me)
            values = source[slot * block : (slot + 1) * block, :].astype(F32)
            at = 0
            for flat, rows in zip(flats, cuts):
                flat[pl.ds(pl.multiple_of(owner * rows, rows), rows), :] = values[at : at + rows]
                at += rows


def unflatten(flat, out, base):
    for start in range(0, flat.shape[0] // 2, 256):
        out[base + start : base + start + 256, :] = load_flat(flat, 2 * start, 256).astype(BF16)


def arrange_first_kernel(wires, cuts, mine, got, embedding, first, vec, time, flat_one, flat_project, flat_vec):
    place_blocks(wires, cuts, mine, got, (flat_one, flat_project))
    rows_one = flat_one.shape[0] // 2
    unflatten(flat_project, first, rows_one)
    emb = embedding[...].astype(F32)
    act = (emb * sigmoid(emb)).astype(BF16)
    time[...] = jnp.dot(act, first[rows_one:, :], preferred_element_type=F32)
    unflatten(flat_one, first, 0)
    at = wires.slots * sum(cuts)
    flat_vec[...] = mine[at : at + VEC_ROWS, :].astype(F32) + got[at : at + VEC_ROWS, :].astype(F32)
    vec[...] = load_flat(flat_vec, 0, VEC_ROWS // 2)


def arrange_second_kernel(wires, cuts, mine, got, second, flat_two):
    place_blocks(wires, cuts, mine, got, (flat_two,))
    unflatten(flat_two, second, 0)


def grad_kernel(turned, three, flat):
    accumulators(lambda *refs: kernel_grad(refs[-1], *refs[:-1], None, 0), turned, three, flat)


def take_blocks(wires, cuts, flats, send, keep):
    me = wires.me()
    block = sum(cuts)
    for slot in range(wires.slots):
        for other in (True, False):
            owner = wires.owner(slot, other, me)
            at = slot * block
            for flat, rows in zip(flats, cuts):
                values = flat[pl.ds(pl.multiple_of(owner * rows, rows), rows), :]
                if other:
                    send[at : at + rows, :] = values.astype(BF16)
                else:
                    keep[at : at + rows, :] = values
                at += rows


def pack_first_kernel(
    wires, cuts, flat_one, embedding, dc_sum, sums_one, sums_two, g_sum, two, two_got,
    send, keep, two_send, two_keep, flat_project,
):
    halve_kernel(two, two_got, two_send, two_keep, 0)
    emb = embedding[...].astype(F32)
    q = (emb * sigmoid(emb)).astype(BF16).astype(F32)
    q = jnp.broadcast_to(q, (LANES, q.shape[1])).T
    dc = dc_sum[...]
    store_flat(flat_project, 0, jnp.concatenate([q * dc[:, :LANES], q * dc[:, LANES:]], axis=1))
    take_blocks(wires, cuts, (flat_one, flat_project), send, keep)
    at = wires.slots * sum(cuts)
    vectors = [sums_one[0:1, :], sums_one[1:2, :], dc, sums_two[0:1, :], sums_two[1:2, :], g_sum[...]]
    halves = [row[:, i * LANES : (i + 1) * LANES] for row in vectors for i in range(2)]
    values = jnp.concatenate(halves + [jnp.zeros((VEC_ROWS - len(halves), LANES), F32)], axis=0)
    keep[at : at + VEC_ROWS, :] = values
    send[at : at + VEC_ROWS, :] = values.astype(BF16)


def pack_second_kernel(wires, cuts, flat, send, keep):
    take_blocks(wires, cuts, (flat,), send, keep)


def finish_kernel(wires, cuts, n_vec, keep, got, one, project, two, vec):
    at = 0
    for out, rows in zip((one, project, two), cuts):
        out[...] = keep[at : at + rows, :] + got[at : at + rows, :].astype(F32)
        at += rows
    vectors = keep[at : at + VEC_ROWS, :] + got[at : at + VEC_ROWS, :].astype(F32)
    start = wires.me() * n_vec
    row, lane = start // LANES, start % LANES
    place = lax.broadcasted_iota(jnp.int32, vectors.shape, 0)
    own = jnp.sum(jnp.where(place == row, vectors, 0.0), 0, keepdims=True)
    following = jnp.sum(jnp.where(place == row + 1, vectors, 0.0), 0, keepdims=True)
    column = lax.broadcasted_iota(jnp.int32, own.shape, 1)
    shifted = pltpu.roll(jnp.where(column >= lane, own, following), (LANES - lane) % LANES, 1)
    vec[...] = shifted[:, :n_vec]


def call(body, outs, *args, scratch=(), flops=0, size=4 << 20, after=(), far=(), far_outs=(), semaphores=(), same=None):
    held, n_in = len(after), len(args)

    def run(*refs):
        body(*refs[:n_in], *refs[n_in + held :])

    args = [pltpu.with_memory_space_constraint(v, pltpu.HBM) if i in far else v for i, v in enumerate(args)]

    def spec(is_far):
        return pl.BlockSpec(memory_space=pltpu.HBM if is_far else pltpu.VMEM)

    return pl.pallas_call(
        run,
        out_shape=[
            pltpu.HBM(shape, dtype) if i in far_outs else jax.ShapeDtypeStruct(shape, dtype)
            for i, (shape, dtype) in enumerate(outs)
        ],
        in_specs=[spec(i in far) for i in range(n_in)] + [pl.BlockSpec(memory_space=pl.ANY)] * held,
        out_specs=[spec(i in far_outs) for i in range(len(outs))],
        scratch_shapes=[pltpu.VMEM(shape, dtype) for shape, dtype in scratch]
        + [pltpu.SemaphoreType.DMA((n,)) for n in semaphores],
        input_output_aliases=same or {},
        compiler_params=pltpu.CompilerParams(vmem_limit_bytes=VMEM_BYTES),
        cost_estimate=pl.CostEstimate(flops=0, bytes_accessed=0, transcendentals=0),
    )(*args, *after)


def joined(held, tail=VEC_ROWS):
    return ((2 * (held.shape[0] - tail) + tail, LANES), BF16)


def gather_start(wires, cuts, held, beside):
    last = wires.stages - 1
    for stage in range(last - 1):
        after = beside.get(stage, ())
        held, = call(join_kernel, [joined(held)], held, wires.swap(held, stage), after=after)
    got = wires.swap(held, last - 1)
    slots = wires.slots // 2
    shapes = [(slots * sum(cuts[:-1]) + VEC_ROWS, LANES), (slots * cuts[-1], LANES)]
    outs = [(shape, BF16) for shape in shapes]
    first, second = call(functools.partial(part_kernel, cuts), outs, held, got, after=beside.get(last - 1, ()))
    first_got, second_got = wires.swap(first, last), wires.swap(second, last)
    first, = call(join_kernel, [joined(first)], first, first_got, after=beside.get(last, ()))
    second, mark = call(join_second_kernel, [joined(second, 0), ((1, LANES), F32)], second, second_got)
    return first, wires.swap(first, wires.stages), second, wires.swap(second, wires.stages), mark


def in_order(wires, cuts, mine, got):
    block = sum(cuts)
    rows = wires.slots * block
    both = jnp.concatenate([mine[:rows], got[:rows]]).reshape(wires.n, block, LANES)
    me = wires.me()
    owners = jnp.stack([wires.owner(j, other, me) for other in (False, True) for j in range(wires.slots)])
    both = jnp.zeros_like(both).at[owners].set(both)
    ends = [sum(cuts[:i]) for i in range(len(cuts) + 1)]
    return [both[:, a:b].reshape(-1, 2 * LANES) for a, b in zip(ends, ends[1:])]


def arrange_first(wires, cuts, mine, got, embedding, after):
    channels = 2 * LANES
    totals = [wires.n * rows for rows in cuts]
    if all(rows % 8 == 0 for rows in cuts):
        return call(
            functools.partial(arrange_first_kernel, wires, cuts),
            [((sum(totals) // 2, channels), BF16), ((VEC_ROWS // 2, channels), F32), ((1, channels), F32)],
            mine,
            got,
            embedding,
            scratch=[((rows, LANES), F32) for rows in (*totals, VEC_ROWS)],
            after=after,
        )
    one, project = in_order(wires, cuts, mine, got)
    vec = (mine[-VEC_ROWS:].astype(F32) + got[-VEC_ROWS:].astype(F32)).reshape(VEC_ROWS // 2, channels)
    act = jax.nn.silu(embedding.astype(F32)).astype(BF16)
    return jnp.concatenate([one, project]), vec, jnp.dot(act, project, preferred_element_type=F32)


def arrange_second(wires, cuts, mine, got, after):
    rows = wires.n * cuts[0]
    if cuts[0] % 8 == 0:
        body = functools.partial(arrange_second_kernel, wires, cuts)
        return call(body, [((rows // 2, 2 * LANES), BF16)], mine, got, scratch=[((rows, LANES), F32)], after=after)[0]
    return in_order(wires, cuts, mine, got)[0]


def out_of_order(wires, cuts, parts, tail):
    me = wires.me()
    blocks = jnp.concatenate([v.reshape(wires.n, rows, LANES) for v, rows in zip(parts, cuts)], axis=1)
    halves = []
    for other in (True, False):
        owners = jnp.stack([wires.owner(j, other, me) for j in range(wires.slots)])
        halves.append(jnp.concatenate([blocks[owners].reshape(-1, LANES), tail]))
    return halves[0].astype(BF16), halves[1]


def pack_first(wires, cuts, flat_one, embedding, dc_sum, sums_one, sums_two, g_sum, two, two_got):
    shape = (wires.slots * sum(cuts) + VEC_ROWS, LANES)
    if all(rows % 8 == 0 for rows in cuts):
        return call(
            functools.partial(pack_first_kernel, wires, cuts),
            [(shape, BF16), (shape, F32), *halved(two, 0)],
            flat_one,
            embedding,
            dc_sum,
            sums_one,
            sums_two,
            g_sum,
            two,
            two_got,
            scratch=[((wires.n * cuts[1], LANES), F32)],
        )
    q = jax.nn.silu(embedding.astype(F32)).astype(BF16).astype(F32).reshape(-1, 1)
    vec = jnp.concatenate([sums_one, dc_sum, sums_two, g_sum]).reshape(-1, LANES)
    vec = jnp.pad(vec, ((0, VEC_ROWS - vec.shape[0]), (0, 0)))
    send, keep = out_of_order(wires, cuts, (flat_one, (q * dc_sum).reshape(-1, LANES)), vec)
    return send, keep, *call(halve_second_kernel, halved(two, 0), two, two_got)


def pack_second(wires, cuts, flat):
    if cuts[0] % 8 == 0:
        shape = (wires.slots * cuts[0], LANES)
        return call(functools.partial(pack_second_kernel, wires, cuts), [(shape, BF16), (shape, F32)], flat)
    return out_of_order(wires, cuts, (flat,), jnp.zeros((0, LANES), F32))


def halved(keep, tail=VEC_ROWS):
    shape = ((keep.shape[0] - tail) // 2 + tail, LANES)
    return [(shape, BF16), (shape, F32)]


def local(sizes, images, embedding, conv_first, conv_second, projection, vectors, cotangent):
    count, height, width, channels = images.shape
    emb_width = embedding.shape[-1]
    wires = Wires(*sizes)
    n_vec = vectors.shape[0]
    assert count == 1 and channels == 2 * LANES and n_vec <= LANES
    cuts = [v.shape[0] // LANES for v in (conv_first, conv_second, projection)]
    pixels = height * width
    three = ((3, height + 2, width, channels), BF16)
    maps = ((height, width, channels), BF16)
    flat = ((pixels, channels), F32)
    line = ((1, channels), F32)
    pair = ((2, channels), F32)
    taps = ((18 * channels, LANES), F32)
    padded = ((height + 2, width, channels), BF16)
    turned = ((2, channels, pixels + 2 * width), BF16)
    conv_flops = 2 * 9 * pixels * channels * channels

    x, g = images[0], cotangent[0]
    stats, x_near = call(stats_kernel, [pair, maps], x, far=(0,), semaphores=(4,))
    g_three, g_sum = call(
        spread_kernel, [three, line], g, scratch=[maps, three], far=(0,), far_outs=(0,), semaphores=(4, 4)
    )
    wide = VEC_ROWS * LANES
    placed = lax.dynamic_slice(jnp.pad(vectors, (wide, wide - n_vec)), (wide - wires.me() * n_vec,), (wide,))
    start = jnp.concatenate([v.reshape(-1, LANES) for v in (conv_first, projection, conv_second, placed)])
    beside = {wires.stages - 2: (g_sum,), wires.stages - 1: (stats,)}
    one, one_got, two, two_got, mark = gather_start(wires, (cuts[0], cuts[2], cuts[1]), start, beside)
    first, vec, time = arrange_first(wires, (cuts[0], cuts[2]), one, one_got, embedding, (mark,))

    turned_one, raw, stats_two = call(
        first_kernel, [turned, flat, pair], x_near, stats, vec, time, first, scratch=[three], flops=conv_flops
    )
    kernel_two = arrange_second(wires, cuts[1:2], two, two_got, (stats_two,))
    act_two, sums_two, grad_two, e_three, dc_sum = call(
        second_kernel,
        [padded, pair, taps, three, line],
        g_three,
        raw,
        stats_two,
        vec,
        kernel_two,
        scratch=[flat, turned],
        flops=2 * conv_flops,
    )
    last = wires.stages
    two_send, two = pack_second(wires, cuts[1:2], grad_two)
    two_got = wires.swap(two_send, last)
    dh_one, sums_one = call(third_kernel, [flat, pair], e_three, x_near, stats, vec, first, flops=conv_flops)
    two_send, two = call(halve_second_kernel, halved(two, 0), two, two_got, after=(sums_one,))
    two_got = wires.swap(two_send, last - 1)
    grad_one, = call(grad_kernel, [taps], turned_one, e_three, flops=conv_flops)
    one_cuts = (cuts[0], cuts[2])
    one_send, one, two_send, two = pack_first(
        wires, one_cuts, grad_one, embedding, dc_sum, sums_one, sums_two, g_sum, two, two_got
    )
    input_grad, embedding_grad, input_done = call(
        input_kernel,
        [(maps[0], F32), ((1, emb_width), F32), line],
        dh_one,
        x,
        g,
        stats,
        sums_one,
        vec,
        dc_sum,
        first,
        embedding,
    )
    parts = 2
    rows = height // parts
    output, output_done = (), []
    for part in range(parts):
        *output, done = call(
            functools.partial(last_kernel, part, parts),
            [maps, line],
            act_two,
            x_near,
            vec,
            kernel_two,
            *output,
            scratch=[((3, rows + 2, width, channels), BF16), ((rows, width, channels), BF16)],
            far=(4,),
            far_outs=(0,),
            semaphores=(rows // (UNITS * ROWS),),
            same={4: 0} if output else None,
            flops=conv_flops // parts,
        )
        output_done.append(done)
    one_got = wires.swap(one_send, last)
    one_send, one = call(halve_kernel, halved(one), one, one_got)
    one_got = wires.swap(one_send, last - 1)
    wide, narrow = sum(one_cuts), cuts[1]
    shape = (wires.slots // 4 * (wide + narrow) + VEC_ROWS, LANES)
    send, keep = call(
        functools.partial(merge_kernel, wide, narrow),
        [(shape, BF16), (shape, F32)],
        one,
        one_got,
        two_send,
        two,
        after=(output_done[0],),
    )
    for stage in range(last - 2, 0, -1):
        after = {last - 2: (output_done[1],), last - 3: (input_done,)}.get(stage, ())
        send, keep = call(halve_kernel, halved(keep), keep, wires.swap(send, stage), after=after)
    all_cuts = (*one_cuts, cuts[1])
    first_sum, project_sum, second_sum, vec_sum = call(
        functools.partial(finish_kernel, wires, all_cuts, n_vec),
        [*[((rows, LANES), F32) for rows in all_cuts], ((1, n_vec), F32)],
        keep,
        wires.swap(send, 0),
    )
    summed = (first_sum, second_sum, project_sum, vec_sum)
    return (output[0][None], input_grad[None], embedding_grad, *[v.reshape(-1) for v in summed])


def solution(mesh):
    sizes = (mesh.shape["dp"], mesh.shape["fsdp"])
    split = P(AXES)
    maps = P(AXES, None, None, None)
    in_specs = (maps, P(AXES, None), split, split, split, split, maps)
    out_specs = (maps, maps, P(AXES, None), split, split, split, split)

    def body(*args):
        return local(sizes, *args)

    return jax.shard_map(body, mesh=mesh, in_specs=in_specs, out_specs=out_specs, check_vma=False)
```

```python
import functools
import math

import jax
import jax.numpy as jnp
from jax import lax
from jax.experimental import pallas as pl
from jax.experimental.pallas import tpu as pltpu
from jax.sharding import PartitionSpec as P

GROUPS = 32
EPS = 1e-05
AXES = ("dp", "fsdp")
LANES = 128
VEC_ROWS = 16


class Wires:
    def __init__(self, n_dp, n_fsdp):
        self.n_fsdp = n_fsdp
        self.n = n_dp * n_fsdp
        self.bits = int(math.log2(self.n))
        fsdp_bits = int(math.log2(n_fsdp))
        assert 1 << self.bits == self.n and 1 << fsdp_bits == n_fsdp and fsdp_bits >= 3 and n_dp >= 2
        a, b = 1, fsdp_bits
        far = [bit for bit in range(self.bits - 1, 0, -1) if bit not in (a, b)]
        self.order = {0: [*far, a, b], 1: [*far[::-1], b, a]}
        self.stages = self.bits - 1
        self.slots = 1 << self.stages

    def swap(self, value, stage):
        def bit(core):
            return 0 if stage == self.stages else self.order[core][stage]

        return lax.ppermute(value, AXES, [(i, i ^ (1 << bit(i & 1))) for i in range(self.n)])

    def mask(self, slot, core):
        return sum(1 << self.order[core][i] for i in range(self.stages) if slot >> i & 1)

    def me(self):
        return lax.axis_index("dp") * self.n_fsdp + lax.axis_index("fsdp")

    def owner(self, slot, other, me):
        core = me & 1
        if other:
            me, core = me ^ 1, 1 - core
        return me ^ jnp.where(core == 0, self.mask(slot, 0), self.mask(slot, 1))


def owner(self, slot, other, me):
        core = me & 1
        if other:
            me, core = me ^ 1, 1 - core
        return me ^ jnp.where(core == 0, self.mask(slot, 0), self.mask(slot, 1))


ROWS = 4
UNITS = 2
PIECE = 64
F32 = jnp.float32
BF16 = jnp.bfloat16
VMEM_BYTES = 14 * 1024 * 1024


def group_sum(totals):
    channels = totals.shape[1]
    lane = lax.broadcasted_iota(jnp.int32, totals.shape, 1)
    span = 1
    while span < channels // GROUPS:
        up = pltpu.roll(totals, channels - span, 1)
        down = pltpu.roll(totals, span, 1)
        totals = totals + jnp.where((lane & span) == 0, up, down)
        span *= 2
    return totals


def fold(values):
    channels = values.shape[-1]
    return jnp.sum(values.reshape(-1, 8, channels), 0)


def total(partial):
    return jnp.sum(partial, 0, keepdims=True)


def sigmoid(v):
    return 0.5 * jnp.tanh(0.5 * v) + 0.5


def clear_edges(three):
    height = three.shape[1] - 2
    zero = jnp.zeros((3, 1) + three.shape[2:], three.dtype)
    three[:, 0:1] = zero
    three[:, height + 1 : height + 2] = zero


def store_three(three, row, value):
    width = value.shape[0]
    column = lax.broadcasted_iota(jnp.int32, value.shape, 0)
    left = jnp.where(column == 0, 0.0, pltpu.roll(value, 1, 0))
    right = jnp.where(column == width - 1, 0.0, pltpu.roll(value, width - 1, 0))
    three[0, row + 1] = left.astype(three.dtype)
    three[1, row + 1] = value.astype(three.dtype)
    three[2, row + 1] = right.astype(three.dtype)


def accumulators(body, *refs):
    groups = 4

    def run(*accs):
        accs = iter(accs)
        body(*refs, [[[next(accs) for _ in range(ROWS)] for _ in range(groups)] for _ in range(UNITS)])

    pl.run_scoped(run, *[pltpu.ACC(unit)((PIECE, 2 * LANES), F32) for unit in range(UNITS) for _ in range(groups * ROWS)])


def interleave(pieces, slots):
    return [pieces * (i + 1) // slots - pieces * i // slots for i in range(slots)]


def times(value, size):
    return value * size if isinstance(value, int) else pl.multiple_of(value * size, size)


def conv_step(accs, three, kernel, step, parity, back, others=()):
    others = list(others)
    for tap, share in enumerate(interleave(len(others), 9)):
        at = (8 - tap if back else tap) * three.shape[3]
        stage = (parity + tap) % 2
        for unit in range(UNITS):
            pltpu.matmul_push_rhs(kernel[at : at + three.shape[3], :], stage, unit, transpose=back)
        for piece in range(ROWS):
            for unit in range(UNITS):
                row = (UNITS * step + unit) * ROWS + piece + tap // 3
                pltpu.matmul_acc_lhs(
                    accs[unit][parity][piece], three[tap % 3, row], load_staged_rhs=stage if piece == 0 else None
                )
        for _ in range(share):
            others.pop(0)()


def conv_rows(accs, step, parity, use):
    def one(unit, piece):
        use((UNITS * step + unit) * ROWS + piece, pltpu.matmul_pop(accs[unit][parity][piece]))

    return [functools.partial(one, unit, piece) for unit in range(UNITS) for piece in range(ROWS)]


def conv_all(accs, three, kernel, back, use):
    steps = (three.shape[1] - 2) // (UNITS * ROWS)
    for step in range(steps):
        others = conv_rows(accs, step - 1, (step - 1) % 2, use) if step else ()
        conv_step(accs, three, kernel, step, step % 2, back, others)
    for other in conv_rows(accs, steps - 1, (steps - 1) % 2, use):
        other()


class Sums:
    def __init__(self, channels, count):
        self.values = [jnp.zeros((8, channels), F32)] * count

    def add(self, *values):
        self.values = [s + fold(v) for s, v in zip(self.values, values)]

    def totals(self):
        return [total(s) for s in self.values]


def store_turned(turned, padded, row):
    width, channels = padded.shape[1:]
    size = ROWS * width
    lanes = pl.ds(times(row // ROWS, size), size)
    turned[0, :, lanes] = padded[pl.ds(row + 1, ROWS)].reshape(size, channels).T
    turned[1, :, lanes] = padded[pl.ds(row, ROWS)].reshape(size, channels).T


def turn_end(turned, padded):
    height = padded.shape[0] - 2
    width, channels = padded.shape[1:]
    at = height * width
    turned[1, :, at : at + 2 * width] = padded[height : height + 2].reshape(2 * width, channels).T


def grad_step(accs, turned, three, work, stage, others=()):
    others = list(others)
    width, channels = three.shape[2:]
    size = ROWS * width
    for unit, column, chunk, _ in work:
        rhs = three[column, pl.ds(1 + times(chunk, ROWS), ROWS)].reshape(size, channels)
        pltpu.matmul_push_rhs(rhs, stage, unit)
    shares = iter(interleave(len(others), 3 * ROWS))
    for row in range(3):
        for piece in range(ROWS):
            for unit, _, chunk, groups in work:
                source, at = (0, times(chunk, size)) if row == 1 else (1, times(chunk, size) + row * width)
                lhs = turned[source, piece * PIECE : (piece + 1) * PIECE, pl.ds(at, size)]
                first = row == 0 and piece == 0
                pltpu.matmul_acc_lhs(accs[unit][groups[row]][piece], lhs, load_staged_rhs=stage if first else None)
            for _ in range(next(shares)):
                others.pop(0)()


def kernel_grad(accs, turned, three, flat, beside, carry):
    height, channels = three.shape[1] - 2, three.shape[3]
    chunks = height // ROWS

    def outer(i, carry):
        kept = [carry]

        def other(row):
            kept[0] = beside(row, kept[0])

        for k in range(4):
            chunk = 4 * i + k
            work = [(0, 0, chunk, (0, 1, 2)), (1, 2, chunk, (0, 1, 2))]
            others = [functools.partial(other, ROWS * chunk + j) for j in range(ROWS)] if beside else ()
            grad_step(accs, turned, three, work, k % 2, others)
        return kept[0]

    if beside:
        carry = lax.fori_loop(0, chunks // 4, outer, carry)
    else:
        for i in range(chunks // 4):
            outer(i, carry)

    def store(tap, piece, value):
        store_flat(flat, (tap * channels + piece * PIECE) * 2, value)

    def side(unit, column, row, piece):
        store(3 * row + 2 - column, piece, pltpu.matmul_pop(accs[unit][row][piece]))

    for row in range(2):
        for unit, column in ((0, 0), (1, 2)):
            for piece in range(ROWS):
                side(unit, column, row, piece)
    half = chunks // UNITS
    for chunk in range(half):
        work = [(unit, 1, unit * half + chunk, (3, 0, 1)) for unit in range(UNITS)]
        others = [functools.partial(side, unit, 2 * unit, 2, piece) for unit in range(UNITS) for piece in range(ROWS)]
        grad_step(accs, turned, three, work, chunk % 2, others if chunk == 0 else ())
    for row, group in enumerate((3, 0, 1)):
        for piece in range(ROWS):
            store(3 * row + 1, piece, pltpu.matmul_pop(accs[0][group][piece]) + pltpu.matmul_pop(accs[1][group][piece]))
    return carry


def store_flat(flat, start, value):
    rows = value.shape[0]
    flat[pl.ds(start, rows, stride=2), :] = value[:, :LANES]
    flat[pl.ds(start + 1, rows, stride=2), :] = value[:, LANES:]


def load_flat(flat, start, rows):
    left = flat[pl.ds(start, rows, stride=2), :]
    right = flat[pl.ds(start + 1, rows, stride=2), :]
    return jnp.concatenate([left, right], axis=1)


def stats_kernel(x_hbm, stats, x, arrived):
    height, width, channels = x.shape
    count = height * width * (channels // GROUPS)
    zero = jnp.zeros((8, channels), F32)
    parts = arrived.shape[0]
    rows = height // parts
    copies = [
        pltpu.make_async_copy(x_hbm.at[pl.ds(k * rows, rows)], x.at[pl.ds(k * rows, rows)], arrived.at[k])
        for k in range(parts)
    ]
    for copy in copies:
        copy.start()
    s = zero
    for k, copy in enumerate(copies):
        copy.wait()
        s = lax.fori_loop(0, rows // 4, lambda i, s, k=k: s + fold(x[pl.ds(k * rows + i * 4, 4)].astype(F32)), s)
    mean = group_sum(total(s)) / count

    def second(i, v):
        d = x[pl.ds(i * 4, 4)].astype(F32) - mean
        return v + fold(d * d)

    v = lax.fori_loop(0, height // 4, second, zero)
    inv = lax.rsqrt(group_sum(total(v)) / count + EPS)
    stats[0:1, :] = mean
    stats[1:2, :] = inv


def spread_kernel(g_hbm, three_hbm, g_sum, g, three, arrived, left):
    height, width, channels = g.shape
    parts = arrived.shape[0]
    rows = height // parts
    copies = [
        pltpu.make_async_copy(g_hbm.at[pl.ds(k * rows, rows)], g.at[pl.ds(k * rows, rows)], arrived.at[k])
        for k in range(parts)
    ]
    for copy in copies:
        copy.start()
    clear_edges(three)
    s = jnp.zeros((8, channels), F32)
    out = []
    for k, copy in enumerate(copies):
        copy.wait()

        def step(i, s, k=k):
            row = k * rows + i * 4
            values = g[pl.ds(row, 4)].astype(F32)
            for j in range(4):
                store_three(three, row + j, values[j])
            return s + fold(values)

        s = lax.fori_loop(0, rows // 4, step, s)
        start = k * rows + (1 if k else 0)
        size = rows + (1 if k == 0 else 0) + (1 if k == parts - 1 else 0)
        away = pltpu.make_async_copy(three.at[:, pl.ds(start, size)], three_hbm.at[:, pl.ds(start, size)], left.at[k])
        away.start()
        out.append(away)
    g_sum[...] = total(s)
    for away in out:
        away.wait()


def first_kernel(x, stats, vec, time, kernel, turned, raw, stats_out, three):
    accumulators(first_body, x, stats, vec, time, kernel, turned, raw, stats_out, three)


def first_body(x, stats, vec, time, kernel, turned, raw, stats_out, three, accs):
    height, width, channels = x.shape
    pixels = height * width
    per_group = channels // GROUPS
    mean, scale, shift = stats[0:1, :], stats[1:2, :] * vec[0:1, :], vec[1:2, :]
    offset = vec[2:3, :] + time[...]
    sums = Sums(channels, 2)
    pivot = []
    clear_edges(three)

    def activate(row):
        h = (x[row].astype(F32) - mean) * scale + shift
        store_three(three, row, h * sigmoid(h))
        if row % ROWS == ROWS - 1:
            store_turned(turned, three.at[1], row + 1 - ROWS)

    def use(row, v):
        if row == 0:
            pivot.append(total(fold(v)) / width)
        raw[row * width : (row + 1) * width, :] = v
        d = v - pivot[0]
        sums.add(d, d * d)

    per_step = UNITS * ROWS
    steps = height // per_step
    for row in range(per_step + 1):
        activate(row)
    for step in range(steps):
        ahead = range((step + 1) * per_step + 1, min((step + 2) * per_step + 1, height))
        others = [functools.partial(activate, row) for row in ahead]
        done = conv_rows(accs, step - 1, (step - 1) % 2, use) if step else []
        mixed = [f for i in range(per_step) for f in (*others[i : i + 1], *done[i : i + 1])]
        conv_step(accs, three, kernel, step, step % 2, False, mixed)
    turn_end(turned, three.at[1])
    for other in conv_rows(accs, steps - 1, (steps - 1) % 2, use):
        other()
    part, square = [v / pixels for v in sums.totals()]
    spread = square - part * part
    middle = pivot[0] + part + offset
    mean_two = group_sum(middle) / per_group
    away = middle - mean_two
    stats_out[0:1, :] = offset - mean_two
    stats_out[1:2, :] = lax.rsqrt(group_sum(spread + away * away) / per_group + EPS)


def second_kernel(g_three, raw, stats, vec, kernel, act, sums, flat, three, dc_sum, dh, turned):
    accumulators(second_body, g_three, raw, stats, vec, kernel, act, sums, flat, three, dc_sum, dh, turned)


def second_body(g_three, raw, stats, vec, kernel, act, sums, flat, three, dc_sum, dh, turned, accs):
    height, width, channels = act.shape[0] - 2, act.shape[1], act.shape[2]
    count = height * width * (channels // GROUPS)
    move, inv, gain, shift = stats[0:1, :], stats[1:2, :], vec[3:4, :], vec[4:5, :]
    scale = inv * gain
    both = Sums(channels, 2)
    act[0:1] = jnp.zeros((1, width, channels), BF16)
    act[height + 1 : height + 2] = jnp.zeros((1, width, channels), BF16)
    clear_edges(three)

    def use(row, v):
        at = slice(row * width, (row + 1) * width)
        c = raw[at, :] + move
        h = c * scale + shift
        sig = sigmoid(h)
        a = h * sig
        act[row + 1] = a.astype(BF16)
        d = v * (sig + a * (1.0 - sig))
        dh[at, :] = d
        both.add(d, d * c)
        if row % ROWS == ROWS - 1:
            store_turned(turned, act, row + 1 - ROWS)

    conv_all(accs, g_three, kernel, True, use)
    turn_end(turned, act)
    s, sc = both.totals()
    sn = sc * inv
    sums[0:1, :] = sn
    sums[1:2, :] = s
    base = inv * (group_sum(s * gain) / count)
    slope = inv * inv * (group_sum(sn * gain) / count)

    def back(row, dc):
        at = pl.ds(times(row, width), width)
        d = dh[at, :] * scale - base - (raw[at, :] + move) * slope
        store_three(three, row, d)
        return dc + fold(d)

    dc_sum[...] = total(kernel_grad(accs, turned, g_three, flat, back, jnp.zeros((8, channels), F32)))


def third_kernel(three, x, stats, vec, kernel, dh, sums):
    accumulators(third_body, three, x, stats, vec, kernel, dh, sums)


def third_body(three, x, stats, vec, kernel, dh, sums, accs):
    height, width, channels = x.shape
    mean, scale, shift = stats[0:1, :], stats[1:2, :] * vec[0:1, :], vec[1:2, :]
    both = Sums(channels, 2)

    def use(row, v):
        c = x[row].astype(F32) - mean
        h = c * scale + shift
        sig = sigmoid(h)
        d = v * (sig + h * sig * (1.0 - sig))
        dh[row * width : (row + 1) * width, :] = d
        both.add(d, d * c)

    conv_all(accs, three, kernel, True, use)
    s, sn = both.totals()
    sums[0:1, :] = sn * stats[1:2, :]
    sums[1:2, :] = s


def input_kernel(dh, x, g, stats, sums, vec, dc_sum, kernel, embedding, result, emb_grad, done):
    height, width, channels = x.shape
    count = height * width * (channels // GROUPS)
    mean, inv, gain = stats[0:1, :], stats[1:2, :], vec[0:1, :]
    scale = inv * gain
    base = inv * (group_sum(sums[1:2, :] * gain) / count)
    slope = inv * inv * (group_sum(sums[0:1, :] * gain) / count)

    def back(i, _):
        row = i * 4
        d = dh[pl.ds(row * width, 4 * width), :].reshape(4, width, channels)
        c = x[pl.ds(row, 4)].astype(F32) - mean
        result[pl.ds(row, 4)] = g[pl.ds(row, 4)].astype(F32) + (d * scale - base - c * slope)
        return 0

    lax.fori_loop(0, height // 4, back, 0)
    dq = lax.dot_general(
        dc_sum[...],
        kernel[9 * channels :, :].astype(F32),
        (((1,), (1,)), ((), ())),
        precision=lax.Precision.HIGHEST,
        preferred_element_type=F32,
    )
    emb = embedding[...].astype(F32)
    sig = sigmoid(emb)
    emb_grad[...] = dq * (sig * (1.0 + emb * (1.0 - sig)))
    done[...] = base


def last_kernel(part, parts, *refs):
    accumulators(functools.partial(last_body, part, parts), *refs)


def last_body(part, parts, act, x, vec, kernel, *refs):
    out, done, three, result, left, accs = refs[-6:]
    height = x.shape[0]
    rows = height // parts
    base = part * rows
    bias = vec[5:6, :]

    def spread(row):
        if 0 <= base + row < height:
            store_three(three, row, act[base + row + 1].astype(F32))
        else:
            three[:, row + 1 : row + 2] = jnp.zeros((3, 1) + three.shape[2:], BF16)

    def use(row, v):
        result[row] = (x[base + row].astype(F32) + v + bias).astype(BF16)

    per_step = UNITS * ROWS
    steps = rows // per_step
    copies = []

    def send(step):
        here = pl.ds(step * per_step, per_step)
        copies.append(pltpu.make_async_copy(result.at[here], out.at[pl.ds(base + step * per_step, per_step)], left.at[step]))
        copies[-1].start()

    for row in range(-1, per_step + 1):
        spread(row)
    for step in range(steps):
        ahead = range((step + 1) * per_step + 1, min((step + 2) * per_step, rows) + 1)
        others = [functools.partial(spread, row) for row in ahead]
        done_rows = conv_rows(accs, step - 1, (step - 1) % 2, use) if step else []
        mixed = [f for i in range(per_step) for f in (*others[i : i + 1], *done_rows[i : i + 1])]
        conv_step(accs, three, kernel, step, step % 2, False, mixed)
        if step:
            send(step - 1)
    for other in conv_rows(accs, steps - 1, (steps - 1) % 2, use):
        other()
    send(steps - 1)
    done[...] = bias
    for copy in copies:
        copy.wait()


def join_kernel(mine, got, out, tail=VEC_ROWS):
    rows = mine.shape[0] - tail
    out[0:rows, :] = mine[0:rows, :]
    out[rows : 2 * rows, :] = got[0:rows, :]
    if tail:
        out[2 * rows :, :] = mine[rows:, :] + got[rows:, :]


def join_second_kernel(mine, got, out, mark):
    join_kernel(mine, got, out, 0)
    mark[...] = jnp.zeros_like(mark)


def part_kernel(cuts, mine, got, first, second):
    block, cut = sum(cuts), sum(cuts[:-1])
    slots = (mine.shape[0] - VEC_ROWS) // block
    for half, source in enumerate((mine, got)):
        for slot in range(slots):
            at, to = slot * block, half * slots + slot
            first[to * cut : (to + 1) * cut, :] = source[at : at + cut, :]
            second[to * cuts[-1] : (to + 1) * cuts[-1], :] = source[at + cut : at + block, :]
    first[2 * slots * cut :, :] = mine[slots * block :, :] + got[slots * block :, :]


def halve_kernel(keep, got, send_next, keep_next, tail=VEC_ROWS):
    rows = (keep.shape[0] - tail) // 2
    keep_next[0:rows, :] = keep[0:rows, :] + got[0:rows, :].astype(F32)
    send_next[0:rows, :] = (keep[rows : 2 * rows, :] + got[rows : 2 * rows, :].astype(F32)).astype(BF16)
    if tail:
        vec = keep[2 * rows :, :] + got[2 * rows :, :].astype(F32)
        keep_next[rows:, :] = vec
        send_next[rows:, :] = vec.astype(BF16)


def halve_second_kernel(keep, got, send_next, keep_next):
    halve_kernel(keep, got, send_next, keep_next, 0)


def merge_kernel(wide, narrow, one, one_got, two, two_got, send, keep):
    slots = two.shape[0] // narrow // 2
    for slot in range(slots):
        to = slot * (wide + narrow)
        for mine, got, rows in ((one, one_got, wide), (two, two_got, narrow)):
            at, up = slot * rows, (slots + slot) * rows
            keep[to : to + rows, :] = mine[at : at + rows, :] + got[at : at + rows, :].astype(F32)
            send[to : to + rows, :] = (mine[up : up + rows, :] + got[up : up + rows, :].astype(F32)).astype(BF16)
            to += rows
    at, to = 2 * slots * wide, slots * (wide + narrow)
    values = one[at:, :] + one_got[at:, :].astype(F32)
    keep[to:, :] = values
    send[to:, :] = values.astype(BF16)


def place_blocks(wires, cuts, mine, got, flats):
    me = wires.me()
    block = sum(cuts)
    for slot in range(wires.slots):
        for other, source in ((False, mine), (True, got)):
            owner = wires.owner(slot, other, me)
            values = source[slot * block : (slot + 1) * block, :].astype(F32)
            at = 0
            for flat, rows in zip(flats, cuts):
                flat[pl.ds(pl.multiple_of(owner * rows, rows), rows), :] = values[at : at + rows]
                at += rows


def unflatten(flat, out, base):
    for start in range(0, flat.shape[0] // 2, 256):
        out[base + start : base + start + 256, :] = load_flat(flat, 2 * start, 256).astype(BF16)


def arrange_first_kernel(wires, cuts, mine, got, embedding, first, vec, time, flat_one, flat_project, flat_vec):
    place_blocks(wires, cuts, mine, got, (flat_one, flat_project))
    rows_one = flat_one.shape[0] // 2
    unflatten(flat_project, first, rows_one)
    emb = embedding[...].astype(F32)
    act = (emb * sigmoid(emb)).astype(BF16)
    time[...] = jnp.dot(act, first[rows_one:, :], preferred_element_type=F32)
    unflatten(flat_one, first, 0)
    at = wires.slots * sum(cuts)
    flat_vec[...] = mine[at : at + VEC_ROWS, :].astype(F32) + got[at : at + VEC_ROWS, :].astype(F32)
    vec[...] = load_flat(flat_vec, 0, VEC_ROWS // 2)


def arrange_second_kernel(wires, cuts, mine, got, second, flat_two):
    place_blocks(wires, cuts, mine, got, (flat_two,))
    unflatten(flat_two, second, 0)


def grad_kernel(turned, three, flat):
    accumulators(lambda *refs: kernel_grad(refs[-1], *refs[:-1], None, 0), turned, three, flat)


def take_blocks(wires, cuts, flats, send, keep):
    me = wires.me()
    block = sum(cuts)
    for slot in range(wires.slots):
        for other in (True, False):
            owner = wires.owner(slot, other, me)
            at = slot * block
            for flat, rows in zip(flats, cuts):
                values = flat[pl.ds(pl.multiple_of(owner * rows, rows), rows), :]
                if other:
                    send[at : at + rows, :] = values.astype(BF16)
                else:
                    keep[at : at + rows, :] = values
                at += rows


def pack_first_kernel(
    wires, cuts, flat_one, dc_sum, sums_one, sums_two, g_sum, two, two_got, send, keep, two_send, two_keep
):
    halve_kernel(two, two_got, two_send, two_keep, 0)
    take_blocks(wires, cuts, (flat_one,), send, keep)
    at = wires.slots * sum(cuts)
    vectors = [sums_one[0:1, :], sums_one[1:2, :], dc_sum[...], sums_two[0:1, :], sums_two[1:2, :], g_sum[...]]
    halves = [row[:, i * LANES : (i + 1) * LANES] for row in vectors for i in range(2)]
    values = jnp.concatenate(halves + [jnp.zeros((VEC_ROWS - len(halves), LANES), F32)], axis=0)
    keep[at : at + VEC_ROWS, :] = values
    send[at : at + VEC_ROWS, :] = values.astype(BF16)


def pack_second_kernel(wires, cuts, flat_two, embedding, dc_sum, send, keep, flat_project):
    emb = embedding[...].astype(F32)
    q = (emb * sigmoid(emb)).astype(BF16).astype(F32)
    q = jnp.broadcast_to(q, (LANES, q.shape[1])).T
    dc = dc_sum[...]
    store_flat(flat_project, 0, jnp.concatenate([q * dc[:, :LANES], q * dc[:, LANES:]], axis=1))
    take_blocks(wires, cuts, (flat_two, flat_project), send, keep)


def finish_kernel(wires, cuts, n_vec, keep, got, one, two, project, vec):
    at = 0
    for out, rows in zip((one, two, project), cuts):
        out[...] = keep[at : at + rows, :] + got[at : at + rows, :].astype(F32)
        at += rows
    vectors = keep[at : at + VEC_ROWS, :] + got[at : at + VEC_ROWS, :].astype(F32)
    start = wires.me() * n_vec
    row, lane = start // LANES, start % LANES
    place = lax.broadcasted_iota(jnp.int32, vectors.shape, 0)
    own = jnp.sum(jnp.where(place == row, vectors, 0.0), 0, keepdims=True)
    following = jnp.sum(jnp.where(place == row + 1, vectors, 0.0), 0, keepdims=True)
    column = lax.broadcasted_iota(jnp.int32, own.shape, 1)
    shifted = pltpu.roll(jnp.where(column >= lane, own, following), (LANES - lane) % LANES, 1)
    vec[...] = shifted[:, :n_vec]


def call(body, outs, *args, scratch=(), flops=0, size=4 << 20, after=(), far=(), far_outs=(), semaphores=(), same=None):
    held, n_in = len(after), len(args)

    def run(*refs):
        body(*refs[:n_in], *refs[n_in + held :])

    args = [pltpu.with_memory_space_constraint(v, pltpu.HBM) if i in far else v for i, v in enumerate(args)]

    def spec(is_far):
        return pl.BlockSpec(memory_space=pltpu.HBM if is_far else pltpu.VMEM)

    return pl.pallas_call(
        run,
        out_shape=[
            pltpu.HBM(shape, dtype) if i in far_outs else jax.ShapeDtypeStruct(shape, dtype)
            for i, (shape, dtype) in enumerate(outs)
        ],
        in_specs=[spec(i in far) for i in range(n_in)] + [pl.BlockSpec(memory_space=pl.ANY)] * held,
        out_specs=[spec(i in far_outs) for i in range(len(outs))],
        scratch_shapes=[pltpu.VMEM(shape, dtype) for shape, dtype in scratch]
        + [pltpu.SemaphoreType.DMA((n,)) for n in semaphores],
        input_output_aliases=same or {},
        compiler_params=pltpu.CompilerParams(vmem_limit_bytes=VMEM_BYTES),
        cost_estimate=pl.CostEstimate(flops=0, bytes_accessed=0, transcendentals=0),
    )(*args, *after)


def joined(held, tail=VEC_ROWS):
    return ((2 * (held.shape[0] - tail) + tail, LANES), BF16)


def gather_start(wires, cuts, held, beside):
    last = wires.stages - 1
    for stage in range(last - 1):
        after = beside.get(stage, ())
        held, = call(join_kernel, [joined(held)], held, wires.swap(held, stage), after=after)
    got = wires.swap(held, last - 1)
    slots = wires.slots // 2
    shapes = [(slots * sum(cuts[:-1]) + VEC_ROWS, LANES), (slots * cuts[-1], LANES)]
    outs = [(shape, BF16) for shape in shapes]
    first, second = call(functools.partial(part_kernel, cuts), outs, held, got, after=beside.get(last - 1, ()))
    first_got, second_got = wires.swap(first, last), wires.swap(second, last)
    first, = call(join_kernel, [joined(first)], first, first_got, after=beside.get(last, ()))
    second, mark = call(join_second_kernel, [joined(second, 0), ((1, LANES), F32)], second, second_got)
    return first, wires.swap(first, wires.stages), second, wires.swap(second, wires.stages), mark


def in_order(wires, cuts, mine, got):
    block = sum(cuts)
    rows = wires.slots * block
    both = jnp.concatenate([mine[:rows], got[:rows]]).reshape(wires.n, block, LANES)
    me = wires.me()
    owners = jnp.stack([wires.owner(j, other, me) for other in (False, True) for j in range(wires.slots)])
    both = jnp.zeros_like(both).at[owners].set(both)
    ends = [sum(cuts[:i]) for i in range(len(cuts) + 1)]
    return [both[:, a:b].reshape(-1, 2 * LANES) for a, b in zip(ends, ends[1:])]


def arrange_first(wires, cuts, mine, got, embedding, after):
    channels = 2 * LANES
    totals = [wires.n * rows for rows in cuts]
    if all(rows % 8 == 0 for rows in cuts):
        return call(
            functools.partial(arrange_first_kernel, wires, cuts),
            [((sum(totals) // 2, channels), BF16), ((VEC_ROWS // 2, channels), F32), ((1, channels), F32)],
            mine,
            got,
            embedding,
            scratch=[((rows, LANES), F32) for rows in (*totals, VEC_ROWS)],
            after=after,
        )
    one, project = in_order(wires, cuts, mine, got)
    vec = (mine[-VEC_ROWS:].astype(F32) + got[-VEC_ROWS:].astype(F32)).reshape(VEC_ROWS // 2, channels)
    act = jax.nn.silu(embedding.astype(F32)).astype(BF16)
    return jnp.concatenate([one, project]), vec, jnp.dot(act, project, preferred_element_type=F32)


def arrange_second(wires, cuts, mine, got, after):
    rows = wires.n * cuts[0]
    if cuts[0] % 8 == 0:
        body = functools.partial(arrange_second_kernel, wires, cuts)
        return call(body, [((rows // 2, 2 * LANES), BF16)], mine, got, scratch=[((rows, LANES), F32)], after=after)[0]
    return in_order(wires, cuts, mine, got)[0]


def out_of_order(wires, cuts, parts, tail):
    me = wires.me()
    blocks = jnp.concatenate([v.reshape(wires.n, rows, LANES) for v, rows in zip(parts, cuts)], axis=1)
    halves = []
    for other in (True, False):
        owners = jnp.stack([wires.owner(j, other, me) for j in range(wires.slots)])
        halves.append(jnp.concatenate([blocks[owners].reshape(-1, LANES), tail]))
    return halves[0].astype(BF16), halves[1]


def pack_first(wires, cuts, flat_one, dc_sum, sums_one, sums_two, g_sum, two, two_got):
    shape = (wires.slots * sum(cuts) + VEC_ROWS, LANES)
    if all(rows % 8 == 0 for rows in cuts):
        return call(
            functools.partial(pack_first_kernel, wires, cuts),
            [(shape, BF16), (shape, F32), *halved(two, 0)],
            flat_one,
            dc_sum,
            sums_one,
            sums_two,
            g_sum,
            two,
            two_got,
        )
    vec = jnp.concatenate([sums_one, dc_sum, sums_two, g_sum]).reshape(-1, LANES)
    vec = jnp.pad(vec, ((0, VEC_ROWS - vec.shape[0]), (0, 0)))
    send, keep = out_of_order(wires, cuts, (flat_one,), vec)
    return send, keep, *call(halve_second_kernel, halved(two, 0), two, two_got)


def pack_second(wires, cuts, flat_two, embedding, dc_sum):
    if all(rows % 8 == 0 for rows in cuts):
        shape = (wires.slots * sum(cuts), LANES)
        return call(
            functools.partial(pack_second_kernel, wires, cuts),
            [(shape, BF16), (shape, F32)],
            flat_two,
            embedding,
            dc_sum,
            scratch=[((wires.n * cuts[1], LANES), F32)],
        )
    q = jax.nn.silu(embedding.astype(F32)).astype(BF16).astype(F32).reshape(-1, 1)
    parts = (flat_two, (q * dc_sum).reshape(-1, LANES))
    return out_of_order(wires, cuts, parts, jnp.zeros((0, LANES), F32))


def halved(keep, tail=VEC_ROWS):
    shape = ((keep.shape[0] - tail) // 2 + tail, LANES)
    return [(shape, BF16), (shape, F32)]


def local(sizes, images, embedding, conv_first, conv_second, projection, vectors, cotangent):
    count, height, width, channels = images.shape
    emb_width = embedding.shape[-1]
    wires = Wires(*sizes)
    n_vec = vectors.shape[0]
    assert count == 1 and channels == 2 * LANES and n_vec <= LANES
    cuts = [v.shape[0] // LANES for v in (conv_first, conv_second, projection)]
    pixels = height * width
    three = ((3, height + 2, width, channels), BF16)
    maps = ((height, width, channels), BF16)
    flat = ((pixels, channels), F32)
    line = ((1, channels), F32)
    pair = ((2, channels), F32)
    taps = ((18 * channels, LANES), F32)
    padded = ((height + 2, width, channels), BF16)
    turned = ((2, channels, pixels + 2 * width), BF16)
    conv_flops = 2 * 9 * pixels * channels * channels

    x, g = images[0], cotangent[0]
    stats, x_near = call(stats_kernel, [pair, maps], x, far=(0,), semaphores=(4,))
    g_three, g_sum = call(
        spread_kernel, [three, line], g, scratch=[maps, three], far=(0,), far_outs=(0,), semaphores=(4, 4)
    )
    wide = VEC_ROWS * LANES
    placed = lax.dynamic_slice(jnp.pad(vectors, (wide, wide - n_vec)), (wide - wires.me() * n_vec,), (wide,))
    start = jnp.concatenate([v.reshape(-1, LANES) for v in (conv_first, projection, conv_second, placed)])
    beside = {wires.stages - 2: (g_sum,), wires.stages - 1: (stats,)}
    one, one_got, two, two_got, mark = gather_start(wires, (cuts[0], cuts[2], cuts[1]), start, beside)
    first, vec, time = arrange_first(wires, (cuts[0], cuts[2]), one, one_got, embedding, (mark,))

    turned_one, raw, stats_two = call(
        first_kernel, [turned, flat, pair], x_near, stats, vec, time, first, scratch=[three], flops=conv_flops
    )
    kernel_two = arrange_second(wires, cuts[1:2], two, two_got, (stats_two,))
    act_two, sums_two, grad_two, e_three, dc_sum = call(
        second_kernel,
        [padded, pair, taps, three, line],
        g_three,
        raw,
        stats_two,
        vec,
        kernel_two,
        scratch=[flat, turned],
        flops=2 * conv_flops,
    )
    last = wires.stages
    two_send, two = pack_second(wires, cuts[1:], grad_two, embedding, dc_sum)
    two_got = wires.swap(two_send, last)
    dh_one, sums_one = call(third_kernel, [flat, pair], e_three, x_near, stats, vec, first, flops=conv_flops)
    grad_one, = call(grad_kernel, [taps], turned_one, e_three, flops=conv_flops)
    one_send, one, two_send, two = pack_first(
        wires, cuts[:1], grad_one, dc_sum, sums_one, sums_two, g_sum, two, two_got
    )
    input_grad, embedding_grad, input_done = call(
        input_kernel,
        [(maps[0], F32), ((1, emb_width), F32), line],
        dh_one,
        x,
        g,
        stats,
        sums_one,
        vec,
        dc_sum,
        first,
        embedding,
    )
    parts = 2
    rows = height // parts
    output, output_done = (), []
    for part in range(parts):
        *output, done = call(
            functools.partial(last_kernel, part, parts),
            [maps, line],
            act_two,
            x_near,
            vec,
            kernel_two,
            *output,
            scratch=[((3, rows + 2, width, channels), BF16), ((rows, width, channels), BF16)],
            far=(4,),
            far_outs=(0,),
            semaphores=(rows // (UNITS * ROWS),),
            same={4: 0} if output else None,
            flops=conv_flops // parts,
        )
        output_done.append(done)
    two_got = wires.swap(two_send, last - 1)
    one_send, one = call(halve_kernel, halved(one), one, wires.swap(one_send, last))
    one_got = wires.swap(one_send, last - 1)
    wide, narrow = cuts[0], sum(cuts[1:])
    shape = (wires.slots // 4 * (wide + narrow) + VEC_ROWS, LANES)
    send, keep = call(
        functools.partial(merge_kernel, wide, narrow),
        [(shape, BF16), (shape, F32)],
        one,
        one_got,
        two,
        two_got,
        after=output_done[:1],
    )
    for stage in range(last - 2, 0, -1):
        after = {last - 3: (input_done,), last - 2: (output_done[1],)}.get(stage, ())
        send, keep = call(halve_kernel, halved(keep), keep, wires.swap(send, stage), after=after)
    summed = call(
        functools.partial(finish_kernel, wires, cuts, n_vec),
        [*[((rows, LANES), F32) for rows in cuts], ((1, n_vec), F32)],
        keep,
        wires.swap(send, 0),
    )
    return (output[0][None], input_grad[None], embedding_grad, *[v.reshape(-1) for v in summed])


def solution(mesh):
    sizes = (mesh.shape["dp"], mesh.shape["fsdp"])
    split = P(AXES)
    maps = P(AXES, None, None, None)
    in_specs = (maps, P(AXES, None), split, split, split, split, maps)
    out_specs = (maps, maps, P(AXES, None), split, split, split, split)

    def body(*args):
        return local(sizes, *args)

    return jax.shard_map(body, mesh=mesh, in_specs=in_specs, out_specs=out_specs, check_vma=False)
```

```python
import functools
import math

import jax
import jax.numpy as jnp
from jax import lax
from jax.experimental import pallas as pl
from jax.experimental.pallas import tpu as pltpu
from jax.sharding import PartitionSpec as P

GROUPS = 32
EPS = 1e-05
AXES = ("dp", "fsdp")
LANES = 128
VEC_ROWS = 16


class Wires:
    def __init__(self, n_dp, n_fsdp):
        self.n_fsdp = n_fsdp
        self.n = n_dp * n_fsdp
        self.bits = int(math.log2(self.n))
        fsdp_bits = int(math.log2(n_fsdp))
        assert 1 << self.bits == self.n and 1 << fsdp_bits == n_fsdp and fsdp_bits >= 3 and n_dp >= 2
        a, b = 1, fsdp_bits
        far = [bit for bit in range(self.bits - 1, 0, -1) if bit not in (a, b)]
        self.order = {0: [*far, a, b], 1: [*far[::-1], b, a]}
        self.stages = self.bits - 1
        self.slots = 1 << self.stages

    def swap(self, value, stage):
        def bit(core):
            return 0 if stage == self.stages else self.order[core][stage]

        return lax.ppermute(value, AXES, [(i, i ^ (1 << bit(i & 1))) for i in range(self.n)])

    def mask(self, slot, core):
        return sum(1 << self.order[core][i] for i in range(self.stages) if slot >> i & 1)

    def me(self):
        return lax.axis_index("dp") * self.n_fsdp + lax.axis_index("fsdp")

    def owner(self, slot, other, me):
        core = me & 1
        if other:
            me, core = me ^ 1, 1 - core
        return me ^ jnp.where(core == 0, self.mask(slot, 0), self.mask(slot, 1))


def owner(self, slot, other, me):
        core = me & 1
        if other:
            me, core = me ^ 1, 1 - core
        return me ^ jnp.where(core == 0, self.mask(slot, 0), self.mask(slot, 1))


ROWS = 4
UNITS = 2
PIECE = 64
F32 = jnp.float32
BF16 = jnp.bfloat16
VMEM_BYTES = 15 * 1024 * 1024


def group_sum(totals):
    channels = totals.shape[1]
    lane = lax.broadcasted_iota(jnp.int32, totals.shape, 1)
    span = 1
    while span < channels // GROUPS:
        up = pltpu.roll(totals, channels - span, 1)
        down = pltpu.roll(totals, span, 1)
        totals = totals + jnp.where((lane & span) == 0, up, down)
        span *= 2
    return totals


def fold(values):
    channels = values.shape[-1]
    return jnp.sum(values.reshape(-1, 8, channels), 0)


def total(partial):
    return jnp.sum(partial, 0, keepdims=True)


def sigmoid(v):
    return 0.5 * jnp.tanh(0.5 * v) + 0.5


def clear_edges(three):
    height = three.shape[1] - 2
    zero = jnp.zeros((3, 1) + three.shape[2:], three.dtype)
    three[:, 0:1] = zero
    three[:, height + 1 : height + 2] = zero


def store_three(three, row, value):
    width = value.shape[0]
    column = lax.broadcasted_iota(jnp.int32, (8, value.shape[1]), 0)
    left = pltpu.roll(value, 1, 0)
    left = jnp.concatenate([jnp.where(column == 0, 0.0, left[:8]), left[8:]], axis=0)
    right = pltpu.roll(value, width - 1, 0)
    right = jnp.concatenate([right[: width - 8], jnp.where(column == 7, 0.0, right[width - 8 :])], axis=0)
    three[0, row + 1] = left.astype(three.dtype)
    three[1, row + 1] = value.astype(three.dtype)
    three[2, row + 1] = right.astype(three.dtype)


def accumulators(body, *refs):
    groups = 4

    def run(*accs):
        accs = iter(accs)
        body(*refs, [[[next(accs) for _ in range(ROWS)] for _ in range(groups)] for _ in range(UNITS)])

    pl.run_scoped(run, *[pltpu.ACC(unit)((PIECE, 2 * LANES), F32) for unit in range(UNITS) for _ in range(groups * ROWS)])


def interleave(pieces, slots):
    return [pieces * (i + 1) // slots - pieces * i // slots for i in range(slots)]


def times(value, size):
    return value * size if isinstance(value, int) else pl.multiple_of(value * size, size)


def conv_step(accs, three, kernel, step, parity, back, others=()):
    others = list(others)
    for tap, share in enumerate(interleave(len(others), 9)):
        at = (8 - tap if back else tap) * three.shape[3]
        stage = (parity + tap) % 2
        for unit in range(UNITS):
            pltpu.matmul_push_rhs(kernel[at : at + three.shape[3], :], stage, unit, transpose=back)
        for piece in range(ROWS):
            for unit in range(UNITS):
                row = (UNITS * step + unit) * ROWS + piece + tap // 3
                pltpu.matmul_acc_lhs(
                    accs[unit][parity][piece], three[tap % 3, row], load_staged_rhs=stage if piece == 0 else None
                )
        for _ in range(share):
            others.pop(0)()


def conv_rows(accs, step, parity, use):
    def one(unit, piece):
        use((UNITS * step + unit) * ROWS + piece, pltpu.matmul_pop(accs[unit][parity][piece]))

    return [functools.partial(one, unit, piece) for unit in range(UNITS) for piece in range(ROWS)]


def conv_all(accs, three, kernel, back, use):
    steps = (three.shape[1] - 2) // (UNITS * ROWS)
    for step in range(steps):
        others = conv_rows(accs, step - 1, (step - 1) % 2, use) if step else ()
        conv_step(accs, three, kernel, step, step % 2, back, others)
    assert steps % 2 == 0
    return conv_rows(accs, steps - 1, 1, use)


class Sums:
    def __init__(self, channels, count):
        self.values = [jnp.zeros((8, channels), F32)] * count

    def add(self, *values):
        self.values = [s + fold(v) for s, v in zip(self.values, values)]

    def totals(self):
        return [total(s) for s in self.values]


def store_turned(turned, padded, row):
    width, channels = padded.shape[1:]
    size = ROWS * width
    lanes = pl.ds(times(row // ROWS, size), size)
    turned[0, :, lanes] = padded[pl.ds(row + 1, ROWS)].reshape(size, channels).T
    turned[1, :, lanes] = padded[pl.ds(row, ROWS)].reshape(size, channels).T


def turn_end(turned, padded):
    height = padded.shape[0] - 2
    width, channels = padded.shape[1:]
    at = height * width
    turned[1, :, at : at + 2 * width] = padded[height : height + 2].reshape(2 * width, channels).T


def grad_step(accs, turned, three, work, stage, others=()):
    others = list(others)
    width, channels = three.shape[2:]
    size = ROWS * width
    for unit, column, chunk, _ in work:
        rhs = three[column, pl.ds(1 + times(chunk, ROWS), ROWS)].reshape(size, channels)
        pltpu.matmul_push_rhs(rhs, stage, unit)
    shares = iter(interleave(len(others), 3 * ROWS))
    for row in range(3):
        for piece in range(ROWS):
            for unit, _, chunk, groups in work:
                source, at = (0, times(chunk, size)) if row == 1 else (1, times(chunk, size) + row * width)
                lhs = turned[source, piece * PIECE : (piece + 1) * PIECE, pl.ds(at, size)]
                first = row == 0 and piece == 0
                pltpu.matmul_acc_lhs(accs[unit][groups[row]][piece], lhs, load_staged_rhs=stage if first else None)
            for _ in range(next(shares)):
                others.pop(0)()


def kernel_grad(accs, turned, three, flat, first, more):
    height, channels = three.shape[1] - 2, three.shape[3]
    chunks = height // ROWS
    lead, step = 4, 4
    outer_groups, inner_groups = (0, 2, 3), (1, 0, 2)

    def sides(chunk, stage, others):
        work = [(0, 0, chunk, outer_groups), (1, 2, chunk, outer_groups)]
        grad_step(accs, turned, three, work, stage, others)

    first = list(first)
    for chunk, share in enumerate(interleave(len(first), lead)):
        sides(chunk, chunk % 2, [first.pop(0) for _ in range(share)])
    beside, carry = more() or (None, 0)
    kept = [carry]

    def other(row):
        kept[0] = beside(row, kept[0])

    def loop(i, carry):
        kept[0] = carry
        for k in range(step):
            at = step * i + k
            sides(lead + at, k % 2, [functools.partial(other, ROWS * at + j) for j in range(ROWS)] if beside else ())
        return kept[0]

    if beside:
        kept[0] = lax.fori_loop(0, (chunks - lead) // step, loop, carry)
    else:
        for i in range((chunks - lead) // step):
            loop(i, carry)

    def store(tap, piece, value):
        store_flat(flat, (tap * channels + piece * PIECE) * 2, value)

    def side(unit, row, piece):
        store(3 * row + 2 - 2 * unit, piece, pltpu.matmul_pop(accs[unit][outer_groups[row]][piece]))

    for row in range(2):
        for unit in range(UNITS):
            for piece in range(ROWS):
                side(unit, row, piece)
    half = chunks // UNITS
    rest = [functools.partial(other, row) for row in range(ROWS * (chunks - lead), height)] if beside else []
    for chunk, share in enumerate(interleave(len(rest), half)):
        work = [(unit, 1, unit * half + chunk, inner_groups) for unit in range(UNITS)]
        others = [functools.partial(side, unit, 2, piece) for unit in range(UNITS) for piece in range(ROWS)]
        more_rows = [rest.pop(0) for _ in range(share)]
        grad_step(accs, turned, three, work, chunk % 2, (others if chunk == 0 else []) + more_rows)
    for row, group in enumerate(inner_groups):
        for piece in range(ROWS):
            store(3 * row + 1, piece, pltpu.matmul_pop(accs[0][group][piece]) + pltpu.matmul_pop(accs[1][group][piece]))
    return kept[0]


def store_flat(flat, start, value):
    rows = value.shape[0]
    flat[pl.ds(start, rows, stride=2), :] = value[:, :LANES]
    flat[pl.ds(start + 1, rows, stride=2), :] = value[:, LANES:]


def load_flat(flat, start, rows):
    left = flat[pl.ds(start, rows, stride=2), :]
    right = flat[pl.ds(start + 1, rows, stride=2), :]
    return jnp.concatenate([left, right], axis=1)


def stats_kernel(x_hbm, stats, x, arrived):
    height, width, channels = x.shape
    count = height * width * (channels // GROUPS)
    zero = jnp.zeros((8, channels), F32)
    parts = arrived.shape[0]
    rows = height // parts
    copies = [
        pltpu.make_async_copy(x_hbm.at[pl.ds(k * rows, rows)], x.at[pl.ds(k * rows, rows)], arrived.at[k])
        for k in range(parts)
    ]
    for copy in copies:
        copy.start()
    s = zero
    for k, copy in enumerate(copies):
        copy.wait()
        s = lax.fori_loop(0, rows // 4, lambda i, s, k=k: s + fold(x[pl.ds(k * rows + i * 4, 4)].astype(F32)), s)
    mean = group_sum(total(s)) / count

    def second(i, v):
        d = x[pl.ds(i * 4, 4)].astype(F32) - mean
        return v + fold(d * d)

    v = lax.fori_loop(0, height // 4, second, zero)
    inv = lax.rsqrt(group_sum(total(v)) / count + EPS)
    stats[0:1, :] = mean
    stats[1:2, :] = inv


def spread_kernel(g_hbm, three_hbm, g_sum, g, three, arrived, left):
    height, width, channels = g.shape
    parts = arrived.shape[0]
    rows = height // parts
    copies = [
        pltpu.make_async_copy(g_hbm.at[pl.ds(k * rows, rows)], g.at[pl.ds(k * rows, rows)], arrived.at[k])
        for k in range(parts)
    ]
    for copy in copies:
        copy.start()
    clear_edges(three)
    s = jnp.zeros((8, channels), F32)
    out = []
    for k, copy in enumerate(copies):
        copy.wait()

        def step(i, s, k=k):
            row = k * rows + i * 4
            values = g[pl.ds(row, 4)].astype(F32)
            for j in range(4):
                store_three(three, row + j, values[j])
            return s + fold(values)

        s = lax.fori_loop(0, rows // 4, step, s)
        start = k * rows + (1 if k else 0)
        size = rows + (1 if k == 0 else 0) + (1 if k == parts - 1 else 0)
        away = pltpu.make_async_copy(three.at[:, pl.ds(start, size)], three_hbm.at[:, pl.ds(start, size)], left.at[k])
        away.start()
        out.append(away)
    g_sum[...] = total(s)
    for away in out:
        away.wait()


def first_kernel(x, stats, vec, time, kernel, turned, raw, stats_out, three):
    accumulators(first_body, x, stats, vec, time, kernel, turned, raw, stats_out, three)


def first_body(x, stats, vec, time, kernel, turned, raw, stats_out, three, accs):
    height, width, channels = x.shape
    pixels = height * width
    per_group = channels // GROUPS
    mean, scale, shift = stats[0:1, :], 0.5 * stats[1:2, :] * vec[0:1, :], 0.5 * vec[1:2, :]
    offset = vec[2:3, :] + time[...]
    sums = Sums(channels, 2)
    pivot = []
    clear_edges(three)

    def activate(row):
        half = (x[row].astype(F32) - mean) * scale + shift
        store_three(three, row, half * (1.0 + jnp.tanh(half)))
        if row % ROWS == ROWS - 1:
            store_turned(turned, three.at[1], row + 1 - ROWS)

    def use(row, v):
        if row == 0:
            pivot.append(total(fold(v)) / width)
        raw[row * width : (row + 1) * width, :] = v
        d = v - pivot[0]
        sums.add(d, d * d)

    per_step = UNITS * ROWS
    steps = height // per_step
    for row in range(per_step + 1):
        activate(row)
    for step in range(steps):
        ahead = range((step + 1) * per_step + 1, min((step + 2) * per_step + 1, height))
        others = [functools.partial(activate, row) for row in ahead]
        done = conv_rows(accs, step - 1, (step - 1) % 2, use) if step else []
        mixed = [f for i in range(per_step) for f in (*others[i : i + 1], *done[i : i + 1])]
        conv_step(accs, three, kernel, step, step % 2, False, mixed)
    turn_end(turned, three.at[1])
    for other in conv_rows(accs, steps - 1, (steps - 1) % 2, use):
        other()
    part, square = [v / pixels for v in sums.totals()]
    spread = square - part * part
    middle = pivot[0] + part + offset
    mean_two = group_sum(middle) / per_group
    away = middle - mean_two
    stats_out[0:1, :] = offset - mean_two
    stats_out[1:2, :] = lax.rsqrt(group_sum(spread + away * away) / per_group + EPS)


def second_kernel(g_three, raw, stats, vec, kernel, act, sums, flat, three, dc_sum, dh, turned):
    accumulators(second_body, g_three, raw, stats, vec, kernel, act, sums, flat, three, dc_sum, dh, turned)


def second_body(g_three, raw, stats, vec, kernel, act, sums, flat, three, dc_sum, dh, turned, accs):
    height, width, channels = act.shape[0] - 2, act.shape[1], act.shape[2]
    count = height * width * (channels // GROUPS)
    move, inv, gain, shift = stats[0:1, :], stats[1:2, :], vec[3:4, :], vec[4:5, :]
    scale, shift = 0.5 * inv * gain, 0.5 * shift
    both = Sums(channels, 2)
    act[0:1] = jnp.zeros((1, width, channels), BF16)
    act[height + 1 : height + 2] = jnp.zeros((1, width, channels), BF16)
    clear_edges(three)

    def use(row, v):
        at = slice(row * width, (row + 1) * width)
        c = raw[at, :] + move
        half = c * scale + shift
        t = jnp.tanh(half)
        u = 1.0 + t
        a = half * u
        act[row + 1] = a.astype(BF16)
        d = v * (u + a * (1.0 - t))
        dh[at, :] = d
        both.add(d, d * c)
        if row % ROWS == ROWS - 1:
            store_turned(turned, act, row + 1 - ROWS)

    last = conv_all(accs, g_three, kernel, True, use)

    def more():
        turn_end(turned, act)
        s, sc = [0.5 * v for v in both.totals()]
        sn = sc * inv
        sums[0:1, :] = sn
        sums[1:2, :] = s
        base = inv * (group_sum(s * gain) / count)
        slope = inv * inv * (group_sum(sn * gain) / count)
        base = base + move * slope

        def back(row, dc):
            at = pl.ds(times(row, width), width)
            d = dh[at, :] * scale - raw[at, :] * slope - base
            store_three(three, row, d)
            return dc + fold(d)

        return back, jnp.zeros((8, channels), F32)

    dc_sum[...] = total(kernel_grad(accs, turned, g_three, flat, last, more))


def third_kernel(turned, three, x, stats, vec, kernel, dh, sums, flat):
    accumulators(third_body, turned, three, x, stats, vec, kernel, dh, sums, flat)


def third_body(turned, three, x, stats, vec, kernel, dh, sums, flat, accs):
    height, width, channels = x.shape
    mean, scale, shift = stats[0:1, :], 0.5 * stats[1:2, :] * vec[0:1, :], 0.5 * vec[1:2, :]
    both = Sums(channels, 2)

    def use(row, v):
        c = x[row].astype(F32) - mean
        half = c * scale + shift
        t = jnp.tanh(half)
        d = v * ((1.0 + t) * (1.0 + half * (1.0 - t)))
        dh[row * width : (row + 1) * width, :] = d
        both.add(d, d * c)

    last = conv_all(accs, three, kernel, True, use)

    def more():
        s, sn = [0.5 * v for v in both.totals()]
        sums[0:1, :] = sn * stats[1:2, :]
        sums[1:2, :] = s

    kernel_grad(accs, turned, three, flat, last, more)


def input_kernel(dh, x, g, stats, sums, vec, dc_sum, kernel, embedding, result, emb_grad, done):
    height, width, channels = x.shape
    count = height * width * (channels // GROUPS)
    mean, inv, gain = stats[0:1, :], stats[1:2, :], vec[0:1, :]
    scale = 0.5 * inv * gain
    base = inv * (group_sum(sums[1:2, :] * gain) / count)
    slope = inv * inv * (group_sum(sums[0:1, :] * gain) / count)

    def back(i, _):
        row = i * 4
        d = dh[pl.ds(row * width, 4 * width), :].reshape(4, width, channels)
        c = x[pl.ds(row, 4)].astype(F32) - mean
        result[pl.ds(row, 4)] = g[pl.ds(row, 4)].astype(F32) + (d * scale - base - c * slope)
        return 0

    lax.fori_loop(0, height // 4, back, 0)
    dq = lax.dot_general(
        dc_sum[...],
        kernel[9 * channels :, :].astype(F32),
        (((1,), (1,)), ((), ())),
        precision=lax.Precision.HIGHEST,
        preferred_element_type=F32,
    )
    emb = embedding[...].astype(F32)
    sig = sigmoid(emb)
    emb_grad[...] = dq * (sig * (1.0 + emb * (1.0 - sig)))
    done[...] = base


def last_kernel(part, parts, *refs):
    accumulators(functools.partial(last_body, part, parts), *refs)


def last_body(part, parts, act, x, vec, kernel, *refs):
    out, done, three, result, left, accs = refs[-6:]
    height = x.shape[0]
    rows = height // parts
    base = part * rows
    bias = vec[5:6, :]

    def spread(row):
        if 0 <= base + row < height:
            store_three(three, row, act[base + row + 1].astype(F32))
        else:
            three[:, row + 1 : row + 2] = jnp.zeros((3, 1) + three.shape[2:], BF16)

    def use(row, v):
        result[row] = (x[base + row].astype(F32) + v + bias).astype(BF16)

    per_step = UNITS * ROWS
    steps = rows // per_step
    copies = []

    def send(step):
        here = pl.ds(step * per_step, per_step)
        copies.append(pltpu.make_async_copy(result.at[here], out.at[pl.ds(base + step * per_step, per_step)], left.at[step]))
        copies[-1].start()

    for row in range(-1, per_step + 1):
        spread(row)
    for step in range(steps):
        ahead = range((step + 1) * per_step + 1, min((step + 2) * per_step, rows) + 1)
        others = [functools.partial(spread, row) for row in ahead]
        done_rows = conv_rows(accs, step - 1, (step - 1) % 2, use) if step else []
        mixed = [f for i in range(per_step) for f in (*others[i : i + 1], *done_rows[i : i + 1])]
        conv_step(accs, three, kernel, step, step % 2, False, mixed)
        if step:
            send(step - 1)
    for other in conv_rows(accs, steps - 1, (steps - 1) % 2, use):
        other()
    send(steps - 1)
    done[...] = bias
    for copy in copies:
        copy.wait()


def join_kernel(mine, got, out, tail=VEC_ROWS):
    rows = mine.shape[0] - tail
    out[0:rows, :] = mine[0:rows, :]
    out[rows : 2 * rows, :] = got[0:rows, :]
    if tail:
        out[2 * rows :, :] = mine[rows:, :] + got[rows:, :]


def join_second_kernel(mine, got, out, mark):
    join_kernel(mine, got, out, 0)
    mark[...] = jnp.zeros_like(mark)


def part_kernel(cuts, mine, got, first, second):
    block, cut = sum(cuts), sum(cuts[:-1])
    slots = (mine.shape[0] - VEC_ROWS) // block
    for half, source in enumerate((mine, got)):
        for slot in range(slots):
            at, to = slot * block, half * slots + slot
            first[to * cut : (to + 1) * cut, :] = source[at : at + cut, :]
            second[to * cuts[-1] : (to + 1) * cuts[-1], :] = source[at + cut : at + block, :]
    first[2 * slots * cut :, :] = mine[slots * block :, :] + got[slots * block :, :]


def halve_kernel(keep, got, send_next, keep_next, tail=VEC_ROWS):
    rows = (keep.shape[0] - tail) // 2
    keep_next[0:rows, :] = keep[0:rows, :] + got[0:rows, :].astype(F32)
    send_next[0:rows, :] = (keep[rows : 2 * rows, :] + got[rows : 2 * rows, :].astype(F32)).astype(BF16)
    if tail:
        vec = keep[2 * rows :, :] + got[2 * rows :, :].astype(F32)
        keep_next[rows:, :] = vec
        send_next[rows:, :] = vec.astype(BF16)


def halve_second_kernel(keep, got, send_next, keep_next):
    halve_kernel(keep, got, send_next, keep_next, 0)


def merge_kernel(wide, narrow, one, one_got, two, two_got, send, keep):
    slots = two.shape[0] // narrow // 2
    for slot in range(slots):
        to = slot * (wide + narrow)
        for mine, got, rows in ((one, one_got, wide), (two, two_got, narrow)):
            at, up = slot * rows, (slots + slot) * rows
            keep[to : to + rows, :] = mine[at : at + rows, :] + got[at : at + rows, :].astype(F32)
            send[to : to + rows, :] = (mine[up : up + rows, :] + got[up : up + rows, :].astype(F32)).astype(BF16)
            to += rows
    at, to = 2 * slots * wide, slots * (wide + narrow)
    values = one[at:, :] + one_got[at:, :].astype(F32)
    keep[to:, :] = values
    send[to:, :] = values.astype(BF16)


def place_blocks(wires, cuts, mine, got, flats):
    me = wires.me()
    block = sum(cuts)
    for slot in range(wires.slots):
        for other, source in ((False, mine), (True, got)):
            owner = wires.owner(slot, other, me)
            values = source[slot * block : (slot + 1) * block, :].astype(F32)
            at = 0
            for flat, rows in zip(flats, cuts):
                flat[pl.ds(pl.multiple_of(owner * rows, rows), rows), :] = values[at : at + rows]
                at += rows


def unflatten(flat, out, base):
    for start in range(0, flat.shape[0] // 2, 256):
        out[base + start : base + start + 256, :] = load_flat(flat, 2 * start, 256).astype(BF16)


def arrange_first_kernel(wires, cuts, mine, got, embedding, first, vec, time, flat_one, flat_project, flat_vec):
    place_blocks(wires, cuts, mine, got, (flat_one, flat_project))
    rows_one = flat_one.shape[0] // 2
    unflatten(flat_project, first, rows_one)
    emb = embedding[...].astype(F32)
    act = (emb * sigmoid(emb)).astype(BF16)
    time[...] = jnp.dot(act, first[rows_one:, :], preferred_element_type=F32)
    unflatten(flat_one, first, 0)
    at = wires.slots * sum(cuts)
    flat_vec[...] = mine[at : at + VEC_ROWS, :].astype(F32) + got[at : at + VEC_ROWS, :].astype(F32)
    vec[...] = load_flat(flat_vec, 0, VEC_ROWS // 2)


def arrange_second_kernel(wires, cuts, mine, got, second, flat_two):
    place_blocks(wires, cuts, mine, got, (flat_two,))
    unflatten(flat_two, second, 0)


def take_blocks(wires, cuts, flats, send, keep):
    me = wires.me()
    block = sum(cuts)
    for slot in range(wires.slots):
        for other in (True, False):
            owner = wires.owner(slot, other, me)
            at = slot * block
            for flat, rows in zip(flats, cuts):
                values = flat[pl.ds(pl.multiple_of(owner * rows, rows), rows), :]
                if other:
                    send[at : at + rows, :] = values.astype(BF16)
                else:
                    keep[at : at + rows, :] = values
                at += rows


def pack_first_kernel(
    wires, cuts, flat_one, dc_sum, sums_one, sums_two, g_sum, two, two_got, send, keep, two_send, two_keep
):
    halve_kernel(two, two_got, two_send, two_keep, 0)
    take_blocks(wires, cuts, (flat_one,), send, keep)
    at = wires.slots * sum(cuts)
    vectors = [sums_one[0:1, :], sums_one[1:2, :], dc_sum[...], sums_two[0:1, :], sums_two[1:2, :], g_sum[...]]
    halves = [row[:, i * LANES : (i + 1) * LANES] for row in vectors for i in range(2)]
    values = jnp.concatenate(halves + [jnp.zeros((VEC_ROWS - len(halves), LANES), F32)], axis=0)
    keep[at : at + VEC_ROWS, :] = values
    send[at : at + VEC_ROWS, :] = values.astype(BF16)


def pack_second_kernel(wires, cuts, flat_two, embedding, dc_sum, send, keep, flat_project):
    emb = embedding[...].astype(F32)
    q = (emb * sigmoid(emb)).astype(BF16).astype(F32)
    q = jnp.broadcast_to(q, (LANES, q.shape[1])).T
    dc = dc_sum[...]
    store_flat(flat_project, 0, jnp.concatenate([q * dc[:, :LANES], q * dc[:, LANES:]], axis=1))
    take_blocks(wires, cuts, (flat_two, flat_project), send, keep)


def finish_kernel(wires, cuts, n_vec, keep, got, one, two, project, vec):
    at = 0
    for out, rows in zip((one, two, project), cuts):
        out[...] = keep[at : at + rows, :] + got[at : at + rows, :].astype(F32)
        at += rows
    vectors = keep[at : at + VEC_ROWS, :] + got[at : at + VEC_ROWS, :].astype(F32)
    start = wires.me() * n_vec
    row, lane = start // LANES, start % LANES
    place = lax.broadcasted_iota(jnp.int32, vectors.shape, 0)
    own = jnp.sum(jnp.where(place == row, vectors, 0.0), 0, keepdims=True)
    following = jnp.sum(jnp.where(place == row + 1, vectors, 0.0), 0, keepdims=True)
    column = lax.broadcasted_iota(jnp.int32, own.shape, 1)
    shifted = pltpu.roll(jnp.where(column >= lane, own, following), (LANES - lane) % LANES, 1)
    vec[...] = shifted[:, :n_vec]


def call(body, outs, *args, scratch=(), flops=0, size=4 << 20, after=(), far=(), far_outs=(), semaphores=(), same=None):
    held, n_in = len(after), len(args)

    def run(*refs):
        body(*refs[:n_in], *refs[n_in + held :])

    args = [pltpu.with_memory_space_constraint(v, pltpu.HBM) if i in far else v for i, v in enumerate(args)]

    def spec(is_far):
        return pl.BlockSpec(memory_space=pltpu.HBM if is_far else pltpu.VMEM)

    return pl.pallas_call(
        run,
        out_shape=[
            pltpu.HBM(shape, dtype) if i in far_outs else jax.ShapeDtypeStruct(shape, dtype)
            for i, (shape, dtype) in enumerate(outs)
        ],
        in_specs=[spec(i in far) for i in range(n_in)] + [pl.BlockSpec(memory_space=pl.ANY)] * held,
        out_specs=[spec(i in far_outs) for i in range(len(outs))],
        scratch_shapes=[pltpu.VMEM(shape, dtype) for shape, dtype in scratch]
        + [pltpu.SemaphoreType.DMA((n,)) for n in semaphores],
        input_output_aliases=same or {},
        compiler_params=pltpu.CompilerParams(vmem_limit_bytes=VMEM_BYTES),
        cost_estimate=pl.CostEstimate(flops=0, bytes_accessed=0, transcendentals=0),
    )(*args, *after)


def joined(held, tail=VEC_ROWS):
    return ((2 * (held.shape[0] - tail) + tail, LANES), BF16)


def gather_start(wires, cuts, held, beside):
    last = wires.stages - 1
    for stage in range(last - 1):
        after = beside.get(stage, ())
        held, = call(join_kernel, [joined(held)], held, wires.swap(held, stage), after=after)
    got = wires.swap(held, last - 1)
    slots = wires.slots // 2
    shapes = [(slots * sum(cuts[:-1]) + VEC_ROWS, LANES), (slots * cuts[-1], LANES)]
    outs = [(shape, BF16) for shape in shapes]
    first, second = call(functools.partial(part_kernel, cuts), outs, held, got, after=beside.get(last - 1, ()))
    first_got, second_got = wires.swap(first, last), wires.swap(second, last)
    first, = call(join_kernel, [joined(first)], first, first_got, after=beside.get(last, ()))
    second, mark = call(join_second_kernel, [joined(second, 0), ((1, LANES), F32)], second, second_got)
    return first, wires.swap(first, wires.stages), second, wires.swap(second, wires.stages), mark


def in_order(wires, cuts, mine, got):
    block = sum(cuts)
    rows = wires.slots * block
    both = jnp.concatenate([mine[:rows], got[:rows]]).reshape(wires.n, block, LANES)
    me = wires.me()
    owners = jnp.stack([wires.owner(j, other, me) for other in (False, True) for j in range(wires.slots)])
    both = jnp.zeros_like(both).at[owners].set(both)
    ends = [sum(cuts[:i]) for i in range(len(cuts) + 1)]
    return [both[:, a:b].reshape(-1, 2 * LANES) for a, b in zip(ends, ends[1:])]


def arrange_first(wires, cuts, mine, got, embedding, after):
    channels = 2 * LANES
    totals = [wires.n * rows for rows in cuts]
    if all(rows % 8 == 0 for rows in cuts):
        return call(
            functools.partial(arrange_first_kernel, wires, cuts),
            [((sum(totals) // 2, channels), BF16), ((VEC_ROWS // 2, channels), F32), ((1, channels), F32)],
            mine,
            got,
            embedding,
            scratch=[((rows, LANES), F32) for rows in (*totals, VEC_ROWS)],
            after=after,
        )
    one, project = in_order(wires, cuts, mine, got)
    vec = (mine[-VEC_ROWS:].astype(F32) + got[-VEC_ROWS:].astype(F32)).reshape(VEC_ROWS // 2, channels)
    act = jax.nn.silu(embedding.astype(F32)).astype(BF16)
    return jnp.concatenate([one, project]), vec, jnp.dot(act, project, preferred_element_type=F32)


def arrange_second(wires, cuts, mine, got, after):
    rows = wires.n * cuts[0]
    if cuts[0] % 8 == 0:
        body = functools.partial(arrange_second_kernel, wires, cuts)
        return call(body, [((rows // 2, 2 * LANES), BF16)], mine, got, scratch=[((rows, LANES), F32)], after=after)[0]
    return in_order(wires, cuts, mine, got)[0]


def out_of_order(wires, cuts, parts, tail):
    me = wires.me()
    blocks = jnp.concatenate([v.reshape(wires.n, rows, LANES) for v, rows in zip(parts, cuts)], axis=1)
    halves = []
    for other in (True, False):
        owners = jnp.stack([wires.owner(j, other, me) for j in range(wires.slots)])
        halves.append(jnp.concatenate([blocks[owners].reshape(-1, LANES), tail]))
    return halves[0].astype(BF16), halves[1]


def pack_first(wires, cuts, flat_one, dc_sum, sums_one, sums_two, g_sum, two, two_got):
    shape = (wires.slots * sum(cuts) + VEC_ROWS, LANES)
    if all(rows % 8 == 0 for rows in cuts):
        return call(
            functools.partial(pack_first_kernel, wires, cuts),
            [(shape, BF16), (shape, F32), *halved(two, 0)],
            flat_one,
            dc_sum,
            sums_one,
            sums_two,
            g_sum,
            two,
            two_got,
        )
    vec = jnp.concatenate([sums_one, dc_sum, sums_two, g_sum]).reshape(-1, LANES)
    vec = jnp.pad(vec, ((0, VEC_ROWS - vec.shape[0]), (0, 0)))
    send, keep = out_of_order(wires, cuts, (flat_one,), vec)
    return send, keep, *call(halve_second_kernel, halved(two, 0), two, two_got)


def pack_second(wires, cuts, flat_two, embedding, dc_sum):
    if all(rows % 8 == 0 for rows in cuts):
        shape = (wires.slots * sum(cuts), LANES)
        return call(
            functools.partial(pack_second_kernel, wires, cuts),
            [(shape, BF16), (shape, F32)],
            flat_two,
            embedding,
            dc_sum,
            scratch=[((wires.n * cuts[1], LANES), F32)],
        )
    q = jax.nn.silu(embedding.astype(F32)).astype(BF16).astype(F32).reshape(-1, 1)
    parts = (flat_two, (q * dc_sum).reshape(-1, LANES))
    return out_of_order(wires, cuts, parts, jnp.zeros((0, LANES), F32))


def halved(keep, tail=VEC_ROWS):
    shape = ((keep.shape[0] - tail) // 2 + tail, LANES)
    return [(shape, BF16), (shape, F32)]


def local(sizes, images, embedding, conv_first, conv_second, projection, vectors, cotangent):
    count, height, width, channels = images.shape
    emb_width = embedding.shape[-1]
    wires = Wires(*sizes)
    n_vec = vectors.shape[0]
    assert count == 1 and channels == 2 * LANES and n_vec <= LANES
    cuts = [v.shape[0] // LANES for v in (conv_first, conv_second, projection)]
    pixels = height * width
    three = ((3, height + 2, width, channels), BF16)
    maps = ((height, width, channels), BF16)
    flat = ((pixels, channels), F32)
    line = ((1, channels), F32)
    pair = ((2, channels), F32)
    taps = ((18 * channels, LANES), F32)
    padded = ((height + 2, width, channels), BF16)
    turned = ((2, channels, pixels + 2 * width), BF16)
    conv_flops = 2 * 9 * pixels * channels * channels

    x, g = images[0], cotangent[0]
    stats, x_near = call(stats_kernel, [pair, maps], x, far=(0,), semaphores=(4,))
    g_three, g_sum = call(
        spread_kernel, [three, line], g, scratch=[maps, three], far=(0,), far_outs=(0,), semaphores=(4, 4)
    )
    wide = VEC_ROWS * LANES
    placed = lax.dynamic_slice(jnp.pad(vectors, (wide, wide - n_vec)), (wide - wires.me() * n_vec,), (wide,))
    start = jnp.concatenate([v.reshape(-1, LANES) for v in (conv_first, projection, conv_second, placed)])
    beside = {wires.stages - 2: (g_sum,), wires.stages - 1: (stats,)}
    one, one_got, two, two_got, mark = gather_start(wires, (cuts[0], cuts[2], cuts[1]), start, beside)
    first, vec, time = arrange_first(wires, (cuts[0], cuts[2]), one, one_got, embedding, (mark,))

    turned_one, raw, stats_two = call(
        first_kernel, [turned, flat, pair], x_near, stats, vec, time, first, scratch=[three], flops=conv_flops
    )
    kernel_two = arrange_second(wires, cuts[1:2], two, two_got, (stats_two,))
    act_two, sums_two, grad_two, e_three, dc_sum = call(
        second_kernel,
        [padded, pair, taps, three, line],
        g_three,
        raw,
        stats_two,
        vec,
        kernel_two,
        scratch=[flat, turned],
        flops=2 * conv_flops,
    )
    last = wires.stages
    two_send, two = pack_second(wires, cuts[1:], grad_two, embedding, dc_sum)
    two_got = wires.swap(two_send, last)
    dh_one, sums_one, grad_one = call(
        third_kernel, [flat, pair, taps], turned_one, e_three, x_near, stats, vec, first
    )
    one_send, one, two_send, two = pack_first(
        wires, cuts[:1], grad_one, dc_sum, sums_one, sums_two, g_sum, two, two_got
    )
    input_grad, embedding_grad, input_done = call(
        input_kernel,
        [(maps[0], F32), ((1, emb_width), F32), line],
        dh_one,
        x,
        g,
        stats,
        sums_one,
        vec,
        dc_sum,
        first,
        embedding,
    )
    parts = 2
    rows = height // parts
    output, output_done = (), []
    for part in range(parts):
        *output, done = call(
            functools.partial(last_kernel, part, parts),
            [maps, line],
            act_two,
            x_near,
            vec,
            kernel_two,
            *output,
            scratch=[((3, rows + 2, width, channels), BF16), ((rows, width, channels), BF16)],
            far=(4,),
            far_outs=(0,),
            semaphores=(rows // (UNITS * ROWS),),
            same={4: 0} if output else None,
            flops=conv_flops // parts,
        )
        output_done.append(done)
    two_got = wires.swap(two_send, last - 1)
    one_send, one = call(halve_kernel, halved(one), one, wires.swap(one_send, last))
    one_got = wires.swap(one_send, last - 1)
    wide, narrow = cuts[0], sum(cuts[1:])
    shape = (wires.slots // 4 * (wide + narrow) + VEC_ROWS, LANES)
    send, keep = call(
        functools.partial(merge_kernel, wide, narrow),
        [(shape, BF16), (shape, F32)],
        one,
        one_got,
        two,
        two_got,
        after=output_done[:1],
    )
    for stage in range(last - 2, 0, -1):
        after = {last - 3: (input_done,), last - 2: (output_done[1],)}.get(stage, ())
        send, keep = call(halve_kernel, halved(keep), keep, wires.swap(send, stage), after=after)
    summed = call(
        functools.partial(finish_kernel, wires, cuts, n_vec),
        [*[((rows, LANES), F32) for rows in cuts], ((1, n_vec), F32)],
        keep,
        wires.swap(send, 0),
    )
    return (output[0][None], input_grad[None], embedding_grad, *[v.reshape(-1) for v in summed])


def solution(mesh):
    sizes = (mesh.shape["dp"], mesh.shape["fsdp"])
    split = P(AXES)
    maps = P(AXES, None, None, None)
    in_specs = (maps, P(AXES, None), split, split, split, split, maps)
    out_specs = (maps, maps, P(AXES, None), split, split, split, split)

    def body(*args):
        return local(sizes, *args)

    return jax.shard_map(body, mesh=mesh, in_specs=in_specs, out_specs=out_specs, check_vma=False)
```

```python
import functools
import math

import jax
import jax.numpy as jnp
from jax import lax
from jax.experimental import pallas as pl
from jax.experimental.pallas import tpu as pltpu
from jax.sharding import PartitionSpec as P

GROUPS = 32
EPS = 1e-05
AXES = ("dp", "fsdp")
LANES = 128
VEC_ROWS = 16


class Wires:
    def __init__(self, n_dp, n_fsdp):
        self.n_fsdp = n_fsdp
        self.n = n_dp * n_fsdp
        self.bits = int(math.log2(self.n))
        fsdp_bits = int(math.log2(n_fsdp))
        assert 1 << self.bits == self.n and 1 << fsdp_bits == n_fsdp and fsdp_bits >= 3 and n_dp >= 2
        a, b = 1, fsdp_bits
        far = [bit for bit in range(self.bits - 1, 0, -1) if bit not in (a, b)]
        self.order = {0: [*far, a, b], 1: [*far[::-1], b, a]}
        self.stages = self.bits - 1
        self.slots = 1 << self.stages

    def swap(self, value, stage):
        def bit(core):
            return 0 if stage == self.stages else self.order[core][stage]

        return lax.ppermute(value, AXES, [(i, i ^ (1 << bit(i & 1))) for i in range(self.n)])

    def mask(self, slot, core):
        return sum(1 << self.order[core][i] for i in range(self.stages) if slot >> i & 1)

    def me(self):
        return lax.axis_index("dp") * self.n_fsdp + lax.axis_index("fsdp")

    def owner(self, slot, other, me):
        core = me & 1
        if other:
            me, core = me ^ 1, 1 - core
        return me ^ jnp.where(core == 0, self.mask(slot, 0), self.mask(slot, 1))


def owner(self, slot, other, me):
        core = me & 1
        if other:
            me, core = me ^ 1, 1 - core
        return me ^ jnp.where(core == 0, self.mask(slot, 0), self.mask(slot, 1))


ROWS = 4
UNITS = 2
PIECE = 64
F32 = jnp.float32
BF16 = jnp.bfloat16
VMEM_BYTES = 15 * 1024 * 1024


def group_sum(totals):
    channels = totals.shape[1]
    lane = lax.broadcasted_iota(jnp.int32, totals.shape, 1)
    span = 1
    while span < channels // GROUPS:
        up = pltpu.roll(totals, channels - span, 1)
        down = pltpu.roll(totals, span, 1)
        totals = totals + jnp.where((lane & span) == 0, up, down)
        span *= 2
    return totals


def fold(values):
    channels = values.shape[-1]
    return jnp.sum(values.reshape(-1, 8, channels), 0)


def total(partial):
    return jnp.sum(partial, 0, keepdims=True)


def sigmoid(v):
    return 0.5 * jnp.tanh(0.5 * v) + 0.5


def clear_edges(three):
    height = three.shape[1] - 2
    zero = jnp.zeros((3, 1) + three.shape[2:], three.dtype)
    three[:, 0:1] = zero
    three[:, height + 1 : height + 2] = zero


def store_three(three, row, value):
    width = value.shape[0]
    column = lax.broadcasted_iota(jnp.int32, (8, value.shape[1]), 0)
    left = pltpu.roll(value, 1, 0)
    left = jnp.concatenate([jnp.where(column == 0, 0.0, left[:8]), left[8:]], axis=0)
    right = pltpu.roll(value, width - 1, 0)
    right = jnp.concatenate([right[: width - 8], jnp.where(column == 7, 0.0, right[width - 8 :])], axis=0)
    three[0, row + 1] = left.astype(three.dtype)
    three[1, row + 1] = value.astype(three.dtype)
    three[2, row + 1] = right.astype(three.dtype)


def accumulators(body, *refs):
    groups = 4

    def run(*accs):
        accs = iter(accs)
        body(*refs, [[[next(accs) for _ in range(ROWS)] for _ in range(groups)] for _ in range(UNITS)])

    pl.run_scoped(run, *[pltpu.ACC(unit)((PIECE, 2 * LANES), F32) for unit in range(UNITS) for _ in range(groups * ROWS)])


def interleave(pieces, slots):
    return [pieces * (i + 1) // slots - pieces * i // slots for i in range(slots)]


def times(value, size):
    return value * size if isinstance(value, int) else pl.multiple_of(value * size, size)


def conv_step(accs, three, kernel, step, parity, back, others=()):
    others = list(others)
    for tap, share in enumerate(interleave(len(others), 9)):
        at = (8 - tap if back else tap) * three.shape[3]
        stage = (parity + tap) % 2
        for unit in range(UNITS):
            pltpu.matmul_push_rhs(kernel[at : at + three.shape[3], :], stage, unit, transpose=back)
        for piece in range(ROWS):
            for unit in range(UNITS):
                row = (UNITS * step + unit) * ROWS + piece + tap // 3
                pltpu.matmul_acc_lhs(
                    accs[unit][parity][piece], three[tap % 3, row], load_staged_rhs=stage if piece == 0 else None
                )
        for _ in range(share):
            others.pop(0)()


def conv_rows(accs, step, parity, use):
    def one(unit, piece):
        use((UNITS * step + unit) * ROWS + piece, pltpu.matmul_pop(accs[unit][parity][piece]))

    return [functools.partial(one, unit, piece) for unit in range(UNITS) for piece in range(ROWS)]


def conv_all(accs, three, kernel, back, use):
    steps = (three.shape[1] - 2) // (UNITS * ROWS)
    for step in range(steps):
        others = conv_rows(accs, step - 1, (step - 1) % 2, use) if step else ()
        conv_step(accs, three, kernel, step, step % 2, back, others)
    assert steps % 2 == 0
    return conv_rows(accs, steps - 1, 1, use)


class Sums:
    def __init__(self, channels, count):
        self.values = [jnp.zeros((8, channels), F32)] * count

    def add(self, *values):
        self.values = [s + fold(v) for s, v in zip(self.values, values)]

    def totals(self):
        return [total(s) for s in self.values]


def store_turned(turned, padded, row):
    width, channels = padded.shape[1:]
    size = ROWS * width
    lanes = pl.ds(times(row // ROWS, size), size)
    turned[0, :, lanes] = padded[pl.ds(row + 1, ROWS)].reshape(size, channels).T
    turned[1, :, lanes] = padded[pl.ds(row, ROWS)].reshape(size, channels).T


def turn_end(turned, padded):
    height = padded.shape[0] - 2
    width, channels = padded.shape[1:]
    at = height * width
    turned[1, :, at : at + 2 * width] = padded[height : height + 2].reshape(2 * width, channels).T


def grad_step(accs, turned, three, work, stage, others=()):
    others = list(others)
    width, channels = three.shape[2:]
    size = ROWS * width
    for unit, column, chunk, _ in work:
        rhs = three[column, pl.ds(1 + times(chunk, ROWS), ROWS)].reshape(size, channels)
        pltpu.matmul_push_rhs(rhs, stage, unit)
    shares = iter(interleave(len(others), 3 * ROWS))
    for row in range(3):
        for piece in range(ROWS):
            for unit, _, chunk, groups in work:
                source, at = (0, times(chunk, size)) if row == 1 else (1, times(chunk, size) + row * width)
                lhs = turned[source, piece * PIECE : (piece + 1) * PIECE, pl.ds(at, size)]
                first = row == 0 and piece == 0
                pltpu.matmul_acc_lhs(accs[unit][groups[row]][piece], lhs, load_staged_rhs=stage if first else None)
            for _ in range(next(shares)):
                others.pop(0)()


def kernel_grad(accs, turned, three, flat, first, more):
    height, channels = three.shape[1] - 2, three.shape[3]
    chunks = height // ROWS
    lead, step = 4, 4
    outer_groups, inner_groups = (0, 2, 3), (1, 0, 2)

    def sides(chunk, stage, others):
        work = [(0, 0, chunk, outer_groups), (1, 2, chunk, outer_groups)]
        grad_step(accs, turned, three, work, stage, others)

    first = list(first)
    for chunk, share in enumerate(interleave(len(first), lead)):
        sides(chunk, chunk % 2, [first.pop(0) for _ in range(share)])
    beside, carry = more() or (None, 0)
    kept = [carry]

    def other(row):
        kept[0] = beside(row, kept[0])

    def loop(i, carry):
        kept[0] = carry
        for k in range(step):
            at = step * i + k
            sides(lead + at, k % 2, [functools.partial(other, ROWS * at + j) for j in range(ROWS)] if beside else ())
        return kept[0]

    if beside:
        kept[0] = lax.fori_loop(0, (chunks - lead) // step, loop, carry)
    else:
        for i in range((chunks - lead) // step):
            loop(i, carry)

    def store(tap, piece, value):
        store_flat(flat, (tap * channels + piece * PIECE) * 2, value)

    def side(unit, row, piece):
        store(3 * row + 2 - 2 * unit, piece, pltpu.matmul_pop(accs[unit][outer_groups[row]][piece]))

    for row in range(2):
        for unit in range(UNITS):
            for piece in range(ROWS):
                side(unit, row, piece)
    half = chunks // UNITS
    rest = [functools.partial(other, row) for row in range(ROWS * (chunks - lead), height)] if beside else []
    for chunk, share in enumerate(interleave(len(rest), half)):
        work = [(unit, 1, unit * half + chunk, inner_groups) for unit in range(UNITS)]
        others = [functools.partial(side, unit, 2, piece) for unit in range(UNITS) for piece in range(ROWS)]
        more_rows = [rest.pop(0) for _ in range(share)]
        grad_step(accs, turned, three, work, chunk % 2, (others if chunk == 0 else []) + more_rows)
    for row, group in enumerate(inner_groups):
        for piece in range(ROWS):
            store(3 * row + 1, piece, pltpu.matmul_pop(accs[0][group][piece]) + pltpu.matmul_pop(accs[1][group][piece]))
    return kept[0]


def store_flat(flat, start, value):
    rows = value.shape[0]
    flat[pl.ds(start, rows, stride=2), :] = value[:, :LANES]
    flat[pl.ds(start + 1, rows, stride=2), :] = value[:, LANES:]


def load_flat(flat, start, rows):
    left = flat[pl.ds(start, rows, stride=2), :]
    right = flat[pl.ds(start + 1, rows, stride=2), :]
    return jnp.concatenate([left, right], axis=1)


def stats_kernel(x_hbm, stats, x, arrived):
    height, width, channels = x.shape
    count = height * width * (channels // GROUPS)
    zero = jnp.zeros((8, channels), F32)
    parts = arrived.shape[0]
    rows = height // parts
    copies = [
        pltpu.make_async_copy(x_hbm.at[pl.ds(k * rows, rows)], x.at[pl.ds(k * rows, rows)], arrived.at[k])
        for k in range(parts)
    ]
    for copy in copies:
        copy.start()
    s = zero
    for k, copy in enumerate(copies):
        copy.wait()
        s = lax.fori_loop(0, rows // 4, lambda i, s, k=k: s + fold(x[pl.ds(k * rows + i * 4, 4)].astype(F32)), s)
    mean = group_sum(total(s)) / count

    def second(i, v):
        d = x[pl.ds(i * 4, 4)].astype(F32) - mean
        return v + fold(d * d)

    v = lax.fori_loop(0, height // 4, second, zero)
    inv = lax.rsqrt(group_sum(total(v)) / count + EPS)
    stats[0:1, :] = mean
    stats[1:2, :] = inv


def spread_kernel(g_hbm, three_hbm, g_sum, g, three, arrived, left):
    height, width, channels = g.shape
    parts = arrived.shape[0]
    rows = height // parts
    copies = [
        pltpu.make_async_copy(g_hbm.at[pl.ds(k * rows, rows)], g.at[pl.ds(k * rows, rows)], arrived.at[k])
        for k in range(parts)
    ]
    for copy in copies:
        copy.start()
    clear_edges(three)
    s = jnp.zeros((8, channels), F32)
    out = []
    for k, copy in enumerate(copies):
        copy.wait()

        def step(i, s, k=k):
            row = k * rows + i * 4
            values = g[pl.ds(row, 4)].astype(F32)
            for j in range(4):
                store_three(three, row + j, values[j])
            return s + fold(values)

        s = lax.fori_loop(0, rows // 4, step, s)
        start = k * rows + (1 if k else 0)
        size = rows + (1 if k == 0 else 0) + (1 if k == parts - 1 else 0)
        away = pltpu.make_async_copy(three.at[:, pl.ds(start, size)], three_hbm.at[:, pl.ds(start, size)], left.at[k])
        away.start()
        out.append(away)
    g_sum[...] = total(s)
    for away in out:
        away.wait()


def first_kernel(x, stats, vec, time, kernel, turned, raw, stats_out, three):
    accumulators(first_body, x, stats, vec, time, kernel, turned, raw, stats_out, three)


def first_body(x, stats, vec, time, kernel, turned, raw, stats_out, three, accs):
    height, width, channels = x.shape
    pixels = height * width
    per_group = channels // GROUPS
    mean, scale, shift = stats[0:1, :], 0.5 * stats[1:2, :] * vec[0:1, :], 0.5 * vec[1:2, :]
    offset = vec[2:3, :] + time[...]
    sums = Sums(channels, 2)
    pivot = []
    clear_edges(three)

    def activate(row):
        half = (x[row].astype(F32) - mean) * scale + shift
        store_three(three, row, half * (1.0 + jnp.tanh(half)))
        if row % ROWS == ROWS - 1:
            store_turned(turned, three.at[1], row + 1 - ROWS)

    def use(row, v):
        if row == 0:
            pivot.append(total(fold(v)) / width)
        raw[row * width : (row + 1) * width, :] = v
        d = v - pivot[0]
        sums.add(d, d * d)

    per_step = UNITS * ROWS
    steps = height // per_step
    for row in range(per_step + 1):
        activate(row)
    for step in range(steps):
        ahead = range((step + 1) * per_step + 1, min((step + 2) * per_step + 1, height))
        others = [functools.partial(activate, row) for row in ahead]
        done = conv_rows(accs, step - 1, (step - 1) % 2, use) if step else []
        mixed = [f for i in range(per_step) for f in (*others[i : i + 1], *done[i : i + 1])]
        conv_step(accs, three, kernel, step, step % 2, False, mixed)
    turn_end(turned, three.at[1])
    for other in conv_rows(accs, steps - 1, (steps - 1) % 2, use):
        other()
    part, square = [v / pixels for v in sums.totals()]
    spread = square - part * part
    middle = pivot[0] + part + offset
    mean_two = group_sum(middle) / per_group
    away = middle - mean_two
    stats_out[0:1, :] = offset - mean_two
    stats_out[1:2, :] = lax.rsqrt(group_sum(spread + away * away) / per_group + EPS)


def second_kernel(g_three, raw, stats, vec, kernel, act, sums, flat, three, dc_sum, dh, turned):
    accumulators(second_body, g_three, raw, stats, vec, kernel, act, sums, flat, three, dc_sum, dh, turned)


def second_body(g_three, raw, stats, vec, kernel, act, sums, flat, three, dc_sum, dh, turned, accs):
    height, width, channels = act.shape[0] - 2, act.shape[1], act.shape[2]
    count = height * width * (channels // GROUPS)
    move, inv, gain, shift = stats[0:1, :], stats[1:2, :], vec[3:4, :], vec[4:5, :]
    scale, shift = 0.5 * inv * gain, 0.5 * shift
    both = Sums(channels, 2)
    act[0:1] = jnp.zeros((1, width, channels), BF16)
    act[height + 1 : height + 2] = jnp.zeros((1, width, channels), BF16)
    clear_edges(three)

    def use(row, v):
        at = slice(row * width, (row + 1) * width)
        c = raw[at, :] + move
        half = c * scale + shift
        t = jnp.tanh(half)
        u = 1.0 + t
        a = half * u
        act[row + 1] = a.astype(BF16)
        d = v * (u + a * (1.0 - t))
        dh[at, :] = d
        both.add(d, d * c)
        if row % ROWS == ROWS - 1:
            store_turned(turned, act, row + 1 - ROWS)

    last = conv_all(accs, g_three, kernel, True, use)

    def more():
        turn_end(turned, act)
        s, sc = [0.5 * v for v in both.totals()]
        sn = sc * inv
        sums[0:1, :] = sn
        sums[1:2, :] = s
        base = inv * (group_sum(s * gain) / count)
        slope = inv * inv * (group_sum(sn * gain) / count)
        base = base + move * slope

        def back(row, dc):
            at = pl.ds(times(row, width), width)
            d = dh[at, :] * scale - raw[at, :] * slope - base
            store_three(three, row, d)
            return dc + fold(d)

        return back, jnp.zeros((8, channels), F32)

    dc_sum[...] = total(kernel_grad(accs, turned, g_three, flat, last, more))


def third_kernel(turned, three, x, stats, vec, kernel, dh, sums, flat):
    accumulators(third_body, turned, three, x, stats, vec, kernel, dh, sums, flat)


def third_body(turned, three, x, stats, vec, kernel, dh, sums, flat, accs):
    height, width, channels = x.shape
    mean, scale, shift = stats[0:1, :], 0.5 * stats[1:2, :] * vec[0:1, :], 0.5 * vec[1:2, :]
    both = Sums(channels, 2)

    def use(row, v):
        c = x[row].astype(F32) - mean
        half = c * scale + shift
        t = jnp.tanh(half)
        d = v * ((1.0 + t) * (1.0 + half * (1.0 - t)))
        dh[row * width : (row + 1) * width, :] = d
        both.add(d, d * c)

    last = conv_all(accs, three, kernel, True, use)

    def more():
        s, sn = [0.5 * v for v in both.totals()]
        sums[0:1, :] = sn * stats[1:2, :]
        sums[1:2, :] = s

    kernel_grad(accs, turned, three, flat, last, more)


def input_kernel(dh, x, g, stats, sums, vec, dc_sum, kernel, embedding, result, emb_grad, done):
    height, width, channels = x.shape
    count = height * width * (channels // GROUPS)
    mean, inv, gain = stats[0:1, :], stats[1:2, :], vec[0:1, :]
    scale = 0.5 * inv * gain
    base = inv * (group_sum(sums[1:2, :] * gain) / count)
    slope = inv * inv * (group_sum(sums[0:1, :] * gain) / count)

    def back(i, _):
        row = i * 4
        d = dh[pl.ds(row * width, 4 * width), :].reshape(4, width, channels)
        c = x[pl.ds(row, 4)].astype(F32) - mean
        result[pl.ds(row, 4)] = g[pl.ds(row, 4)].astype(F32) + (d * scale - base - c * slope)
        return 0

    lax.fori_loop(0, height // 4, back, 0)
    dq = lax.dot_general(
        dc_sum[...],
        kernel[9 * channels :, :].astype(F32),
        (((1,), (1,)), ((), ())),
        precision=lax.Precision.HIGHEST,
        preferred_element_type=F32,
    )
    emb = embedding[...].astype(F32)
    sig = sigmoid(emb)
    emb_grad[...] = dq * (sig * (1.0 + emb * (1.0 - sig)))
    done[...] = base


def last_kernel(part, parts, *refs):
    accumulators(functools.partial(last_body, part, parts), *refs)


def last_body(part, parts, act, x, vec, kernel, *refs):
    out, done, three, result, left, accs = refs[-6:]
    height = x.shape[0]
    rows = height // parts
    base = part * rows
    bias = vec[5:6, :]

    def spread(row):
        if 0 <= base + row < height:
            store_three(three, row, act[base + row + 1].astype(F32))
        else:
            three[:, row + 1 : row + 2] = jnp.zeros((3, 1) + three.shape[2:], BF16)

    def use(row, v):
        result[row] = (x[base + row].astype(F32) + v + bias).astype(BF16)

    per_step = UNITS * ROWS
    steps = rows // per_step
    copies = []

    def send(step):
        here = pl.ds(step * per_step, per_step)
        copies.append(pltpu.make_async_copy(result.at[here], out.at[pl.ds(base + step * per_step, per_step)], left.at[step]))
        copies[-1].start()

    for row in range(-1, per_step + 1):
        spread(row)
    for step in range(steps):
        ahead = range((step + 1) * per_step + 1, min((step + 2) * per_step, rows) + 1)
        others = [functools.partial(spread, row) for row in ahead]
        done_rows = conv_rows(accs, step - 1, (step - 1) % 2, use) if step else []
        mixed = [f for i in range(per_step) for f in (*others[i : i + 1], *done_rows[i : i + 1])]
        conv_step(accs, three, kernel, step, step % 2, False, mixed)
        if step:
            send(step - 1)
    for other in conv_rows(accs, steps - 1, (steps - 1) % 2, use):
        other()
    send(steps - 1)
    done[...] = bias
    for copy in copies:
        copy.wait()


def start_kernel(wires, n_vec, *refs):
    *parts, vectors, out, own, arrived = refs
    copies, at = [], 0
    for i, part in enumerate(parts):
        copies.append(pltpu.make_async_copy(part, out.at[pl.ds(at, part.shape[0])], arrived.at[i]))
        at += part.shape[0]
    copies.append(pltpu.make_async_copy(vectors, own, arrived.at[len(parts)]))
    for copy in copies:
        copy.start()
    copies[-1].wait()
    first = wires.me() * n_vec
    row, lane = first // LANES, first % LANES
    values = jnp.concatenate([own[...].astype(F32), jnp.zeros((1, LANES - n_vec), F32)], axis=1)
    values = jnp.broadcast_to(pltpu.roll(values, lane, 1), (VEC_ROWS, LANES))
    place = lax.broadcasted_iota(jnp.int32, values.shape, 0)
    column = lax.broadcasted_iota(jnp.int32, values.shape, 1)
    here = ((place == row) & (column >= lane)) | ((place == row + 1) & (column < lane))
    out[at : at + VEC_ROWS, :] = jnp.where(here, values, 0.0).astype(BF16)
    for copy in copies[:-1]:
        copy.wait()


def join_kernel(mine, got, out, tail=VEC_ROWS):
    rows = mine.shape[0] - tail
    out[0:rows, :] = mine[0:rows, :]
    out[rows : 2 * rows, :] = got[0:rows, :]
    if tail:
        out[2 * rows :, :] = mine[rows:, :] + got[rows:, :]


def join_second_kernel(mine, got, out, mark):
    join_kernel(mine, got, out, 0)
    mark[...] = jnp.zeros_like(mark)


def part_kernel(cuts, mine, got, first, second):
    block, cut = sum(cuts), sum(cuts[:-1])
    slots = (mine.shape[0] - VEC_ROWS) // block
    for half, source in enumerate((mine, got)):
        for slot in range(slots):
            at, to = slot * block, half * slots + slot
            first[to * cut : (to + 1) * cut, :] = source[at : at + cut, :]
            second[to * cuts[-1] : (to + 1) * cuts[-1], :] = source[at + cut : at + block, :]
    first[2 * slots * cut :, :] = mine[slots * block :, :] + got[slots * block :, :]


def halve_kernel(keep, got, send_next, keep_next, tail=VEC_ROWS):
    rows = (keep.shape[0] - tail) // 2
    keep_next[0:rows, :] = keep[0:rows, :] + got[0:rows, :].astype(F32)
    send_next[0:rows, :] = (keep[rows : 2 * rows, :] + got[rows : 2 * rows, :].astype(F32)).astype(BF16)
    if tail:
        vec = keep[2 * rows :, :] + got[2 * rows :, :].astype(F32)
        keep_next[rows:, :] = vec
        send_next[rows:, :] = vec.astype(BF16)


def halve_second_kernel(keep, got, send_next, keep_next):
    halve_kernel(keep, got, send_next, keep_next, 0)


def merge_kernel(wide, narrow, one, one_got, two, two_got, send, keep):
    slots = two.shape[0] // narrow // 2
    for slot in range(slots):
        to = slot * (wide + narrow)
        for mine, got, rows in ((one, one_got, wide), (two, two_got, narrow)):
            at, up = slot * rows, (slots + slot) * rows
            keep[to : to + rows, :] = mine[at : at + rows, :] + got[at : at + rows, :].astype(F32)
            send[to : to + rows, :] = (mine[up : up + rows, :] + got[up : up + rows, :].astype(F32)).astype(BF16)
            to += rows
    at, to = 2 * slots * wide, slots * (wide + narrow)
    values = one[at:, :] + one_got[at:, :].astype(F32)
    keep[to:, :] = values
    send[to:, :] = values.astype(BF16)


def place_blocks(wires, cuts, mine, got, flats):
    me = wires.me()
    block = sum(cuts)
    for slot in range(wires.slots):
        for other, source in ((False, mine), (True, got)):
            owner = wires.owner(slot, other, me)
            values = source[slot * block : (slot + 1) * block, :].astype(F32)
            at = 0
            for flat, rows in zip(flats, cuts):
                flat[pl.ds(pl.multiple_of(owner * rows, rows), rows), :] = values[at : at + rows]
                at += rows


def unflatten(flat, out, base):
    for start in range(0, flat.shape[0] // 2, 256):
        out[base + start : base + start + 256, :] = load_flat(flat, 2 * start, 256).astype(BF16)


def arrange_first_kernel(wires, cuts, mine, got, embedding, first, vec, time, flat_one, flat_project, flat_vec):
    place_blocks(wires, cuts, mine, got, (flat_one, flat_project))
    rows_one = flat_one.shape[0] // 2
    unflatten(flat_project, first, rows_one)
    emb = embedding[...].astype(F32)
    act = (emb * sigmoid(emb)).astype(BF16)
    time[...] = jnp.dot(act, first[rows_one:, :], preferred_element_type=F32)
    unflatten(flat_one, first, 0)
    at = wires.slots * sum(cuts)
    flat_vec[...] = mine[at : at + VEC_ROWS, :].astype(F32) + got[at : at + VEC_ROWS, :].astype(F32)
    vec[...] = load_flat(flat_vec, 0, VEC_ROWS // 2)


def arrange_second_kernel(wires, cuts, mine, got, second, flat_two):
    place_blocks(wires, cuts, mine, got, (flat_two,))
    unflatten(flat_two, second, 0)


def take_blocks(wires, cuts, flats, send, keep):
    me = wires.me()
    block = sum(cuts)
    for slot in range(wires.slots):
        for other in (True, False):
            owner = wires.owner(slot, other, me)
            at = slot * block
            for flat, rows in zip(flats, cuts):
                values = flat[pl.ds(pl.multiple_of(owner * rows, rows), rows), :]
                if other:
                    send[at : at + rows, :] = values.astype(BF16)
                else:
                    keep[at : at + rows, :] = values
                at += rows


def pack_first_kernel(
    wires, cuts, flat_one, dc_sum, sums_one, sums_two, g_sum, two, two_got, send, keep, two_send, two_keep
):
    halve_kernel(two, two_got, two_send, two_keep, 0)
    take_blocks(wires, cuts, (flat_one,), send, keep)
    at = wires.slots * sum(cuts)
    vectors = [sums_one[0:1, :], sums_one[1:2, :], dc_sum[...], sums_two[0:1, :], sums_two[1:2, :], g_sum[...]]
    halves = [row[:, i * LANES : (i + 1) * LANES] for row in vectors for i in range(2)]
    values = jnp.concatenate(halves + [jnp.zeros((VEC_ROWS - len(halves), LANES), F32)], axis=0)
    keep[at : at + VEC_ROWS, :] = values
    send[at : at + VEC_ROWS, :] = values.astype(BF16)


def pack_second_kernel(wires, cuts, flat_two, embedding, dc_sum, send, keep, flat_project):
    emb = embedding[...].astype(F32)
    q = (emb * sigmoid(emb)).astype(BF16).astype(F32)
    q = jnp.broadcast_to(q, (LANES, q.shape[1])).T
    dc = dc_sum[...]
    store_flat(flat_project, 0, jnp.concatenate([q * dc[:, :LANES], q * dc[:, LANES:]], axis=1))
    take_blocks(wires, cuts, (flat_two, flat_project), send, keep)


def finish_kernel(wires, cuts, n_vec, keep, got, one, two, project, vec):
    at = 0
    for out, rows in zip((one, two, project), cuts):
        out[...] = keep[at : at + rows, :] + got[at : at + rows, :].astype(F32)
        at += rows
    vectors = keep[at : at + VEC_ROWS, :] + got[at : at + VEC_ROWS, :].astype(F32)
    start = wires.me() * n_vec
    row, lane = start // LANES, start % LANES
    place = lax.broadcasted_iota(jnp.int32, vectors.shape, 0)
    own = jnp.sum(jnp.where(place == row, vectors, 0.0), 0, keepdims=True)
    following = jnp.sum(jnp.where(place == row + 1, vectors, 0.0), 0, keepdims=True)
    column = lax.broadcasted_iota(jnp.int32, own.shape, 1)
    shifted = pltpu.roll(jnp.where(column >= lane, own, following), (LANES - lane) % LANES, 1)
    vec[...] = shifted[:, :n_vec]


def call(body, outs, *args, scratch=(), flops=0, size=4 << 20, after=(), far=(), far_outs=(), semaphores=(), same=None):
    held, n_in = len(after), len(args)

    def run(*refs):
        body(*refs[:n_in], *refs[n_in + held :])

    args = [pltpu.with_memory_space_constraint(v, pltpu.HBM) if i in far else v for i, v in enumerate(args)]

    def spec(is_far):
        return pl.BlockSpec(memory_space=pltpu.HBM if is_far else pltpu.VMEM)

    return pl.pallas_call(
        run,
        out_shape=[
            pltpu.HBM(shape, dtype) if i in far_outs else jax.ShapeDtypeStruct(shape, dtype)
            for i, (shape, dtype) in enumerate(outs)
        ],
        in_specs=[spec(i in far) for i in range(n_in)] + [pl.BlockSpec(memory_space=pl.ANY)] * held,
        out_specs=[spec(i in far_outs) for i in range(len(outs))],
        scratch_shapes=[pltpu.VMEM(shape, dtype) for shape, dtype in scratch]
        + [pltpu.SemaphoreType.DMA((n,)) for n in semaphores],
        input_output_aliases=same or {},
        compiler_params=pltpu.CompilerParams(vmem_limit_bytes=VMEM_BYTES),
        cost_estimate=pl.CostEstimate(flops=0, bytes_accessed=0, transcendentals=0),
    )(*args, *after)


def joined(held, tail=VEC_ROWS):
    return ((2 * (held.shape[0] - tail) + tail, LANES), BF16)


def gather_start(wires, cuts, held, beside):
    last = wires.stages - 1
    for stage in range(last - 1):
        after = beside.get(stage, ())
        held, = call(join_kernel, [joined(held)], held, wires.swap(held, stage), after=after)
    got = wires.swap(held, last - 1)
    slots = wires.slots // 2
    shapes = [(slots * sum(cuts[:-1]) + VEC_ROWS, LANES), (slots * cuts[-1], LANES)]
    outs = [(shape, BF16) for shape in shapes]
    first, second = call(functools.partial(part_kernel, cuts), outs, held, got, after=beside.get(last - 1, ()))
    first_got, second_got = wires.swap(first, last), wires.swap(second, last)
    first, = call(join_kernel, [joined(first)], first, first_got, after=beside.get(last, ()))
    second, mark = call(join_second_kernel, [joined(second, 0), ((1, LANES), F32)], second, second_got)
    return first, wires.swap(first, wires.stages), second, wires.swap(second, wires.stages), mark


def in_order(wires, cuts, mine, got):
    block = sum(cuts)
    rows = wires.slots * block
    both = jnp.concatenate([mine[:rows], got[:rows]]).reshape(wires.n, block, LANES)
    me = wires.me()
    owners = jnp.stack([wires.owner(j, other, me) for other in (False, True) for j in range(wires.slots)])
    both = jnp.zeros_like(both).at[owners].set(both)
    ends = [sum(cuts[:i]) for i in range(len(cuts) + 1)]
    return [both[:, a:b].reshape(-1, 2 * LANES) for a, b in zip(ends, ends[1:])]


def arrange_first(wires, cuts, mine, got, embedding, after):
    channels = 2 * LANES
    totals = [wires.n * rows for rows in cuts]
    if all(rows % 8 == 0 for rows in cuts):
        return call(
            functools.partial(arrange_first_kernel, wires, cuts),
            [((sum(totals) // 2, channels), BF16), ((VEC_ROWS // 2, channels), F32), ((1, channels), F32)],
            mine,
            got,
            embedding,
            scratch=[((rows, LANES), F32) for rows in (*totals, VEC_ROWS)],
            after=after,
        )
    one, project = in_order(wires, cuts, mine, got)
    vec = (mine[-VEC_ROWS:].astype(F32) + got[-VEC_ROWS:].astype(F32)).reshape(VEC_ROWS // 2, channels)
    act = jax.nn.silu(embedding.astype(F32)).astype(BF16)
    return jnp.concatenate([one, project]), vec, jnp.dot(act, project, preferred_element_type=F32)


def arrange_second(wires, cuts, mine, got, after):
    rows = wires.n * cuts[0]
    if cuts[0] % 8 == 0:
        body = functools.partial(arrange_second_kernel, wires, cuts)
        return call(body, [((rows // 2, 2 * LANES), BF16)], mine, got, scratch=[((rows, LANES), F32)], after=after)[0]
    return in_order(wires, cuts, mine, got)[0]


def out_of_order(wires, cuts, parts, tail):
    me = wires.me()
    blocks = jnp.concatenate([v.reshape(wires.n, rows, LANES) for v, rows in zip(parts, cuts)], axis=1)
    halves = []
    for other in (True, False):
        owners = jnp.stack([wires.owner(j, other, me) for j in range(wires.slots)])
        halves.append(jnp.concatenate([blocks[owners].reshape(-1, LANES), tail]))
    return halves[0].astype(BF16), halves[1]


def pack_first(wires, cuts, flat_one, dc_sum, sums_one, sums_two, g_sum, two, two_got):
    shape = (wires.slots * sum(cuts) + VEC_ROWS, LANES)
    if all(rows % 8 == 0 for rows in cuts):
        return call(
            functools.partial(pack_first_kernel, wires, cuts),
            [(shape, BF16), (shape, F32), *halved(two, 0)],
            flat_one,
            dc_sum,
            sums_one,
            sums_two,
            g_sum,
            two,
            two_got,
        )
    vec = jnp.concatenate([sums_one, dc_sum, sums_two, g_sum]).reshape(-1, LANES)
    vec = jnp.pad(vec, ((0, VEC_ROWS - vec.shape[0]), (0, 0)))
    send, keep = out_of_order(wires, cuts, (flat_one,), vec)
    return send, keep, *call(halve_second_kernel, halved(two, 0), two, two_got)


def pack_second(wires, cuts, flat_two, embedding, dc_sum):
    if all(rows % 8 == 0 for rows in cuts):
        shape = (wires.slots * sum(cuts), LANES)
        return call(
            functools.partial(pack_second_kernel, wires, cuts),
            [(shape, BF16), (shape, F32)],
            flat_two,
            embedding,
            dc_sum,
            scratch=[((wires.n * cuts[1], LANES), F32)],
        )
    q = jax.nn.silu(embedding.astype(F32)).astype(BF16).astype(F32).reshape(-1, 1)
    parts = (flat_two, (q * dc_sum).reshape(-1, LANES))
    return out_of_order(wires, cuts, parts, jnp.zeros((0, LANES), F32))


def halved(keep, tail=VEC_ROWS):
    shape = ((keep.shape[0] - tail) // 2 + tail, LANES)
    return [(shape, BF16), (shape, F32)]


def local(sizes, images, embedding, conv_first, conv_second, projection, vectors, cotangent):
    count, height, width, channels = images.shape
    emb_width = embedding.shape[-1]
    wires = Wires(*sizes)
    n_vec = vectors.shape[0]
    assert count == 1 and channels == 2 * LANES and n_vec <= LANES
    cuts = [v.shape[0] // LANES for v in (conv_first, conv_second, projection)]
    pixels = height * width
    three = ((3, height + 2, width, channels), BF16)
    maps = ((height, width, channels), BF16)
    flat = ((pixels, channels), F32)
    line = ((1, channels), F32)
    pair = ((2, channels), F32)
    taps = ((18 * channels, LANES), F32)
    padded = ((height + 2, width, channels), BF16)
    turned = ((2, channels, pixels + 2 * width), BF16)
    conv_flops = 2 * 9 * pixels * channels * channels

    x, g = images[0], cotangent[0]
    stats, x_near = call(stats_kernel, [pair, maps], x, far=(0,), semaphores=(4,))
    g_three, g_sum = call(
        spread_kernel, [three, line], g, scratch=[maps, three], far=(0,), far_outs=(0,), semaphores=(4, 4)
    )
    order = (conv_first, projection, conv_second)
    if all(rows % 16 == 0 for rows in cuts):
        start, = call(
            functools.partial(start_kernel, wires, n_vec),
            [((sum(cuts) + VEC_ROWS, LANES), BF16)],
            *[v.reshape(-1, LANES) for v in order],
            vectors.reshape(1, n_vec),
            scratch=[((1, n_vec), BF16)],
            far=(0, 1, 2, 3),
            semaphores=(4,),
        )
    else:
        wide = VEC_ROWS * LANES
        placed = lax.dynamic_slice(jnp.pad(vectors, (wide, wide - n_vec)), (wide - wires.me() * n_vec,), (wide,))
        start = jnp.concatenate([v.reshape(-1, LANES) for v in (*order, placed)])
    beside = {wires.stages - 2: (g_sum,), wires.stages - 1: (stats,)}
    one, one_got, two, two_got, mark = gather_start(wires, (cuts[0], cuts[2], cuts[1]), start, beside)
    first, vec, time = arrange_first(wires, (cuts[0], cuts[2]), one, one_got, embedding, (mark,))

    turned_one, raw, stats_two = call(
        first_kernel, [turned, flat, pair], x_near, stats, vec, time, first, scratch=[three], flops=conv_flops
    )
    kernel_two = arrange_second(wires, cuts[1:2], two, two_got, (stats_two,))
    act_two, sums_two, grad_two, e_three, dc_sum = call(
        second_kernel,
        [padded, pair, taps, three, line],
        g_three,
        raw,
        stats_two,
        vec,
        kernel_two,
        scratch=[flat, turned],
        flops=2 * conv_flops,
    )
    last = wires.stages
    two_send, two = pack_second(wires, cuts[1:], grad_two, embedding, dc_sum)
    two_got = wires.swap(two_send, last)
    dh_one, sums_one, grad_one = call(
        third_kernel, [flat, pair, taps], turned_one, e_three, x_near, stats, vec, first
    )
    one_send, one, two_send, two = pack_first(
        wires, cuts[:1], grad_one, dc_sum, sums_one, sums_two, g_sum, two, two_got
    )
    input_grad, embedding_grad, input_done = call(
        input_kernel,
        [(maps[0], F32), ((1, emb_width), F32), line],
        dh_one,
        x,
        g,
        stats,
        sums_one,
        vec,
        dc_sum,
        first,
        embedding,
    )
    parts = 2
    rows = height // parts
    output, output_done = (), []
    for part in range(parts):
        *output, done = call(
            functools.partial(last_kernel, part, parts),
            [maps, line],
            act_two,
            x_near,
            vec,
            kernel_two,
            *output,
            scratch=[((3, rows + 2, width, channels), BF16), ((rows, width, channels), BF16)],
            far=(4,),
            far_outs=(0,),
            semaphores=(rows // (UNITS * ROWS),),
            same={4: 0} if output else None,
            flops=conv_flops // parts,
        )
        output_done.append(done)
    two_got = wires.swap(two_send, last - 1)
    one_send, one = call(halve_kernel, halved(one), one, wires.swap(one_send, last))
    one_got = wires.swap(one_send, last - 1)
    wide, narrow = cuts[0], sum(cuts[1:])
    shape = (wires.slots // 4 * (wide + narrow) + VEC_ROWS, LANES)
    send, keep = call(
        functools.partial(merge_kernel, wide, narrow),
        [(shape, BF16), (shape, F32)],
        one,
        one_got,
        two,
        two_got,
        after=output_done[:1],
    )
    for stage in range(last - 2, 0, -1):
        after = {last - 3: (input_done,), last - 2: (output_done[1],)}.get(stage, ())
        send, keep = call(halve_kernel, halved(keep), keep, wires.swap(send, stage), after=after)
    summed = call(
        functools.partial(finish_kernel, wires, cuts, n_vec),
        [*[((rows, LANES), F32) for rows in cuts], ((1, n_vec), F32)],
        keep,
        wires.swap(send, 0),
    )
    return (output[0][None], input_grad[None], embedding_grad, *[v.reshape(-1) for v in summed])


def solution(mesh):
    sizes = (mesh.shape["dp"], mesh.shape["fsdp"])
    split = P(AXES)
    maps = P(AXES, None, None, None)
    in_specs = (maps, P(AXES, None), split, split, split, split, maps)
    out_specs = (maps, maps, P(AXES, None), split, split, split, split)

    def body(*args):
        return local(sizes, *args)

    return jax.shard_map(body, mesh=mesh, in_specs=in_specs, out_specs=out_specs, check_vma=False)
```

```python
import functools
import math

import jax
import jax.numpy as jnp
from jax import lax
from jax.experimental import pallas as pl
from jax.experimental.pallas import tpu as pltpu
from jax.sharding import PartitionSpec as P

GROUPS = 32
EPS = 1e-05
AXES = ("dp", "fsdp")
LANES = 128
VEC_ROWS = 16


class Wires:
    def __init__(self, n_dp, n_fsdp):
        self.n_fsdp = n_fsdp
        self.n = n_dp * n_fsdp
        self.bits = int(math.log2(self.n))
        fsdp_bits = int(math.log2(n_fsdp))
        assert 1 << self.bits == self.n and 1 << fsdp_bits == n_fsdp and fsdp_bits >= 3 and n_dp >= 2
        a, b = 1, fsdp_bits
        far = [bit for bit in range(self.bits - 1, 0, -1) if bit not in (a, b)]
        self.order = {0: [*far, a, b], 1: [*far[::-1], b, a]}
        self.stages = self.bits - 1
        self.slots = 1 << self.stages

    def swap(self, value, stage):
        def bit(core):
            return 0 if stage == self.stages else self.order[core][stage]

        return lax.ppermute(value, AXES, [(i, i ^ (1 << bit(i & 1))) for i in range(self.n)])

    def mask(self, slot, core):
        return sum(1 << self.order[core][i] for i in range(self.stages) if slot >> i & 1)

    def me(self):
        return lax.axis_index("dp") * self.n_fsdp + lax.axis_index("fsdp")

    def owner(self, slot, other, me):
        core = me & 1
        if other:
            me, core = me ^ 1, 1 - core
        return me ^ jnp.where(core == 0, self.mask(slot, 0), self.mask(slot, 1))


def owner(self, slot, other, me):
        core = me & 1
        if other:
            me, core = me ^ 1, 1 - core
        return me ^ jnp.where(core == 0, self.mask(slot, 0), self.mask(slot, 1))


ROWS = 4
UNITS = 2
PIECE = 64
F32 = jnp.float32
BF16 = jnp.bfloat16
VMEM_BYTES = 15 * 1024 * 1024


def group_sum(totals):
    channels = totals.shape[1]
    lane = lax.broadcasted_iota(jnp.int32, totals.shape, 1)
    span = 1
    while span < channels // GROUPS:
        up = pltpu.roll(totals, channels - span, 1)
        down = pltpu.roll(totals, span, 1)
        totals = totals + jnp.where((lane & span) == 0, up, down)
        span *= 2
    return totals


def fold(values):
    channels = values.shape[-1]
    return jnp.sum(values.reshape(-1, 8, channels), 0)


def total(partial):
    return jnp.sum(partial, 0, keepdims=True)


def sigmoid(v):
    return 0.5 * jnp.tanh(0.5 * v) + 0.5


def clear_edges(three):
    height = three.shape[1] - 2
    zero = jnp.zeros((3, 1) + three.shape[2:], three.dtype)
    three[:, 0:1] = zero
    three[:, height + 1 : height + 2] = zero


def store_three(three, row, value):
    width = value.shape[0]
    column = lax.broadcasted_iota(jnp.int32, (8, value.shape[1]), 0)
    left = pltpu.roll(value, 1, 0)
    left = jnp.concatenate([jnp.where(column == 0, 0.0, left[:8]), left[8:]], axis=0)
    right = pltpu.roll(value, width - 1, 0)
    right = jnp.concatenate([right[: width - 8], jnp.where(column == 7, 0.0, right[width - 8 :])], axis=0)
    three[0, row + 1] = left.astype(three.dtype)
    three[1, row + 1] = value.astype(three.dtype)
    three[2, row + 1] = right.astype(three.dtype)


def accumulators(body, *refs):
    groups = 4

    def run(*accs):
        accs = iter(accs)
        body(*refs, [[[next(accs) for _ in range(ROWS)] for _ in range(groups)] for _ in range(UNITS)])

    pl.run_scoped(run, *[pltpu.ACC(unit)((PIECE, 2 * LANES), F32) for unit in range(UNITS) for _ in range(groups * ROWS)])


def interleave(pieces, slots):
    return [pieces * (i + 1) // slots - pieces * i // slots for i in range(slots)]


def times(value, size):
    return value * size if isinstance(value, int) else pl.multiple_of(value * size, size)


def conv_step(accs, three, kernel, step, parity, back, others=(), turn=True):
    others = list(others)
    for tap, share in enumerate(interleave(len(others), 9)):
        at = (8 - tap if back else tap) * three.shape[3]
        stage = (parity + tap) % 2
        for unit in range(UNITS):
            pltpu.matmul_push_rhs(kernel[at : at + three.shape[3], :], stage, unit, transpose=back and turn)
        for piece in range(ROWS):
            for unit in range(UNITS):
                row = (UNITS * step + unit) * ROWS + piece + tap // 3
                pltpu.matmul_acc_lhs(
                    accs[unit][parity][piece], three[tap % 3, row], load_staged_rhs=stage if piece == 0 else None
                )
        for _ in range(share):
            others.pop(0)()


def conv_rows(accs, step, parity, use):
    def one(unit, piece):
        use((UNITS * step + unit) * ROWS + piece, pltpu.matmul_pop(accs[unit][parity][piece]))

    return [functools.partial(one, unit, piece) for unit in range(UNITS) for piece in range(ROWS)]


def conv_all(accs, three, kernel, back, use, turn=True):
    steps = (three.shape[1] - 2) // (UNITS * ROWS)
    for step in range(steps):
        others = conv_rows(accs, step - 1, (step - 1) % 2, use) if step else ()
        conv_step(accs, three, kernel, step, step % 2, back, others, turn)
    assert steps % 2 == 0
    return conv_rows(accs, steps - 1, 1, use)


class Sums:
    def __init__(self, channels, count):
        self.values = [jnp.zeros((8, channels), F32)] * count

    def add(self, *values):
        self.values = [s + fold(v) for s, v in zip(self.values, values)]

    def totals(self):
        return [total(s) for s in self.values]


def store_turned(turned, padded, row):
    width, channels = padded.shape[1:]
    size = ROWS * width
    lanes = pl.ds(times(row // ROWS, size), size)
    turned[0, :, lanes] = padded[pl.ds(row + 1, ROWS)].reshape(size, channels).T
    turned[1, :, lanes] = padded[pl.ds(row, ROWS)].reshape(size, channels).T


def turn_end(turned, padded):
    height = padded.shape[0] - 2
    width, channels = padded.shape[1:]
    at = height * width
    turned[1, :, at : at + 2 * width] = padded[height : height + 2].reshape(2 * width, channels).T


def grad_step(accs, turned, three, work, stage, others=()):
    others = list(others)
    width, channels = three.shape[2:]
    size = ROWS * width
    for unit, column, chunk, _ in work:
        rhs = three[column, pl.ds(1 + times(chunk, ROWS), ROWS)].reshape(size, channels)
        pltpu.matmul_push_rhs(rhs, stage, unit)
    shares = iter(interleave(len(others), 3 * ROWS))
    for row in range(3):
        for piece in range(ROWS):
            for unit, _, chunk, groups in work:
                source, at = (0, times(chunk, size)) if row == 1 else (1, times(chunk, size) + row * width)
                lhs = turned[source, piece * PIECE : (piece + 1) * PIECE, pl.ds(at, size)]
                first = row == 0 and piece == 0
                pltpu.matmul_acc_lhs(accs[unit][groups[row]][piece], lhs, load_staged_rhs=stage if first else None)
            for _ in range(next(shares)):
                others.pop(0)()


def kernel_grad(accs, turned, three, flat, first, more):
    height, channels = three.shape[1] - 2, three.shape[3]
    chunks = height // ROWS
    lead, step = 4, 4
    outer_groups, inner_groups = (0, 2, 3), (1, 0, 2)

    def sides(chunk, stage, others):
        work = [(0, 0, chunk, outer_groups), (1, 2, chunk, outer_groups)]
        grad_step(accs, turned, three, work, stage, others)

    first = list(first)
    for chunk, share in enumerate(interleave(len(first), lead)):
        sides(chunk, chunk % 2, [first.pop(0) for _ in range(share)])
    beside, carry = more() or (None, 0)
    kept = [carry]

    def other(row):
        kept[0] = beside(row, kept[0])

    def loop(i, carry):
        kept[0] = carry
        for k in range(step):
            at = step * i + k
            sides(lead + at, k % 2, [functools.partial(other, ROWS * at + j) for j in range(ROWS)] if beside else ())
        return kept[0]

    if beside:
        kept[0] = lax.fori_loop(0, (chunks - lead) // step, loop, carry)
    else:
        for i in range((chunks - lead) // step):
            loop(i, carry)

    def store(tap, piece, value):
        store_flat(flat, (tap * channels + piece * PIECE) * 2, value)

    def side(unit, row, piece):
        store(3 * row + 2 - 2 * unit, piece, pltpu.matmul_pop(accs[unit][outer_groups[row]][piece]))

    for row in range(2):
        for unit in range(UNITS):
            for piece in range(ROWS):
                side(unit, row, piece)
    half = chunks // UNITS
    rest = [functools.partial(other, row) for row in range(ROWS * (chunks - lead), height)] if beside else []
    for chunk, share in enumerate(interleave(len(rest), half)):
        work = [(unit, 1, unit * half + chunk, inner_groups) for unit in range(UNITS)]
        others = [functools.partial(side, unit, 2, piece) for unit in range(UNITS) for piece in range(ROWS)]
        more_rows = [rest.pop(0) for _ in range(share)]
        grad_step(accs, turned, three, work, chunk % 2, (others if chunk == 0 else []) + more_rows)
    for row, group in enumerate(inner_groups):
        for piece in range(ROWS):
            store(3 * row + 1, piece, pltpu.matmul_pop(accs[0][group][piece]) + pltpu.matmul_pop(accs[1][group][piece]))
    return kept[0]


def store_flat(flat, start, value):
    rows = value.shape[0]
    flat[pl.ds(start, rows, stride=2), :] = value[:, :LANES]
    flat[pl.ds(start + 1, rows, stride=2), :] = value[:, LANES:]


def load_flat(flat, start, rows):
    left = flat[pl.ds(start, rows, stride=2), :]
    right = flat[pl.ds(start + 1, rows, stride=2), :]
    return jnp.concatenate([left, right], axis=1)


def stats_kernel(x_hbm, stats, x, arrived):
    height, width, channels = x.shape
    count = height * width * (channels // GROUPS)
    zero = jnp.zeros((8, channels), F32)
    parts = arrived.shape[0]
    rows = height // parts
    copies = [
        pltpu.make_async_copy(x_hbm.at[pl.ds(k * rows, rows)], x.at[pl.ds(k * rows, rows)], arrived.at[k])
        for k in range(parts)
    ]
    for copy in copies:
        copy.start()
    s = zero
    for k, copy in enumerate(copies):
        copy.wait()
        s = lax.fori_loop(0, rows // 4, lambda i, s, k=k: s + fold(x[pl.ds(k * rows + i * 4, 4)].astype(F32)), s)
    mean = group_sum(total(s)) / count

    def second(i, v):
        d = x[pl.ds(i * 4, 4)].astype(F32) - mean
        return v + fold(d * d)

    v = lax.fori_loop(0, height // 4, second, zero)
    inv = lax.rsqrt(group_sum(total(v)) / count + EPS)
    stats[0:1, :] = mean
    stats[1:2, :] = inv


def spread_kernel(g_hbm, three_hbm, g_sum, g, three, arrived, left):
    height, width, channels = g.shape
    parts = arrived.shape[0]
    rows = height // parts
    copies = [
        pltpu.make_async_copy(g_hbm.at[pl.ds(k * rows, rows)], g.at[pl.ds(k * rows, rows)], arrived.at[k])
        for k in range(parts)
    ]
    for copy in copies:
        copy.start()
    clear_edges(three)
    s = jnp.zeros((8, channels), F32)
    out = []
    for k, copy in enumerate(copies):
        copy.wait()

        def step(i, s, k=k):
            row = k * rows + i * 4
            values = g[pl.ds(row, 4)].astype(F32)
            for j in range(4):
                store_three(three, row + j, values[j])
            return s + fold(values)

        s = lax.fori_loop(0, rows // 4, step, s)
        start = k * rows + (1 if k else 0)
        size = rows + (1 if k == 0 else 0) + (1 if k == parts - 1 else 0)
        away = pltpu.make_async_copy(three.at[:, pl.ds(start, size)], three_hbm.at[:, pl.ds(start, size)], left.at[k])
        away.start()
        out.append(away)
    g_sum[...] = total(s)
    for away in out:
        away.wait()


def first_kernel(x, stats, vec, time, kernel, turned, raw, stats_out, flipped, three):
    accumulators(first_body, x, stats, vec, time, kernel, turned, raw, stats_out, flipped, three)


def first_body(x, stats, vec, time, kernel, turned, raw, stats_out, flipped, three, accs):
    height, width, channels = x.shape
    pixels = height * width
    per_group = channels // GROUPS
    mean, scale, shift = stats[0:1, :], 0.5 * stats[1:2, :] * vec[0:1, :], 0.5 * vec[1:2, :]
    offset = vec[2:3, :] + time[...]
    sums = Sums(channels, 2)
    pivot = []
    clear_edges(three)

    def activate(row):
        half = (x[row].astype(F32) - mean) * scale + shift
        store_three(three, row, half * (1.0 + jnp.tanh(half)))
        if row % ROWS == ROWS - 1:
            store_turned(turned, three.at[1], row + 1 - ROWS)

    def use(row, v):
        if row == 0:
            pivot.append(total(fold(v)) / width)
        raw[row * width : (row + 1) * width, :] = v
        d = v - pivot[0]
        sums.add(d, d * d)

    def flip(tap):
        at = slice(tap * channels, (tap + 1) * channels)
        flipped[at, :] = kernel[at, :].T

    per_step = UNITS * ROWS
    steps = height // per_step
    for row in range(per_step + 1):
        activate(row)
    for step in range(steps):
        ahead = range((step + 1) * per_step + 1, min((step + 2) * per_step + 1, height))
        others = [functools.partial(activate, row) for row in ahead]
        if step == steps - 1:
            others = [functools.partial(flip, tap) for tap in range(9)]
        done = conv_rows(accs, step - 1, (step - 1) % 2, use) if step else []
        mixed = [f for i in range(per_step + 1) for f in (*others[i : i + 1], *done[i : i + 1])]
        conv_step(accs, three, kernel, step, step % 2, False, mixed)
    turn_end(turned, three.at[1])
    for other in conv_rows(accs, steps - 1, (steps - 1) % 2, use):
        other()
    part, square = [v / pixels for v in sums.totals()]
    spread = square - part * part
    middle = pivot[0] + part + offset
    mean_two = group_sum(middle) / per_group
    away = middle - mean_two
    stats_out[0:1, :] = offset - mean_two
    stats_out[1:2, :] = lax.rsqrt(group_sum(spread + away * away) / per_group + EPS)


def second_kernel(g_three, raw, stats, vec, kernel, act, sums, flat, three, dc_sum, dh, turned):
    accumulators(second_body, g_three, raw, stats, vec, kernel, act, sums, flat, three, dc_sum, dh, turned)


def second_body(g_three, raw, stats, vec, kernel, act, sums, flat, three, dc_sum, dh, turned, accs):
    height, width, channels = act.shape[0] - 2, act.shape[1], act.shape[2]
    count = height * width * (channels // GROUPS)
    move, inv, gain, shift = stats[0:1, :], stats[1:2, :], vec[3:4, :], vec[4:5, :]
    scale, shift = 0.5 * inv * gain, 0.5 * shift
    both = Sums(channels, 2)
    act[0:1] = jnp.zeros((1, width, channels), BF16)
    act[height + 1 : height + 2] = jnp.zeros((1, width, channels), BF16)
    clear_edges(three)

    def use(row, v):
        at = slice(row * width, (row + 1) * width)
        c = raw[at, :] + move
        half = c * scale + shift
        t = jnp.tanh(half)
        u = 1.0 + t
        a = half * u
        act[row + 1] = a.astype(BF16)
        d = v * (u + a * (1.0 - t))
        dh[at, :] = d
        both.add(d, d * c)
        if row % ROWS == ROWS - 1:
            store_turned(turned, act, row + 1 - ROWS)

    last = conv_all(accs, g_three, kernel, True, use)

    def more():
        turn_end(turned, act)
        s, sc = [0.5 * v for v in both.totals()]
        sn = sc * inv
        sums[0:1, :] = sn
        sums[1:2, :] = s
        base = inv * (group_sum(s * gain) / count)
        slope = inv * inv * (group_sum(sn * gain) / count)
        base = base + move * slope

        def back(row, dc):
            at = pl.ds(times(row, width), width)
            d = dh[at, :] * scale - raw[at, :] * slope - base
            store_three(three, row, d)
            return dc + fold(d)

        return back, jnp.zeros((8, channels), F32)

    dc_sum[...] = total(kernel_grad(accs, turned, g_three, flat, last, more))


def third_kernel(turned, three, x, stats, vec, kernel, dh, sums, flat):
    accumulators(third_body, turned, three, x, stats, vec, kernel, dh, sums, flat)


def third_body(turned, three, x, stats, vec, kernel, dh, sums, flat, accs):
    height, width, channels = x.shape
    mean, scale, shift = stats[0:1, :], 0.5 * stats[1:2, :] * vec[0:1, :], 0.5 * vec[1:2, :]
    both = Sums(channels, 2)

    def use(row, v):
        c = x[row].astype(F32) - mean
        half = c * scale + shift
        t = jnp.tanh(half)
        d = v * ((1.0 + t) * (1.0 + half * (1.0 - t)))
        dh[row * width : (row + 1) * width, :] = d
        both.add(d, d * c)

    last = conv_all(accs, three, kernel, True, use, False)

    def more():
        s, sn = [0.5 * v for v in both.totals()]
        sums[0:1, :] = sn * stats[1:2, :]
        sums[1:2, :] = s

    kernel_grad(accs, turned, three, flat, last, more)


def input_kernel(dh, x, g, stats, sums, vec, dc_sum, kernel, embedding, result, emb_grad, done):
    height, width, channels = x.shape
    count = height * width * (channels // GROUPS)
    mean, inv, gain = stats[0:1, :], stats[1:2, :], vec[0:1, :]
    scale = 0.5 * inv * gain
    base = inv * (group_sum(sums[1:2, :] * gain) / count)
    slope = inv * inv * (group_sum(sums[0:1, :] * gain) / count)

    def back(i, _):
        row = i * 4
        d = dh[pl.ds(row * width, 4 * width), :].reshape(4, width, channels)
        c = x[pl.ds(row, 4)].astype(F32) - mean
        result[pl.ds(row, 4)] = g[pl.ds(row, 4)].astype(F32) + (d * scale - base - c * slope)
        return 0

    lax.fori_loop(0, height // 4, back, 0)
    dq = lax.dot_general(
        dc_sum[...],
        kernel[9 * channels :, :].astype(F32),
        (((1,), (1,)), ((), ())),
        precision=lax.Precision.HIGHEST,
        preferred_element_type=F32,
    )
    emb = embedding[...].astype(F32)
    sig = sigmoid(emb)
    emb_grad[...] = dq * (sig * (1.0 + emb * (1.0 - sig)))
    done[...] = base


def last_kernel(part, parts, *refs):
    accumulators(functools.partial(last_body, part, parts), *refs)


def last_body(part, parts, act, x, vec, kernel, *refs):
    out, done, three, result, left, accs = refs[-6:]
    height = x.shape[0]
    rows = height // parts
    base = part * rows
    bias = vec[5:6, :]

    def spread(row):
        if 0 <= base + row < height:
            store_three(three, row, act[base + row + 1].astype(F32))
        else:
            three[:, row + 1 : row + 2] = jnp.zeros((3, 1) + three.shape[2:], BF16)

    def use(row, v):
        result[row] = (x[base + row].astype(F32) + v + bias).astype(BF16)

    per_step = UNITS * ROWS
    steps = rows // per_step
    copies = []

    def send(step):
        here = pl.ds(step * per_step, per_step)
        copies.append(pltpu.make_async_copy(result.at[here], out.at[pl.ds(base + step * per_step, per_step)], left.at[step]))
        copies[-1].start()

    for row in range(-1, per_step + 1):
        spread(row)
    for step in range(steps):
        ahead = range((step + 1) * per_step + 1, min((step + 2) * per_step, rows) + 1)
        others = [functools.partial(spread, row) for row in ahead]
        done_rows = conv_rows(accs, step - 1, (step - 1) % 2, use) if step else []
        mixed = [f for i in range(per_step) for f in (*others[i : i + 1], *done_rows[i : i + 1])]
        conv_step(accs, three, kernel, step, step % 2, False, mixed)
        if step:
            send(step - 1)
    for other in conv_rows(accs, steps - 1, (steps - 1) % 2, use):
        other()
    send(steps - 1)
    done[...] = bias
    for copy in copies:
        copy.wait()


def start_kernel(wires, n_vec, *refs):
    *parts, vectors, out, own, arrived = refs
    copies, at = [], 0
    for i, part in enumerate(parts):
        copies.append(pltpu.make_async_copy(part, out.at[pl.ds(at, part.shape[0])], arrived.at[i]))
        at += part.shape[0]
    copies.append(pltpu.make_async_copy(vectors, own, arrived.at[len(parts)]))
    for copy in copies:
        copy.start()
    copies[-1].wait()
    first = wires.me() * n_vec
    row, lane = first // LANES, first % LANES
    values = jnp.concatenate([own[...].astype(F32), jnp.zeros((1, LANES - n_vec), F32)], axis=1)
    values = jnp.broadcast_to(pltpu.roll(values, lane, 1), (VEC_ROWS, LANES))
    place = lax.broadcasted_iota(jnp.int32, values.shape, 0)
    column = lax.broadcasted_iota(jnp.int32, values.shape, 1)
    here = ((place == row) & (column >= lane)) | ((place == row + 1) & (column < lane))
    out[at : at + VEC_ROWS, :] = jnp.where(here, values, 0.0).astype(BF16)
    for copy in copies[:-1]:
        copy.wait()


def join_kernel(mine, got, out, tail=VEC_ROWS):
    rows = mine.shape[0] - tail
    out[0:rows, :] = mine[0:rows, :]
    out[rows : 2 * rows, :] = got[0:rows, :]
    if tail:
        out[2 * rows :, :] = mine[rows:, :] + got[rows:, :]


def join_second_kernel(mine, got, out, mark):
    join_kernel(mine, got, out, 0)
    mark[...] = jnp.zeros_like(mark)


def part_kernel(cuts, mine, got, first, second):
    block, cut = sum(cuts), sum(cuts[:-1])
    slots = (mine.shape[0] - VEC_ROWS) // block
    for half, source in enumerate((mine, got)):
        for slot in range(slots):
            at, to = slot * block, half * slots + slot
            first[to * cut : (to + 1) * cut, :] = source[at : at + cut, :]
            second[to * cuts[-1] : (to + 1) * cuts[-1], :] = source[at + cut : at + block, :]
    first[2 * slots * cut :, :] = mine[slots * block :, :] + got[slots * block :, :]


def halve_kernel(keep, got, send_next, keep_next, tail=VEC_ROWS):
    rows = (keep.shape[0] - tail) // 2
    keep_next[0:rows, :] = keep[0:rows, :] + got[0:rows, :].astype(F32)
    send_next[0:rows, :] = (keep[rows : 2 * rows, :] + got[rows : 2 * rows, :].astype(F32)).astype(BF16)
    if tail:
        vec = keep[2 * rows :, :] + got[2 * rows :, :].astype(F32)
        keep_next[rows:, :] = vec
        send_next[rows:, :] = vec.astype(BF16)


def halve_second_kernel(keep, got, send_next, keep_next):
    halve_kernel(keep, got, send_next, keep_next, 0)


def merge_kernel(wide, narrow, one, one_got, two, two_got, send, keep):
    slots = two.shape[0] // narrow // 2
    for slot in range(slots):
        to = slot * (wide + narrow)
        for mine, got, rows in ((one, one_got, wide), (two, two_got, narrow)):
            at, up = slot * rows, (slots + slot) * rows
            keep[to : to + rows, :] = mine[at : at + rows, :] + got[at : at + rows, :].astype(F32)
            send[to : to + rows, :] = (mine[up : up + rows, :] + got[up : up + rows, :].astype(F32)).astype(BF16)
            to += rows
    at, to = 2 * slots * wide, slots * (wide + narrow)
    values = one[at:, :] + one_got[at:, :].astype(F32)
    keep[to:, :] = values
    send[to:, :] = values.astype(BF16)


def place_blocks(wires, cuts, mine, got, flats):
    me = wires.me()
    block = sum(cuts)
    for slot in range(wires.slots):
        for other, source in ((False, mine), (True, got)):
            owner = wires.owner(slot, other, me)
            values = source[slot * block : (slot + 1) * block, :].astype(F32)
            at = 0
            for flat, rows in zip(flats, cuts):
                flat[pl.ds(pl.multiple_of(owner * rows, rows), rows), :] = values[at : at + rows]
                at += rows


def unflatten(flat, out, base):
    for start in range(0, flat.shape[0] // 2, 256):
        out[base + start : base + start + 256, :] = load_flat(flat, 2 * start, 256).astype(BF16)


def arrange_first_kernel(wires, cuts, mine, got, embedding, first, vec, time, flat_one, flat_project, flat_vec):
    place_blocks(wires, cuts, mine, got, (flat_one, flat_project))
    rows_one = flat_one.shape[0] // 2
    unflatten(flat_project, first, rows_one)
    emb = embedding[...].astype(F32)
    act = (emb * sigmoid(emb)).astype(BF16)
    time[...] = jnp.dot(act, first[rows_one:, :], preferred_element_type=F32)
    unflatten(flat_one, first, 0)
    at = wires.slots * sum(cuts)
    flat_vec[...] = mine[at : at + VEC_ROWS, :].astype(F32) + got[at : at + VEC_ROWS, :].astype(F32)
    vec[...] = load_flat(flat_vec, 0, VEC_ROWS // 2)


def arrange_second_kernel(wires, cuts, mine, got, second, flat_two):
    place_blocks(wires, cuts, mine, got, (flat_two,))
    unflatten(flat_two, second, 0)


def take_blocks(wires, cuts, flats, send, keep):
    me = wires.me()
    block = sum(cuts)
    for slot in range(wires.slots):
        for other in (True, False):
            owner = wires.owner(slot, other, me)
            at = slot * block
            for flat, rows in zip(flats, cuts):
                values = flat[pl.ds(pl.multiple_of(owner * rows, rows), rows), :]
                if other:
                    send[at : at + rows, :] = values.astype(BF16)
                else:
                    keep[at : at + rows, :] = values
                at += rows


def pack_first_kernel(
    wires, cuts, flat_one, dc_sum, sums_one, sums_two, g_sum, two, two_got, send, keep, two_send, two_keep
):
    halve_kernel(two, two_got, two_send, two_keep, 0)
    take_blocks(wires, cuts, (flat_one,), send, keep)
    at = wires.slots * sum(cuts)
    vectors = [sums_one[0:1, :], sums_one[1:2, :], dc_sum[...], sums_two[0:1, :], sums_two[1:2, :], g_sum[...]]
    halves = [row[:, i * LANES : (i + 1) * LANES] for row in vectors for i in range(2)]
    values = jnp.concatenate(halves + [jnp.zeros((VEC_ROWS - len(halves), LANES), F32)], axis=0)
    keep[at : at + VEC_ROWS, :] = values
    send[at : at + VEC_ROWS, :] = values.astype(BF16)


def pack_second_kernel(wires, cuts, flat_two, embedding, dc_sum, send, keep, flat_project):
    emb = embedding[...].astype(F32)
    q = (emb * sigmoid(emb)).astype(BF16).astype(F32)
    q = jnp.broadcast_to(q, (LANES, q.shape[1])).T
    dc = dc_sum[...]
    store_flat(flat_project, 0, jnp.concatenate([q * dc[:, :LANES], q * dc[:, LANES:]], axis=1))
    take_blocks(wires, cuts, (flat_two, flat_project), send, keep)


def finish_kernel(wires, cuts, n_vec, keep, got, one, two, project, vec):
    at = 0
    for out, rows in zip((one, two, project), cuts):
        out[...] = keep[at : at + rows, :] + got[at : at + rows, :].astype(F32)
        at += rows
    vectors = keep[at : at + VEC_ROWS, :] + got[at : at + VEC_ROWS, :].astype(F32)
    start = wires.me() * n_vec
    row, lane = start // LANES, start % LANES
    place = lax.broadcasted_iota(jnp.int32, vectors.shape, 0)
    own = jnp.sum(jnp.where(place == row, vectors, 0.0), 0, keepdims=True)
    following = jnp.sum(jnp.where(place == row + 1, vectors, 0.0), 0, keepdims=True)
    column = lax.broadcasted_iota(jnp.int32, own.shape, 1)
    shifted = pltpu.roll(jnp.where(column >= lane, own, following), (LANES - lane) % LANES, 1)
    vec[...] = shifted[:, :n_vec]


def call(body, outs, *args, scratch=(), flops=0, size=4 << 20, after=(), far=(), far_outs=(), semaphores=(), same=None):
    held, n_in = len(after), len(args)

    def run(*refs):
        body(*refs[:n_in], *refs[n_in + held :])

    args = [pltpu.with_memory_space_constraint(v, pltpu.HBM) if i in far else v for i, v in enumerate(args)]

    def spec(is_far):
        return pl.BlockSpec(memory_space=pltpu.HBM if is_far else pltpu.VMEM)

    return pl.pallas_call(
        run,
        out_shape=[
            pltpu.HBM(shape, dtype) if i in far_outs else jax.ShapeDtypeStruct(shape, dtype)
            for i, (shape, dtype) in enumerate(outs)
        ],
        in_specs=[spec(i in far) for i in range(n_in)] + [pl.BlockSpec(memory_space=pl.ANY)] * held,
        out_specs=[spec(i in far_outs) for i in range(len(outs))],
        scratch_shapes=[pltpu.VMEM(shape, dtype) for shape, dtype in scratch]
        + [pltpu.SemaphoreType.DMA((n,)) for n in semaphores],
        input_output_aliases=same or {},
        compiler_params=pltpu.CompilerParams(vmem_limit_bytes=VMEM_BYTES),
        cost_estimate=pl.CostEstimate(flops=0, bytes_accessed=0, transcendentals=0),
    )(*args, *after)


def joined(held, tail=VEC_ROWS):
    return ((2 * (held.shape[0] - tail) + tail, LANES), BF16)


def gather_start(wires, cuts, held, beside):
    last = wires.stages - 1
    for stage in range(last - 1):
        after = beside.get(stage, ())
        held, = call(join_kernel, [joined(held)], held, wires.swap(held, stage), after=after)
    got = wires.swap(held, last - 1)
    slots = wires.slots // 2
    shapes = [(slots * sum(cuts[:-1]) + VEC_ROWS, LANES), (slots * cuts[-1], LANES)]
    outs = [(shape, BF16) for shape in shapes]
    first, second = call(functools.partial(part_kernel, cuts), outs, held, got, after=beside.get(last - 1, ()))
    first_got, second_got = wires.swap(first, last), wires.swap(second, last)
    first, = call(join_kernel, [joined(first)], first, first_got, after=beside.get(last, ()))
    second, mark = call(join_second_kernel, [joined(second, 0), ((1, LANES), F32)], second, second_got)
    return first, wires.swap(first, wires.stages), second, wires.swap(second, wires.stages), mark


def in_order(wires, cuts, mine, got):
    block = sum(cuts)
    rows = wires.slots * block
    both = jnp.concatenate([mine[:rows], got[:rows]]).reshape(wires.n, block, LANES)
    me = wires.me()
    owners = jnp.stack([wires.owner(j, other, me) for other in (False, True) for j in range(wires.slots)])
    both = jnp.zeros_like(both).at[owners].set(both)
    ends = [sum(cuts[:i]) for i in range(len(cuts) + 1)]
    return [both[:, a:b].reshape(-1, 2 * LANES) for a, b in zip(ends, ends[1:])]


def arrange_first(wires, cuts, mine, got, embedding, after):
    channels = 2 * LANES
    totals = [wires.n * rows for rows in cuts]
    if all(rows % 8 == 0 for rows in cuts):
        return call(
            functools.partial(arrange_first_kernel, wires, cuts),
            [((sum(totals) // 2, channels), BF16), ((VEC_ROWS // 2, channels), F32), ((1, channels), F32)],
            mine,
            got,
            embedding,
            scratch=[((rows, LANES), F32) for rows in (*totals, VEC_ROWS)],
            after=after,
        )
    one, project = in_order(wires, cuts, mine, got)
    vec = (mine[-VEC_ROWS:].astype(F32) + got[-VEC_ROWS:].astype(F32)).reshape(VEC_ROWS // 2, channels)
    act = jax.nn.silu(embedding.astype(F32)).astype(BF16)
    return jnp.concatenate([one, project]), vec, jnp.dot(act, project, preferred_element_type=F32)


def arrange_second(wires, cuts, mine, got, after):
    rows = wires.n * cuts[0]
    if cuts[0] % 8 == 0:
        body = functools.partial(arrange_second_kernel, wires, cuts)
        return call(body, [((rows // 2, 2 * LANES), BF16)], mine, got, scratch=[((rows, LANES), F32)], after=after)[0]
    return in_order(wires, cuts, mine, got)[0]


def out_of_order(wires, cuts, parts, tail):
    me = wires.me()
    blocks = jnp.concatenate([v.reshape(wires.n, rows, LANES) for v, rows in zip(parts, cuts)], axis=1)
    halves = []
    for other in (True, False):
        owners = jnp.stack([wires.owner(j, other, me) for j in range(wires.slots)])
        halves.append(jnp.concatenate([blocks[owners].reshape(-1, LANES), tail]))
    return halves[0].astype(BF16), halves[1]


def pack_first(wires, cuts, flat_one, dc_sum, sums_one, sums_two, g_sum, two, two_got):
    shape = (wires.slots * sum(cuts) + VEC_ROWS, LANES)
    if all(rows % 8 == 0 for rows in cuts):
        return call(
            functools.partial(pack_first_kernel, wires, cuts),
            [(shape, BF16), (shape, F32), *halved(two, 0)],
            flat_one,
            dc_sum,
            sums_one,
            sums_two,
            g_sum,
            two,
            two_got,
        )
    vec = jnp.concatenate([sums_one, dc_sum, sums_two, g_sum]).reshape(-1, LANES)
    vec = jnp.pad(vec, ((0, VEC_ROWS - vec.shape[0]), (0, 0)))
    send, keep = out_of_order(wires, cuts, (flat_one,), vec)
    return send, keep, *call(halve_second_kernel, halved(two, 0), two, two_got)


def pack_second(wires, cuts, flat_two, embedding, dc_sum):
    if all(rows % 8 == 0 for rows in cuts):
        shape = (wires.slots * sum(cuts), LANES)
        return call(
            functools.partial(pack_second_kernel, wires, cuts),
            [(shape, BF16), (shape, F32)],
            flat_two,
            embedding,
            dc_sum,
            scratch=[((wires.n * cuts[1], LANES), F32)],
        )
    q = jax.nn.silu(embedding.astype(F32)).astype(BF16).astype(F32).reshape(-1, 1)
    parts = (flat_two, (q * dc_sum).reshape(-1, LANES))
    return out_of_order(wires, cuts, parts, jnp.zeros((0, LANES), F32))


def halved(keep, tail=VEC_ROWS):
    shape = ((keep.shape[0] - tail) // 2 + tail, LANES)
    return [(shape, BF16), (shape, F32)]


def local(sizes, images, embedding, conv_first, conv_second, projection, vectors, cotangent):
    count, height, width, channels = images.shape
    emb_width = embedding.shape[-1]
    wires = Wires(*sizes)
    n_vec = vectors.shape[0]
    assert count == 1 and channels == 2 * LANES and n_vec <= LANES
    cuts = [v.shape[0] // LANES for v in (conv_first, conv_second, projection)]
    pixels = height * width
    three = ((3, height + 2, width, channels), BF16)
    maps = ((height, width, channels), BF16)
    flat = ((pixels, channels), F32)
    line = ((1, channels), F32)
    pair = ((2, channels), F32)
    taps = ((18 * channels, LANES), F32)
    padded = ((height + 2, width, channels), BF16)
    turned = ((2, channels, pixels + 2 * width), BF16)
    conv_flops = 2 * 9 * pixels * channels * channels

    x, g = images[0], cotangent[0]
    stats, x_near = call(stats_kernel, [pair, maps], x, far=(0,), semaphores=(4,))
    g_three, g_sum = call(
        spread_kernel, [three, line], g, scratch=[maps, three], far=(0,), far_outs=(0,), semaphores=(4, 4)
    )
    order = (conv_first, projection, conv_second)
    if all(rows % 16 == 0 for rows in cuts):
        start, = call(
            functools.partial(start_kernel, wires, n_vec),
            [((sum(cuts) + VEC_ROWS, LANES), BF16)],
            *[v.reshape(-1, LANES) for v in order],
            vectors.reshape(1, n_vec),
            scratch=[((1, n_vec), BF16)],
            far=(0, 1, 2, 3),
            semaphores=(4,),
        )
    else:
        wide = VEC_ROWS * LANES
        placed = lax.dynamic_slice(jnp.pad(vectors, (wide, wide - n_vec)), (wide - wires.me() * n_vec,), (wide,))
        start = jnp.concatenate([v.reshape(-1, LANES) for v in (*order, placed)])
    beside = {wires.stages - 2: (g_sum,), wires.stages - 1: (stats,)}
    one, one_got, two, two_got, mark = gather_start(wires, (cuts[0], cuts[2], cuts[1]), start, beside)
    first, vec, time = arrange_first(wires, (cuts[0], cuts[2]), one, one_got, embedding, (mark,))

    turned_one, raw, stats_two, flipped = call(
        first_kernel, [turned, flat, pair, ((9 * channels, channels), BF16)], x_near, stats, vec, time, first, scratch=[three], flops=conv_flops
    )
    kernel_two = arrange_second(wires, cuts[1:2], two, two_got, (stats_two,))
    act_two, sums_two, grad_two, e_three, dc_sum = call(
        second_kernel,
        [padded, pair, taps, three, line],
        g_three,
        raw,
        stats_two,
        vec,
        kernel_two,
        scratch=[flat, turned],
        flops=2 * conv_flops,
    )
    last = wires.stages
    two_send, two = pack_second(wires, cuts[1:], grad_two, embedding, dc_sum)
    two_got = wires.swap(two_send, last)
    dh_one, sums_one, grad_one = call(
        third_kernel, [flat, pair, taps], turned_one, e_three, x_near, stats, vec, flipped
    )
    one_send, one, two_send, two = pack_first(
        wires, cuts[:1], grad_one, dc_sum, sums_one, sums_two, g_sum, two, two_got
    )
    input_grad, embedding_grad, input_done = call(
        input_kernel,
        [(maps[0], F32), ((1, emb_width), F32), line],
        dh_one,
        x,
        g,
        stats,
        sums_one,
        vec,
        dc_sum,
        first,
        embedding,
    )
    parts = 2
    rows = height // parts
    output, output_done = (), []
    for part in range(parts):
        *output, done = call(
            functools.partial(last_kernel, part, parts),
            [maps, line],
            act_two,
            x_near,
            vec,
            kernel_two,
            *output,
            scratch=[((3, rows + 2, width, channels), BF16), ((rows, width, channels), BF16)],
            far=(4,),
            far_outs=(0,),
            semaphores=(rows // (UNITS * ROWS),),
            same={4: 0} if output else None,
            flops=conv_flops // parts,
        )
        output_done.append(done)
    two_got = wires.swap(two_send, last - 1)
    one_send, one = call(halve_kernel, halved(one), one, wires.swap(one_send, last))
    one_got = wires.swap(one_send, last - 1)
    wide, narrow = cuts[0], sum(cuts[1:])
    shape = (wires.slots // 4 * (wide + narrow) + VEC_ROWS, LANES)
    send, keep = call(
        functools.partial(merge_kernel, wide, narrow),
        [(shape, BF16), (shape, F32)],
        one,
        one_got,
        two,
        two_got,
        after=output_done[:1],
    )
    for stage in range(last - 2, 0, -1):
        after = {last - 3: (input_done,), last - 2: (output_done[1],)}.get(stage, ())
        send, keep = call(halve_kernel, halved(keep), keep, wires.swap(send, stage), after=after)
    summed = call(
        functools.partial(finish_kernel, wires, cuts, n_vec),
        [*[((rows, LANES), F32) for rows in cuts], ((1, n_vec), F32)],
        keep,
        wires.swap(send, 0),
    )
    return (output[0][None], input_grad[None], embedding_grad, *[v.reshape(-1) for v in summed])


def solution(mesh):
    sizes = (mesh.shape["dp"], mesh.shape["fsdp"])
    split = P(AXES)
    maps = P(AXES, None, None, None)
    in_specs = (maps, P(AXES, None), split, split, split, split, maps)
    out_specs = (maps, maps, P(AXES, None), split, split, split, split)

    def body(*args):
        return local(sizes, *args)

    return jax.shard_map(body, mesh=mesh, in_specs=in_specs, out_specs=out_specs, check_vma=False)
```
